32 devices in a mesh: dp: 8 (over y, x, core), tensor: 4 (over z).
Axes of the slice: x: 2, y: 2, z: 4, core: 2. Of those that a mesh axis runs over, the one named last changes fastest.
Arguments:
- tokens: bfloat16 [8192, 2048], P('dp'), may hold values from -6 to 6
- segments: int32 [8192], P('dp'), may hold values from 0 to 768, as said below
- counts: int32 [8], P('dp'), may hold values from 512 to 1024, as said below
- cotangent: bfloat16 [8192, 2048], P('dp'), may hold values from -6 to 6
- attn_gain: float32 [2048], replicated, may hold values from 0.1 to 1.9
- mlp_gain: float32 [2048], replicated, may hold values from 0.1 to 1.9
- query_weight: bfloat16 [2048, 2048], P(None, 'tensor'), may hold values from -0.125 to 0.125
- key_weight: bfloat16 [2048, 256], P(None, 'tensor'), may hold values from -0.125 to 0.125
- value_weight: bfloat16 [2048, 256], P(None, 'tensor'), may hold values from -0.125 to 0.125
- out_weight: bfloat16 [2048, 2048], P('tensor'), may hold values from -0.5 to 0.5
- gate_weight: bfloat16 [2048, 5632], P(None, 'tensor'), may hold values from -0.125 to 0.125
- up_weight: bfloat16 [2048, 5632], P(None, 'tensor'), may hold values from -0.125 to 0.125
- down_weight: bfloat16 [5632, 2048], P('tensor'), may hold values from -0.125 to 0.125
Outputs:
- mixed: bfloat16 [8192, 2048], P('dp')
- tokens_grad: bfloat16 [8192, 2048], P('dp')
- attn_gain_grad: float32 [2048], P('dp')
- mlp_gain_grad: float32 [2048], P('dp')
- query_weight_grad: float32 [2048, 2048], P('dp', 'tensor')
- key_weight_grad: float32 [2048, 256], P('dp', 'tensor')
- value_weight_grad: float32 [2048, 256], P('dp', 'tensor')
- out_weight_grad: float32 [2048, 2048], P('tensor', 'dp')
- gate_weight_grad: float32 [2048, 5632], P('dp', 'tensor')
- up_weight_grad: float32 [2048, 5632], P('dp', 'tensor')
- down_weight_grad: float32 [5632, 2048], P('tensor', 'dp')
The draws below stay inside these ranges and needn't reach their ends.
Inputs may be any that keep to these rules, and one draw needn't show every extreme that they name: `segments`: in each aligned block of 1024 tokens the ids start at 0 and never fall. `counts`: some row is fully live.
All inputs are finite; a program needn't handle non-finite values.
Results may differ from the reference program's by a relative error of at most 0.019.
Values may be sent and summed in bfloat16 or wider, within the bound.
A program may use at most 256 MiB of HBM per device.

```python
import jax
import jax.numpy as jnp
from jax import lax

D = 2048
HEADS = 32
KV = 4
HD = 64
FF = 5632
ROW = 1024
TOKENS = 8192


def draw_segments(key, part):
    key = jax.random.fold_in(key, 11)
    first_key, second_key, third_key, fourth_key = jax.random.split(key, 4)
    packed = TOKENS // ROW
    rows_index = jnp.arange(packed)[:, None]
    doc_length = jax.random.randint(first_key, (packed, 1), ROW // 4, ROW + 1)
    chosen = jax.random.randint(third_key, (), 0, packed)
    other = (chosen + 1 + jax.random.randint(fourth_key, (), 0, packed - 1)) % packed
    doc_length = jnp.where(rows_index == chosen, ROW, doc_length)
    doc_length = jnp.where(rows_index == other, ROW // 4, doc_length)
    starts = (jax.random.randint(second_key, (packed, ROW), 0, 48) == 0).astype(jnp.int32)
    starts = jnp.where(rows_index == other, 1, starts)
    position = jnp.arange(ROW)[None, :]
    flags = jnp.where(position > doc_length, starts, 0)
    flags = jnp.where(position == doc_length, 1, flags)
    return jnp.cumsum(flags, axis=1).astype(jnp.int32).reshape(TOKENS)


def draw_counts(key, part):
    key = jax.random.fold_in(key, 23)
    first_key, second_key, third_key = jax.random.split(key, 3)
    packed = TOKENS // ROW
    live = jax.random.randint(first_key, (packed,), ROW // 2, ROW + 1)
    chosen = jax.random.randint(second_key, (), 0, packed)
    other = (chosen + 1 + jax.random.randint(third_key, (), 0, packed - 1)) % packed
    live = jnp.where(jnp.arange(packed) == other, ROW // 2, live)
    return jnp.where(jnp.arange(packed) == chosen, ROW, live).astype(jnp.int32)


def with_spikes(array, own_key, source, target, parts, factor):
    owner, partner = [(jnp.arange(array.shape[dim]) // (array.shape[dim] // parts)).reshape([-1 if axis == dim else 1 for axis in range(array.ndim)]) for dim in (source, target)]
    chosen = jax.random.permutation(own_key, parts)[partner]
    strong = (owner == chosen) | (owner == (partner + parts // 2) % parts)
    return jnp.where(strong, factor * array, array)


def block_levels(rng, extent, pieces, low, high):
    factor_of, own = 1.0, jax.random.fold_in(rng, 6)
    for dim, parts in pieces:
        draws = jnp.exp(jax.random.uniform(jax.random.fold_in(own, dim), (parts,), jnp.float32, low / len(pieces), high / len(pieces)))
        factor_of = factor_of * jnp.repeat(draws, extent[dim] // parts).reshape([-1 if axis == dim else 1 for axis in range(len(extent))])
    return factor_of


def scatter_about(own_key, dims, spread, most, pieces=(), held_as=jnp.bfloat16):
    values = jax.random.normal(own_key, dims, jnp.float32) * spread
    if len(pieces) > 0:
        values = block_levels(own_key, dims, pieces, -0.22, 0.18) * values
    return jnp.clip(values, min=-most, max=most).astype(held_as)


def gaussian_with(own_key, extent, deviation, limit, cuts, heavy, kind=jnp.bfloat16):
    result = deviation * jax.random.normal(own_key, extent, jnp.float32)
    if cuts:
        result = result * block_levels(own_key, extent, cuts, -0.22, 0.18)
    return jnp.clip(with_spikes(result, jax.random.fold_in(own_key, 3), *heavy), -limit, limit).astype(kind)


def setup_inputs(seed: int = 0) -> dict:
    arg_keys = jax.random.split(jax.random.key(seed), 14)
    tokens = scatter_about(arg_keys[0], (TOKENS, D), 1.0, 6.0, ((0, 8),))
    segments = draw_segments(jax.random.fold_in(arg_keys[13], 71), 0)
    counts = draw_counts(jax.random.fold_in(arg_keys[13], 71), 0)
    cotangent = gaussian_with(arg_keys[3], (TOKENS, D), 1.0, 6.0, ((0, 8),), (0, 1, 8, 2.0))
    attn_gain = jnp.clip(1.0 + 0.18 * jax.random.normal(arg_keys[4], (D,), jnp.float32), 0.1, 1.9)
    mlp_gain = jnp.clip(1.0 + 0.18 * jax.random.normal(arg_keys[5], (D,), jnp.float32), 0.1, 1.9)
    query_weight = scatter_about(arg_keys[6], (D, HEADS * HD), D ** -0.5, 0.125, ((1, 4),))
    key_weight = scatter_about(arg_keys[7], (D, KV * HD), D ** -0.5, 0.125, ((1, 4),))
    value_weight = scatter_about(arg_keys[8], (D, KV * HD), D ** -0.5, 0.125, ((1, 4),))
    out_weight = scatter_about(arg_keys[9], (HEADS * HD, D), (HEADS * HD // 16) ** -0.5, 0.5, ((0, 4),))
    gate_weight = scatter_about(arg_keys[10], (D, FF), D ** -0.5, 0.125, ((1, 4),))
    up_weight = scatter_about(arg_keys[11], (D, FF), D ** -0.5, 0.125, ((1, 4),))
    down_weight = scatter_about(arg_keys[12], (FF, D), (FF // 3) ** -0.5, 0.125, ((0, 4),))
    return {"tokens": tokens, "segments": segments, "counts": counts, "cotangent": cotangent, "attn_gain": attn_gain, "mlp_gain": mlp_gain, "query_weight": query_weight, "key_weight": key_weight, "value_weight": value_weight, "out_weight": out_weight, "gate_weight": gate_weight, "up_weight": up_weight, "down_weight": down_weight}


EPS = 1e-05
THETA = 10000.0
NEGATIVE = -1e+30
HIGH = lax.Precision.HIGHEST

@jax.custom_vjp
def low(v):
    return lax.optimization_barrier(v.astype(jnp.bfloat16)).astype(jnp.float32)

@jax.custom_vjp
def low_back(v):
    return v

def low_keep(v):
    return (low(v), None)

def low_pass(kept, grad):
    return (grad,)

def back_keep(v):
    return (v, None)

def back_low(kept, grad):
    return (low(grad),)
low.defvjp(low_keep, low_pass)
low_back.defvjp(back_keep, back_low)

def tables(seg_row):
    length = seg_row.shape[0]
    index = jnp.arange(length, dtype=jnp.int32)
    change = jnp.concatenate([jnp.ones((1,), jnp.int32), (seg_row[1:] != seg_row[:-1]).astype(jnp.int32)]) > 0
    start = lax.cummax(jnp.where(change, index, 0), axis=0)
    place = (index - start).astype(jnp.float32)
    half = HD // 2
    freq = jnp.power(jnp.float32(THETA), -jnp.arange(half, dtype=jnp.float32) / half)
    angle = place[:, None] * freq[None, :]
    return (jnp.cos(angle), jnp.sin(angle))

def rotate(tensor, cosine, sine):
    half = tensor.shape[-1] // 2
    first = tensor[..., :half]
    second = tensor[..., half:]
    cosine = cosine[:, None, :]
    sine = sine[:, None, :]
    return jnp.concatenate([first * cosine - second * sine, second * cosine + first * sine], axis=-1)

def normed(vector, gain):
    return vector * lax.rsqrt(lax.optimization_barrier(jnp.mean(vector * vector, axis=-1, keepdims=True)) + EPS) * gain

def matmul(left, right):
    return jnp.dot(left, right, precision=HIGH)

def row_forward(params, xrow, visible, cosine, sine):
    attn_gain, mlp_gain, query_weight, key_weight, value_weight, out_weight, gate_weight, up_weight, down_weight = params
    length = xrow.shape[0]
    group = HEADS // KV
    factor = HD ** (-0.5)
    hidden1 = low(normed(xrow, attn_gain))
    query_raw = low_back(matmul(hidden1, query_weight)).reshape(length, HEADS, HD)
    key_raw = low_back(matmul(hidden1, key_weight)).reshape(length, KV, HD)
    values = low(low_back(matmul(hidden1, value_weight))).reshape(length, KV, HD)
    query = low(rotate(query_raw, cosine, sine))
    keys = low(rotate(key_raw, cosine, sine))
    query_groups = query.reshape(length, KV, group, HD).transpose(1, 0, 2, 3)
    key_groups = keys.transpose(1, 0, 2)
    value_groups = values.transpose(1, 0, 2)

    def attend(items):
        query_block, key_block, value_block = items
        scores = low_back(jnp.einsum('qhd,kd->hqk', query_block, key_block, precision=HIGH) * factor)
        scores = jnp.where(visible[None], scores, NEGATIVE)
        probs = jax.nn.softmax(scores, axis=-1)
        return jnp.einsum('hqk,kd->qhd', low(probs), value_block, precision=HIGH)
    heads_out = lax.map(jax.checkpoint(attend), (query_groups, key_groups, value_groups))
    heads_out = low(low_back(heads_out.transpose(1, 0, 2, 3).reshape(length, HEADS * HD)))
    attn = low_back(matmul(heads_out, out_weight))
    resid = xrow + attn
    hidden2 = low(normed(resid, mlp_gain))
    gate = low_back(matmul(hidden2, gate_weight))
    up_value = low_back(matmul(hidden2, up_weight))
    active = low(jax.nn.silu(gate) * up_value)
    branch = low_back(matmul(active, down_weight))
    return resid + branch

def reference(tokens, segments, counts, cotangent, attn_gain, mlp_gain, query_weight, key_weight, value_weight, out_weight, gate_weight, up_weight, down_weight):
    params = (attn_gain.astype(jnp.float32), mlp_gain.astype(jnp.float32), query_weight.astype(jnp.float32), key_weight.astype(jnp.float32), value_weight.astype(jnp.float32), out_weight.astype(jnp.float32), gate_weight.astype(jnp.float32), up_weight.astype(jnp.float32), down_weight.astype(jnp.float32))
    packed = TOKENS // ROW
    xall = tokens.astype(jnp.float32).reshape(packed, ROW, D)
    segall = segments.reshape(packed, ROW)
    cotall = cotangent.astype(jnp.float32).reshape(packed, ROW, D)

    def step(total, items):
        xrow, segrow, count, cotrow = items
        index = jnp.arange(ROW, dtype=jnp.int32)
        live = index < count
        visible = (segrow[:, None] == segrow[None, :]) & (index[None, :] <= index[:, None]) & (live[None, :] | (index[None, :] == index[:, None]))
        cosine, sine = tables(segrow)
        output, backward = jax.vjp(lambda prm, xin: row_forward(prm, xin, visible, cosine, sine), params, xrow)
        grad_params, grad_x = backward(cotrow * live[:, None].astype(jnp.float32))
        total = jax.tree.map(lambda left, right: left + right, total, grad_params)
        return (total, (output.astype(jnp.bfloat16), grad_x.astype(jnp.bfloat16)))
    zeros = jax.tree.map(jnp.zeros_like, params)
    total, (outputs, grads) = lax.scan(step, zeros, (xall, segall, counts, cotall))
    return (outputs.reshape(TOKENS, D), grads.reshape(TOKENS, D), total[0], total[1], total[2], total[3], total[4], total[5], total[6], total[7], total[8])
```

```python
import functools

import jax
import jax.numpy as jnp
from jax import lax
from jax.experimental import pallas as pl
from jax.experimental.pallas import tpu as pltpu
from jax.sharding import PartitionSpec as P

HD = 64
EPS = 1e-05
THETA = 10000.0
NEGATIVE = -1e30
CHUNKS = 4
MESH = pl.DeviceIdType.MESH
BF = jnp.bfloat16
F32 = jnp.float32
ANY = pl.BlockSpec(memory_space=pl.ANY)
VMEM = pl.BlockSpec(memory_space=pltpu.VMEM)
LIMIT = 60 * 1024 * 1024


def nn(a, b):
    return lax.dot_general(a, b, (((1,), (0,)), ((), ())), preferred_element_type=F32)


def nt(a, b):
    return lax.dot_general(a, b, (((1,), (1,)), ((), ())), preferred_element_type=F32)


class Line:
    def __init__(self, piece):
        self.z = lax.axis_index("tensor")
        self.dp = lax.axis_index("dp")
        self.low = self.z < 2
        self.inner = jnp.where(self.low, self.z + 1, self.z - 1)
        self.outer = jnp.where(self.low, self.z - 1, self.z + 1)
        self.end = (self.z == 0) | (self.z == 3)
        self.mid = (self.z == 1) | (self.z == 2)
        self.piece = piece

    def at(self, m):
        place = jnp.where(self.low, m, 3 - m) * self.piece
        return pl.ds(pl.multiple_of(place, self.piece), self.piece)

    def own(self):
        return pl.ds(pl.multiple_of(self.z * self.piece, self.piece), self.piece)

    def copy(self, src, dst, send, recv, target):
        return pltpu.make_async_remote_copy(
            src_ref=src,
            dst_ref=dst,
            send_sem=send,
            recv_sem=recv,
            device_id=(self.dp, target),
            device_id_type=MESH,
        )

    def greet(self):
        barrier = pltpu.get_barrier_semaphore()
        pl.semaphore_signal(barrier, inc=1, device_id=(self.dp, self.inner), device_id_type=MESH)

        @pl.when(self.mid)
        def _():
            pl.semaphore_signal(
                barrier, inc=1, device_id=(self.dp, self.outer), device_id_type=MESH
            )
            pl.semaphore_wait(barrier, 2)

        @pl.when(self.end)
        def _():
            pl.semaphore_wait(barrier, 1)


class Reduce:
    def __init__(self, line, part, held, total, send, recv):
        self.line, self.part, self.held, self.total = line, part, held, total
        self.send, self.recv = send, recv

    def copy(self, c, m, slot, target, number):
        line = self.line
        return line.copy(
            self.part.at[c, line.at(m)],
            self.held.at[c, slot],
            self.send.at[c, number],
            self.recv.at[c, slot],
            target,
        )

    def arrived(self, c, slot):
        self.copy(c, 0, slot, self.line.inner, 0).wait_recv()

    def start(self, c):
        @pl.when(self.line.end)
        def _():
            for m in (3, 2, 1):
                self.copy(c, m, m - 1, self.line.inner, m - 1).start()

    def pass_in(self, c, m):
        line = self.line

        @pl.when(line.mid)
        def _():
            self.arrived(c, m - 1)
            rows = line.at(m)
            self.part[c, rows] = (
                self.part[c, rows].astype(F32) + self.held[c, m - 1].astype(F32)
            ).astype(BF)
            self.copy(c, m, 6 - m, line.inner, 3 - m).start()

    def pass_out(self, c):
        line = self.line

        @pl.when(line.mid)
        def _():
            self.arrived(c, 3)
            rows = line.at(0)
            self.part[c, rows] = (
                self.part[c, rows].astype(F32) + self.held[c, 3].astype(F32)
            ).astype(BF)
            self.copy(c, 0, 3, line.outer, 2).start()

    def finish(self, c):
        line = self.line

        @pl.when(line.end)
        def _():
            self.arrived(c, 3)
            self.total[...] = self.part[c, line.at(0)].astype(F32) + self.held[c, 3].astype(F32)

        @pl.when(line.mid)
        def _():
            self.arrived(c, 0)
            self.arrived(c, 4)
            self.total[...] = (
                self.part[c, line.at(1)].astype(F32)
                + self.held[c, 0].astype(F32)
                + self.held[c, 4].astype(F32)
            )

    def close(self, c):
        for number in range(3):
            self.copy(c, 0, 0, self.line.inner, number).wait_send()


class Gather:
    def __init__(self, line, own, full, send, recv, stay):
        self.line, self.own, self.full = line, own, full
        self.send, self.recv, self.stay = send, recv, stay
        self.chunk = 4 * line.piece

    def rows(self, c, m):
        line = self.line
        place = c * self.chunk + jnp.where(line.low, m, 3 - m) * line.piece
        return pl.ds(pl.multiple_of(place, line.piece), line.piece)

    def mine(self, c):
        line = self.line
        place = c * self.chunk + line.z * line.piece
        return pl.ds(pl.multiple_of(place, line.piece), line.piece)

    def first(self, c, slot, target, number):
        return self.line.copy(
            self.own.at[c],
            self.full.at[self.mine(c)],
            self.send.at[c, number],
            self.recv.at[c, slot],
            target,
        )

    def onward(self, c, m, slot, target, number):
        rows = self.rows(c, m)
        return self.line.copy(
            self.full.at[rows],
            self.full.at[rows],
            self.send.at[c, number],
            self.recv.at[c, slot],
            target,
        )

    def arrived(self, c, m):
        self.onward(c, m, m, self.line.inner, 0).wait_recv()

    def stays(self, c):
        return pltpu.make_async_copy(
            self.own.at[c], self.full.at[self.mine(c)], self.stay.at[c]
        )

    def start(self, c):
        line = self.line
        self.stays(c).start()

        @pl.when(line.end)
        def _():
            self.first(c, 0, line.inner, 0).start()

        @pl.when(line.mid)
        def _():
            self.first(c, 1, line.outer, 0).start()
            self.first(c, 2, line.inner, 1).start()

    def pass_near(self, c):
        line = self.line

        @pl.when(line.mid)
        def _():
            self.arrived(c, 0)
            self.onward(c, 0, 3, line.inner, 2).start()
            self.arrived(c, 2)
            self.onward(c, 2, 2, line.outer, 3).start()

    def pass_far(self, c):
        line = self.line

        @pl.when(line.mid)
        def _():
            self.arrived(c, 3)
            self.onward(c, 3, 3, line.outer, 4).start()

    def close(self, c):
        line = self.line
        self.stays(c).wait()

        @pl.when(line.end)
        def _():
            for m in (1, 2, 3):
                self.arrived(c, m)
            self.first(c, 0, line.inner, 0).wait_send()

        @pl.when(line.mid)
        def _():
            for number in range(5):
                self.first(c, 0, line.inner, number).wait_send()


def visible_bias(seg_row, key_row, c, chunk):
    keys = (c + 1) * chunk
    seg_q = seg_row[:, c * chunk : keys]
    seg_k = key_row[:keys, :]
    shape = (keys, chunk)
    key_at = lax.broadcasted_iota(jnp.int32, shape, 0)
    query_at = lax.broadcasted_iota(jnp.int32, shape, 1) + c * chunk
    seen = ((seg_k == seg_q) & (key_at < query_at)) | (key_at == query_at)
    return jnp.where(seen, 0.0, NEGATIVE)


def attn_kernel(
    chunks,
    tokens,
    gain,
    seg_row,
    seg_key,
    query_t,
    keys,
    values_t,
    out_weight,
    hidden2,
    resid,
    heads_out,
    logs,
    bias,
    heads_t,
    part,
    held,
    total,
    own,
    near,
    tok_sem,
    red_send,
    red_recv,
    gat_send,
    gat_recv,
    gat_stay,
):
    length, width = tokens.shape
    chunk = length // chunks
    piece = chunk // 4
    heads = query_t.shape[0] // HD
    line = Line(piece)
    red = Reduce(line, part, held, total, red_send, red_recv)
    gat = Gather(line, own, hidden2, gat_send, gat_recv, gat_stay)
    for c in range(chunks):
        pltpu.make_async_copy(tokens.at[gat.mine(c)], near.at[c], tok_sem.at[c]).start()
    line.greet()

    def attend(c):
        keys_n = (c + 1) * chunk
        cols = slice(c * chunk, keys_n)
        bias[:keys_n, :] = visible_bias(seg_row[...], seg_key[...], c, chunk)

        def head(h, carry):
            here = pl.ds(pl.multiple_of(h * HD, HD), HD)
            scores = nn(keys[:keys_n, :], query_t[here, cols]) + bias[:keys_n, :]
            peak = jnp.max(scores, axis=0, keepdims=True)
            weights = jnp.exp(scores - peak)
            sums = jnp.sum(weights, axis=0, keepdims=True)
            probs = (weights * (1.0 / sums)).astype(BF)
            heads_t[here, :] = nn(values_t[:, :keys_n], probs)
            logs[h, :, cols] = peak + jnp.log(sums)
            return carry

        lax.fori_loop(0, heads, head, 0)
        heads_c = heads_t[...].T.astype(BF)
        heads_out[cols, :] = heads_c
        step = min(512, width)
        for n in range(0, width, step):
            part[c, :, n : n + step] = nn(heads_c, out_weight[:, n : n + step]).astype(BF)

    def norm(c):
        pltpu.make_async_copy(tokens.at[gat.mine(c)], near.at[c], tok_sem.at[c]).wait()
        vector = near[c].astype(F32) + total[...]
        resid[c] = vector
        scale = lax.rsqrt(jnp.mean(vector * vector, axis=-1, keepdims=True) + EPS)
        own[c] = (vector * scale * gain[...]).astype(BF)

    order = list(reversed(range(chunks)))
    for i in range(chunks + 2):
        now = order[i] if i < chunks else None
        last = order[i - 1] if 0 <= i - 1 < chunks else None
        older = order[i - 2] if i - 2 >= 0 else None
        if now is not None:
            attend(now)
            red.start(now)
        if last is not None:
            red.pass_in(last, 3)
        if older is not None:
            gat.pass_near(older)
        if last is not None:
            red.pass_in(last, 2)
        if older is not None:
            gat.pass_far(older)
        if last is not None:
            red.pass_out(last)
            red.finish(last)
            norm(last)
            gat.start(last)
    for c in order:
        red.close(c)
        gat.close(c)


def mlp_kernel(
    chunks,
    hidden2,
    resid,
    upstream,
    gain,
    gate_weight,
    up_weight,
    down_weight,
    mixed,
    branch,
    grad_resid,
    grad_gain,
    active,
    grad_gate,
    grad_up,
    wg,
    wu,
    wd,
    hid,
    dy,
    act_c,
    gate_c,
    up_c,
    part_a,
    part_b,
    held_a,
    held_b,
    total,
    own_a,
    own_b,
    near,
    w_sem,
    in_sem,
    out_sem,
    near_sem,
    red_send_a,
    red_recv_a,
    red_send_b,
    red_recv_b,
    gat_send_a,
    gat_recv_a,
    gat_stay_a,
    gat_send_b,
    gat_recv_b,
    gat_stay_b,
):
    length, width = hidden2.shape
    chunk = length // chunks
    piece = chunk // 4
    units = wg.shape[1]
    line = Line(piece)
    red_a = Reduce(line, part_a, held_a, total, red_send_a, red_recv_a)
    red_b = Reduce(line, part_b, held_b, total, red_send_b, red_recv_b)
    gat_a = Gather(line, own_a, branch, gat_send_a, gat_recv_a, gat_stay_a)
    gat_b = Gather(line, own_b, mixed, gat_send_b, gat_recv_b, gat_stay_b)
    order = list(reversed(range(chunks)))

    def load(c, slot):
        rows = slice(c * chunk, (c + 1) * chunk)
        return (
            pltpu.make_async_copy(hidden2.at[rows], hid.at[slot], in_sem.at[slot, 0]),
            pltpu.make_async_copy(upstream.at[rows], dy.at[slot], in_sem.at[slot, 1]),
        )

    def near_copy(c):
        return pltpu.make_async_copy(upstream.at[gat_a.mine(c)], near.at[c], near_sem.at[c])

    weights = [
        pltpu.make_async_copy(src, dst, w_sem.at[i])
        for i, (src, dst) in enumerate(((gate_weight, wg), (up_weight, wu), (down_weight, wd)))
    ]
    for copy in load(order[0], 0):
        copy.start()
    for copy in weights:
        copy.start()
    for c in range(chunks):
        near_copy(c).start()
    line.greet()
    grad_gain[...] = jnp.zeros_like(grad_gain)

    def saves(c, slot):
        rows = slice(c * chunk, (c + 1) * chunk)
        return [
            pltpu.make_async_copy(src.at[slot], dst.at[rows], out_sem.at[slot, i])
            for i, (src, dst) in enumerate(((act_c, active), (gate_c, grad_gate), (up_c, grad_up)))
        ]

    def feed(i):
        c, slot = order[i], i % 2
        for copy in load(c, slot):
            copy.wait()
        if i == 0:
            for copy in weights:
                copy.wait()
        if i + 1 < chunks:
            for copy in load(order[i + 1], 1 - slot):
                copy.start()
        if i >= 2:
            for copy in saves(order[i - 2], slot):
                copy.wait()
        step = 512
        for n in range(0, units, step):
            cols = slice(n, min(n + step, units))
            gate = nn(hid[slot], wg[:, cols])
            up = nn(hid[slot], wu[:, cols])
            grad = nt(dy[slot], wd[cols, :])
            sig = 1.0 / (1.0 + jnp.exp(-gate))
            silu = gate * sig
            act_c[slot, :, cols] = (silu * up).astype(BF)
            gate_c[slot, :, cols] = (grad * up * sig * (1.0 + gate * (1.0 - sig))).astype(BF)
            up_c[slot, :, cols] = (grad * silu).astype(BF)
        for copy in saves(c, slot):
            copy.start()
        for n in range(0, width, step):
            cols = slice(n, n + step)
            part_a[c, :, cols] = (
                nt(gate_c[slot], wg[cols, :]) + nt(up_c[slot], wu[cols, :])
            ).astype(BF)
        red_a.start(c)
        for n in range(0, width, step):
            cols = slice(n, n + step)
            part_b[c, :, cols] = nn(act_c[slot], wd[:, cols]).astype(BF)

    def done_a(c):
        near_copy(c).wait()
        grad = total[...]
        vector = resid[c]
        scale = lax.rsqrt(jnp.mean(vector * vector, axis=-1, keepdims=True) + EPS)
        scaled = grad * gain[...]
        inner = jnp.mean(scaled * vector, axis=-1, keepdims=True)
        grad_gain[...] += jnp.sum(grad * vector * scale, axis=0, keepdims=True)
        back = near[c].astype(F32) + scale * scaled - vector * (scale * scale * scale) * inner
        grad_resid[c] = back
        own_a[c] = back.astype(BF)

    def done_b(c):
        own_b[c] = (resid[c] + total[...]).astype(BF)

    slots = [(red_a, gat_a, done_a, c) for c in order] + [(red_b, gat_b, done_b, c) for c in order]
    for i in range(len(slots) + 2):
        if i < chunks:
            feed(i)
        elif i < len(slots):
            red_b.start(slots[i][3])
        last = slots[i - 1] if 0 <= i - 1 < len(slots) else None
        older = slots[i - 2] if i - 2 >= 0 else None
        if last is not None:
            last[0].pass_in(last[3], 3)
        if older is not None:
            older[1].pass_near(older[3])
        if last is not None:
            last[0].pass_in(last[3], 2)
        if older is not None:
            older[1].pass_far(older[3])
        if last is not None:
            red, gat, done, c = last
            red.pass_out(c)
            red.finish(c)
            done(c)
            gat.start(c)
    for i in range(max(0, chunks - 2), chunks):
        for copy in saves(order[i], i % 2):
            copy.wait()
    for red, gat, done, c in slots:
        red.close(c)
        gat.close(c)


def back_kernel(
    chunks,
    branch,
    tokens,
    grad_resid,
    gain,
    seg_row,
    seg_key,
    cosine,
    sine,
    query_t,
    query,
    keys,
    keys_t,
    values,
    logs,
    out_weight,
    query_weight,
    kv_weight,
    tokens_grad,
    grad_gain,
    grad_query,
    grad_kv,
    bias,
    dy,
    do_t,
    do_h,
    dq_t,
    dk,
    dv,
    part,
    held,
    total,
    own,
    near,
    in_sem,
    tok_sem,
    red_send,
    red_recv,
    gat_send,
    gat_recv,
    gat_stay,
):
    length, width = tokens.shape
    chunk = length // chunks
    piece = chunk // 4
    heads = query.shape[0]
    half = HD // 2
    factor = HD ** (-0.5)
    line = Line(piece)
    red = Reduce(line, part, held, total, red_send, red_recv)
    gat = Gather(line, own, tokens_grad, gat_send, gat_recv, gat_stay)
    order = list(reversed(range(chunks)))

    def load(c, slot):
        return pltpu.make_async_copy(
            branch.at[c * chunk : (c + 1) * chunk], dy.at[slot], in_sem.at[slot]
        )

    def near_copy(c):
        return pltpu.make_async_copy(tokens.at[gat.mine(c)], near.at[c], tok_sem.at[c])

    load(order[0], 0).start()
    for c in range(chunks):
        near_copy(c).start()
    line.greet()
    grad_gain[...] = jnp.zeros_like(grad_gain)
    dk[...] = jnp.zeros_like(dk)
    dv[...] = jnp.zeros_like(dv)

    def unrope(t, cols):
        first, second = t[:half], t[half:]
        cos, sin = cosine[:, cols], sine[:, cols]
        return jnp.concatenate([first * cos + second * sin, second * cos - first * sin], axis=0)

    def attend(i):
        c, slot = order[i], i % 2
        load(c, slot).wait()
        if i + 1 < chunks:
            load(order[i + 1], 1 - slot).start()
        keys_n = (c + 1) * chunk
        cols = slice(c * chunk, keys_n)
        bias[:keys_n, :] = visible_bias(seg_row[...], seg_key[...], c, chunk)
        grad_heads = nt(dy[slot], out_weight[...])
        do_t[...] = grad_heads.T.astype(BF)
        for h in range(heads):
            do_h[h] = grad_heads[:, h * HD : (h + 1) * HD].astype(BF)

        def head(h, carry):
            here = pl.ds(pl.multiple_of(h * HD, HD), HD)
            scores = nn(keys[:keys_n, :], query_t[here, cols]) + bias[:keys_n, :]
            probs = jnp.exp(scores - logs[h, :, cols])
            grad_probs = nn(values[:keys_n, :], do_t[here, :])
            delta = jnp.sum(probs * grad_probs, axis=0, keepdims=True)
            grad_scores = (probs * (grad_probs - delta)).astype(BF)
            dv[:keys_n, :] += nn(probs.astype(BF), do_h[h])
            dk[:keys_n, :] += nn(grad_scores, query[h, cols, :])
            grad = nn(keys_t[:, :keys_n], grad_scores) * factor
            dq_t[here, :] = unrope(grad, cols)
            return carry

        lax.fori_loop(0, heads, head, 0)
        grad_q = dq_t[...].T.astype(BF)
        grad_query[cols, :] = grad_q
        grad_k = unrope(dk[cols, :].T, cols).T
        both = jnp.concatenate([grad_k, dv[cols, :]], axis=1).astype(BF)
        grad_kv[cols, :] = both
        step = min(512, width)
        for n in range(0, width, step):
            here = slice(n, n + step)
            part[c, :, here] = (
                nt(grad_q, query_weight[here, :]) + nt(both, kv_weight[here, :])
            ).astype(BF)

    def done(c):
        near_copy(c).wait()
        grad = total[...]
        vector = near[c].astype(F32)
        scale = lax.rsqrt(jnp.mean(vector * vector, axis=-1, keepdims=True) + EPS)
        scaled = grad * gain[...]
        inner = jnp.mean(scaled * vector, axis=-1, keepdims=True)
        grad_gain[...] += jnp.sum(grad * vector * scale, axis=0, keepdims=True)
        back = grad_resid[c] + scale * scaled - vector * (scale * scale * scale) * inner
        own[c] = back.astype(BF)

    for i in range(chunks + 2):
        now = order[i] if i < chunks else None
        last = order[i - 1] if 0 <= i - 1 < chunks else None
        older = order[i - 2] if i - 2 >= 0 else None
        if now is not None:
            attend(i)
            red.start(now)
        if last is not None:
            red.pass_in(last, 3)
        if older is not None:
            gat.pass_near(older)
        if last is not None:
            red.pass_in(last, 2)
        if older is not None:
            gat.pass_far(older)
        if last is not None:
            red.pass_out(last)
            red.finish(last)
            done(last)
            gat.start(last)
    for c in order:
        red.close(c)
        gat.close(c)


def call(kernel, ins, outs, scratch, number, cost):
    return pl.pallas_call(
        kernel,
        in_specs=[spec for spec, _ in ins],
        out_specs=[spec for spec, _, _ in outs],
        out_shape=[jax.ShapeDtypeStruct(shape, kind) for _, shape, kind in outs],
        scratch_shapes=scratch,
        compiler_params=pltpu.CompilerParams(
            collective_id=number, has_side_effects=True, vmem_limit_bytes=LIMIT
        ),
        cost_estimate=pl.CostEstimate(flops=cost, bytes_accessed=cost // 1000, transcendentals=0),
    )(*[array for _, array in ins])


def line_scratch(chunks, piece, width):
    dma = pltpu.SemaphoreType.DMA
    buffers = [
        pltpu.VMEM((chunks, 4 * piece, width), BF),
        pltpu.VMEM((chunks, 5, piece, width), BF),
        pltpu.VMEM((chunks, piece, width), BF),
    ]
    sems = [dma((chunks, 3)), dma((chunks, 5)), dma((chunks, 5)), dma((chunks, 4)), dma((chunks,))]
    return buffers, sems


def tables(seg_row):
    length = seg_row.shape[0]
    start = jnp.sum((seg_row[None, :] < seg_row[:, None]).astype(jnp.int32), axis=1)
    place = (jnp.arange(length, dtype=jnp.int32) - start).astype(F32)
    half = HD // 2
    freq = jnp.power(jnp.float32(THETA), -jnp.arange(half, dtype=F32) / half)
    angle = freq[:, None] * place[None, :]
    return jnp.cos(angle), jnp.sin(angle)


def rope_t(raw, cosine, sine):
    heads = raw.shape[0] // HD
    raw = raw.reshape(heads, HD, -1)
    first, second = raw[:, : HD // 2], raw[:, HD // 2 :]
    return jnp.concatenate(
        [first * cosine - second * sine, second * cosine + first * sine], axis=1
    )


def tn(a, b):
    return lax.dot_general(a, b, (((0,), (0,)), ((), ())), preferred_element_type=F32)


def local(
    tokens,
    segments,
    counts,
    cotangent,
    attn_gain,
    mlp_gain,
    query_weight,
    key_weight,
    value_weight,
    out_weight,
    gate_weight,
    up_weight,
    down_weight,
):
    length, width = tokens.shape
    units = gate_weight.shape[1]
    lanes = query_weight.shape[1]
    heads = lanes // HD
    chunks = CHUNKS
    chunk = length // chunks
    piece = chunk // 4
    dma = pltpu.SemaphoreType.DMA

    live = jnp.arange(length, dtype=jnp.int32) < counts[0]
    seg_row = segments.reshape(1, length)
    seg_key = jnp.where(live, segments, -1).reshape(length, 1)
    cosine, sine = tables(segments)
    xfull = tokens.astype(F32)
    scale1 = lax.rsqrt(jnp.mean(xfull * xfull, axis=-1, keepdims=True) + EPS)
    hidden1 = (xfull * scale1 * attn_gain).astype(BF)
    dims = (((0,), (1,)), ((), ()))
    query_raw = lax.dot_general(query_weight, hidden1, dims, preferred_element_type=F32)
    key_raw = lax.dot_general(key_weight, hidden1, dims, preferred_element_type=F32)
    values = jnp.dot(hidden1, value_weight, preferred_element_type=F32).astype(BF)
    query_h = rope_t(query_raw, cosine, sine).astype(BF) * BF(HD ** (-0.5))
    keys_t = rope_t(key_raw, cosine, sine).astype(BF)[0]
    query_t = query_h.reshape(lanes, length)
    query = query_h.transpose(0, 2, 1)
    keys = keys_t.T
    values_t = values.T
    gain1 = attn_gain.reshape(1, width)
    gain2 = mlp_gain.reshape(1, width)
    upstream = jnp.where(live[:, None], cotangent, BF(0))

    buffers, sems = line_scratch(chunks, piece, width)
    total = pltpu.VMEM((piece, width), F32)
    near = pltpu.VMEM((chunks, piece, width), BF)
    hidden2, resid, heads_out, logs = call(
        functools.partial(attn_kernel, chunks),
        [
            (ANY, tokens),
            (VMEM, gain2),
            (VMEM, seg_row),
            (VMEM, seg_key),
            (VMEM, query_t),
            (VMEM, keys),
            (VMEM, values_t),
            (VMEM, out_weight),
        ],
        [
            (ANY, (length, width), BF),
            (VMEM, (chunks, piece, width), F32),
            (VMEM, (length, lanes), BF),
            (VMEM, (heads, 1, length), F32),
        ],
        [
            pltpu.VMEM((length, chunk), F32),
            pltpu.VMEM((lanes, chunk), F32),
            buffers[0],
            buffers[1],
            total,
            buffers[2],
            near,
            dma((chunks,)),
            *sems,
        ],
        0,
        10**10,
    )

    mixed, branch, grad_resid, grad_gain2, active, grad_gate, grad_up = call(
        functools.partial(mlp_kernel, chunks),
        [
            (ANY, hidden2),
            (VMEM, resid),
            (ANY, upstream),
            (VMEM, gain2),
            (ANY, gate_weight),
            (ANY, up_weight),
            (ANY, down_weight),
        ],
        [
            (ANY, (length, width), BF),
            (ANY, (length, width), BF),
            (VMEM, (chunks, piece, width), F32),
            (VMEM, (1, width), F32),
            (ANY, (length, units), BF),
            (ANY, (length, units), BF),
            (ANY, (length, units), BF),
        ],
        [
            pltpu.VMEM((width, units), BF),
            pltpu.VMEM((width, units), BF),
            pltpu.VMEM((units, width), BF),
            pltpu.VMEM((2, chunk, width), BF),
            pltpu.VMEM((2, chunk, width), BF),
            pltpu.VMEM((2, chunk, units), BF),
            pltpu.VMEM((2, chunk, units), BF),
            pltpu.VMEM((2, chunk, units), BF),
            buffers[0],
            buffers[0],
            buffers[1],
            buffers[1],
            total,
            buffers[2],
            buffers[2],
            near,
            dma((3,)),
            dma((2, 2)),
            dma((2, 3)),
            dma((chunks,)),
            sems[0],
            sems[1],
            sems[0],
            sems[1],
            *sems[2:],
            *sems[2:],
        ],
        1,
        4 * 10**10,
    )

    tokens_grad, grad_gain1, grad_query, grad_kv = call(
        functools.partial(back_kernel, chunks),
        [
            (ANY, branch),
            (ANY, tokens),
            (VMEM, grad_resid),
            (VMEM, gain1),
            (VMEM, seg_row),
            (VMEM, seg_key),
            (VMEM, cosine),
            (VMEM, sine),
            (VMEM, query_t),
            (VMEM, query),
            (VMEM, keys),
            (VMEM, keys_t),
            (VMEM, values),
            (VMEM, logs),
            (VMEM, out_weight),
            (VMEM, query_weight),
            (VMEM, jnp.concatenate([key_weight, value_weight], axis=1)),
        ],
        [
            (ANY, (length, width), BF),
            (VMEM, (1, width), F32),
            (VMEM, (length, lanes), BF),
            (VMEM, (length, 2 * HD), BF),
        ],
        [
            pltpu.VMEM((length, chunk), F32),
            pltpu.VMEM((2, chunk, width), BF),
            pltpu.VMEM((lanes, chunk), BF),
            pltpu.VMEM((heads, chunk, HD), BF),
            pltpu.VMEM((lanes, chunk), F32),
            pltpu.VMEM((length, HD), F32),
            pltpu.VMEM((length, HD), F32),
            buffers[0],
            buffers[1],
            total,
            buffers[2],
            near,
            dma((2,)),
            dma((chunks,)),
            *sems,
        ],
        2,
        2 * 10**10,
    )

    gains = lax.psum(jnp.concatenate([grad_gain1, grad_gain2], axis=0), "tensor")
    gains = lax.psum_scatter(gains, "dp", scatter_dimension=1, tiled=True)

    def scattered(array, dim):
        return lax.psum_scatter(
            array.astype(BF), "dp", scatter_dimension=dim, tiled=True
        ).astype(F32)

    grad_qkv = tn(hidden1, jnp.concatenate([grad_query, grad_kv], axis=1))
    grad_qkv = scattered(grad_qkv, 0)
    return (
        mixed,
        tokens_grad,
        gains[0],
        gains[1],
        grad_qkv[:, :lanes],
        grad_qkv[:, lanes : lanes + HD],
        grad_qkv[:, lanes + HD :],
        scattered(tn(heads_out, branch), 1),
        scattered(tn(hidden2, grad_gate), 0),
        scattered(tn(hidden2, grad_up), 0),
        scattered(tn(active, upstream), 1),
    )


def solution(mesh):
    placed = (
        P("dp", None),
        P("dp"),
        P("dp"),
        P("dp", None),
        P(),
        P(),
        P(None, "tensor"),
        P(None, "tensor"),
        P(None, "tensor"),
        P("tensor", None),
        P(None, "tensor"),
        P(None, "tensor"),
        P("tensor", None),
    )
    return jax.shard_map(
        local,
        mesh=mesh,
        in_specs=placed,
        out_specs=(
            P("dp", None),
            P("dp", None),
            P("dp"),
            P("dp"),
            P("dp", "tensor"),
            P("dp", "tensor"),
            P("dp", "tensor"),
            P("tensor", "dp"),
            P("dp", "tensor"),
            P("dp", "tensor"),
            P("tensor", "dp"),
        ),
        check_vma=False,
    )
```

```python
import functools

import jax
import jax.numpy as jnp
from jax import lax
from jax.experimental import pallas as pl
from jax.experimental.pallas import tpu as pltpu
from jax.sharding import PartitionSpec as P

HD = 64
EPS = 1e-05
THETA = 10000.0
NEGATIVE = -1e30
CHUNKS = 4
MESH = pl.DeviceIdType.MESH
BF = jnp.bfloat16
F32 = jnp.float32
ANY = pl.BlockSpec(memory_space=pl.ANY)
VMEM = pl.BlockSpec(memory_space=pltpu.VMEM)
LIMIT = 60 * 1024 * 1024


def nn(a, b):
    return lax.dot_general(a, b, (((1,), (0,)), ((), ())), preferred_element_type=F32)


def nt(a, b):
    return lax.dot_general(a, b, (((1,), (1,)), ((), ())), preferred_element_type=F32)


def tn(a, b):
    return lax.dot_general(a, b, (((0,), (0,)), ((), ())), preferred_element_type=F32)


class Line:
    def __init__(self, piece):
        self.z = lax.axis_index("tensor")
        self.dp = lax.axis_index("dp")
        self.low = self.z < 2
        self.inner = jnp.where(self.low, self.z + 1, self.z - 1)
        self.outer = jnp.where(self.low, self.z - 1, self.z + 1)
        self.end = (self.z == 0) | (self.z == 3)
        self.mid = (self.z == 1) | (self.z == 2)
        self.piece = piece

    def at(self, m):
        place = jnp.where(self.low, m, 3 - m) * self.piece
        return pl.ds(pl.multiple_of(place, self.piece), self.piece)

    def own(self):
        return pl.ds(pl.multiple_of(self.z * self.piece, self.piece), self.piece)

    def copy(self, src, dst, send, recv, target):
        return pltpu.make_async_remote_copy(
            src_ref=src,
            dst_ref=dst,
            send_sem=send,
            recv_sem=recv,
            device_id=(self.dp, target),
            device_id_type=MESH,
        )

    def greet(self, dps=2):
        barrier = pltpu.get_barrier_semaphore()
        pl.semaphore_signal(barrier, inc=1, device_id=(self.dp, self.inner), device_id_type=MESH)
        self.groups = dps // 2
        self.core = lax.rem(self.dp, 2)
        self.partner = self.dp + 1 - 2 * self.core
        others = [self.partner] + [self.peer(j) for j in range(1, self.groups)]
        extra = 0 if dps == 2 else len(others)
        for other in others[:extra]:
            pl.semaphore_signal(barrier, inc=1, device_id=(other, self.z), device_id_type=MESH)

        @pl.when(self.mid)
        def _():
            pl.semaphore_signal(
                barrier, inc=1, device_id=(self.dp, self.outer), device_id_type=MESH
            )
            pl.semaphore_wait(barrier, 2 + extra)

        @pl.when(self.end)
        def _():
            pl.semaphore_wait(barrier, 1 + extra)

    def group(self, j):
        return lax.rem(self.dp // 2 + j, self.groups)

    def peer(self, j):
        return 2 * self.group(j) + self.core


class Reduce:
    def __init__(self, line, part, held, total, send, recv):
        self.line, self.part, self.held, self.total = line, part, held, total
        self.send, self.recv = send, recv

    def copy(self, c, m, slot, target, number):
        line = self.line
        return line.copy(
            self.part.at[c, line.at(m)],
            self.held.at[c, slot],
            self.send.at[c, number],
            self.recv.at[c, slot],
            target,
        )

    def arrived(self, c, slot):
        self.copy(c, 0, slot, self.line.inner, 0).wait_recv()

    def start(self, c):
        @pl.when(self.line.end)
        def _():
            for m in (3, 2, 1):
                self.copy(c, m, m - 1, self.line.inner, m - 1).start()

    def pass_in(self, c, m):
        line = self.line

        @pl.when(line.mid)
        def _():
            self.arrived(c, m - 1)
            rows = line.at(m)
            self.part[c, rows] = (
                self.part[c, rows].astype(F32) + self.held[c, m - 1].astype(F32)
            ).astype(BF)
            self.copy(c, m, 6 - m, line.inner, 3 - m).start()

    def pass_out(self, c):
        line = self.line

        @pl.when(line.mid)
        def _():
            self.arrived(c, 3)
            rows = line.at(0)
            self.part[c, rows] = (
                self.part[c, rows].astype(F32) + self.held[c, 3].astype(F32)
            ).astype(BF)
            self.copy(c, 0, 3, line.outer, 2).start()

    def finish(self, c):
        line = self.line

        @pl.when(line.end)
        def _():
            self.arrived(c, 3)
            self.total[...] = self.part[c, line.at(0)].astype(F32) + self.held[c, 3].astype(F32)

        @pl.when(line.mid)
        def _():
            self.arrived(c, 0)
            self.arrived(c, 4)
            self.total[...] = (
                self.part[c, line.at(1)].astype(F32)
                + self.held[c, 0].astype(F32)
                + self.held[c, 4].astype(F32)
            )

    def close(self, c):
        for number in range(3):
            self.copy(c, 0, 0, self.line.inner, number).wait_send()


class Spread:
    def __init__(self, line, stage, out, taken, sums, moved, sems):
        self.line, self.stage, self.out = line, stage, out
        self.taken, self.sums, self.moved = taken, sums, moved
        self.send1, self.recv1, self.send2, self.recv2, self.stay = sems

    def give(self, j):
        line = self.line
        return pltpu.make_async_remote_copy(
            src_ref=self.stage.at[1 - line.core],
            dst_ref=self.taken.at[j],
            send_sem=self.send1.at[j],
            recv_sem=self.recv1.at[j],
            device_id=(line.partner, line.z),
            device_id_type=MESH,
        )

    def move(self, j):
        line = self.line
        return pltpu.make_async_remote_copy(
            src_ref=self.sums.at[j],
            dst_ref=self.moved.at[j],
            send_sem=self.send2.at[j],
            recv_sem=self.recv2.at[j],
            device_id=(line.peer(j), line.z),
            device_id_type=MESH,
        )

    def merge_load(self, j):
        self.give(j).wait()
        self.load(self.taken.at[j], 1 - self.line.core).start()

    def load(self, src, slot):
        return pltpu.make_async_copy(src, self.stage.at[slot], self.stay.at[slot])

    def merge_add(self, j):
        core = self.line.core
        self.load(self.taken.at[j], 1 - core).wait()
        self.stage[core] = (
            self.stage[core].astype(F32) + self.stage[1 - core].astype(F32)
        ).astype(BF)
        pltpu.make_async_copy(self.stage.at[core], self.sums.at[j], self.stay.at[core]).start()

    def merge_move(self, j):
        core = self.line.core
        pltpu.make_async_copy(self.stage.at[core], self.sums.at[j], self.stay.at[core]).wait()
        if j:
            self.move(j).start()

    def sources(self):
        return [self.sums.at[0]] + [self.moved.at[j] for j in range(1, self.line.groups)]

    def last_load(self):
        self.load(self.sources()[0], 0).start()

    def last(self):
        sources = self.sources()
        for j, source in enumerate(sources):
            if j + 1 < len(sources):
                self.move(j + 1).wait()
                self.load(sources[j + 1], (j + 1) % 2).start()
            self.load(source, j % 2).wait()
            block = self.stage[j % 2].astype(F32)
            if j:
                self.out[...] += block
            else:
                self.out[...] = block


def merged(spreads, j):
    for spread in spreads:
        spread.merge_load(j)
    for spread in spreads:
        spread.merge_add(j)
    for spread in spreads:
        spread.merge_move(j)


def finished(spreads):
    for spread in spreads:
        spread.last_load()
    for spread in spreads:
        spread.last()


def halves(stage, value, dim):
    size = value.shape[dim] // 2
    if dim == 0:
        stage[0] = value[:size].astype(BF)
        stage[1] = value[size:].astype(BF)
    else:
        stage[0] = value[:, :size].astype(BF)
        stage[1] = value[:, size:].astype(BF)


class Gather:
    def __init__(self, line, own, full, send, recv, stay):
        self.line, self.own, self.full = line, own, full
        self.send, self.recv, self.stay = send, recv, stay
        self.chunk = 4 * line.piece

    def rows(self, c, m):
        line = self.line
        place = c * self.chunk + jnp.where(line.low, m, 3 - m) * line.piece
        return pl.ds(pl.multiple_of(place, line.piece), line.piece)

    def mine(self, c):
        line = self.line
        place = c * self.chunk + line.z * line.piece
        return pl.ds(pl.multiple_of(place, line.piece), line.piece)

    def first(self, c, slot, target, number):
        return self.line.copy(
            self.own.at[c],
            self.full.at[self.mine(c)],
            self.send.at[c, number],
            self.recv.at[c, slot],
            target,
        )

    def onward(self, c, m, slot, target, number):
        rows = self.rows(c, m)
        return self.line.copy(
            self.full.at[rows],
            self.full.at[rows],
            self.send.at[c, number],
            self.recv.at[c, slot],
            target,
        )

    def arrived(self, c, m):
        self.onward(c, m, m, self.line.inner, 0).wait_recv()

    def stays(self, c):
        return pltpu.make_async_copy(
            self.own.at[c], self.full.at[self.mine(c)], self.stay.at[c]
        )

    def start(self, c):
        line = self.line
        self.stays(c).start()

        @pl.when(line.end)
        def _():
            self.first(c, 0, line.inner, 0).start()

        @pl.when(line.mid)
        def _():
            self.first(c, 1, line.outer, 0).start()
            self.first(c, 2, line.inner, 1).start()

    def pass_near(self, c):
        line = self.line

        @pl.when(line.end)
        def _():
            self.arrived(c, 1)

        @pl.when(line.mid)
        def _():
            self.arrived(c, 0)
            self.onward(c, 0, 3, line.inner, 2).start()
            self.arrived(c, 2)
            self.onward(c, 2, 2, line.outer, 3).start()

    def pass_far(self, c):
        line = self.line

        @pl.when(line.mid)
        def _():
            self.arrived(c, 3)
            self.onward(c, 3, 3, line.outer, 4).start()

    def close(self, c):
        line = self.line
        self.stays(c).wait()

        @pl.when(line.end)
        def _():
            for m in (2, 3):
                self.arrived(c, m)
            self.first(c, 0, line.inner, 0).wait_send()

        @pl.when(line.mid)
        def _():
            for number in range(5):
                self.first(c, 0, line.inner, number).wait_send()


def visible_bias(seg_row, key_row, c, chunk):
    keys = (c + 1) * chunk
    seg_q = seg_row[:, c * chunk : keys]
    seg_k = key_row[:keys, :]
    shape = (keys, chunk)
    key_at = lax.broadcasted_iota(jnp.int32, shape, 0)
    query_at = lax.broadcasted_iota(jnp.int32, shape, 1) + c * chunk
    seen = ((seg_k == seg_q) & (key_at < query_at)) | (key_at == query_at)
    return jnp.where(seen, 0.0, NEGATIVE)


def attn_kernel(
    chunks,
    tokens,
    gain,
    seg_row,
    seg_key,
    query_t,
    keys,
    values_t,
    out_weight,
    hidden2,
    resid,
    heads_out,
    logs,
    bias,
    heads_t,
    part,
    held,
    total,
    own,
    near,
    tok_sem,
    red_send,
    red_recv,
    gat_send,
    gat_recv,
    gat_stay,
):
    length, width = tokens.shape
    chunk = length // chunks
    piece = chunk // 4
    heads = query_t.shape[0] // HD
    line = Line(piece)
    red = Reduce(line, part, held, total, red_send, red_recv)
    gat = Gather(line, own, hidden2, gat_send, gat_recv, gat_stay)
    for c in range(chunks):
        pltpu.make_async_copy(tokens.at[gat.mine(c)], near.at[c], tok_sem.at[c]).start()
    line.greet()

    def attend(c):
        keys_n = (c + 1) * chunk
        cols = slice(c * chunk, keys_n)
        bias[:keys_n, :] = visible_bias(seg_row[...], seg_key[...], c, chunk)

        def head(h, carry):
            here = pl.ds(pl.multiple_of(h * HD, HD), HD)
            scores = nn(keys[:keys_n, :], query_t[here, cols]) + bias[:keys_n, :]
            peak = jnp.max(scores, axis=0, keepdims=True)
            weights = jnp.exp(scores - peak)
            sums = jnp.sum(weights, axis=0, keepdims=True)
            probs = (weights * (1.0 / sums)).astype(BF)
            heads_t[here, :] = nn(values_t[:, :keys_n], probs)
            logs[h, :, cols] = peak + jnp.log(sums)
            return carry

        lax.fori_loop(0, heads, head, 0)
        heads_c = heads_t[...].T.astype(BF)
        heads_out[cols, :] = heads_c
        step = min(512, width)
        for n in range(0, width, step):
            part[c, :, n : n + step] = nn(heads_c, out_weight[:, n : n + step]).astype(BF)

    def norm(c):
        pltpu.make_async_copy(tokens.at[gat.mine(c)], near.at[c], tok_sem.at[c]).wait()
        vector = near[c].astype(F32) + total[...]
        resid[c] = vector
        scale = lax.rsqrt(jnp.mean(vector * vector, axis=-1, keepdims=True) + EPS)
        own[c] = (vector * scale * gain[...]).astype(BF)

    order = list(reversed(range(chunks)))
    for i in range(chunks + 2):
        now = order[i] if i < chunks else None
        last = order[i - 1] if 0 <= i - 1 < chunks else None
        older = order[i - 2] if i - 2 >= 0 else None
        if now is not None:
            attend(now)
            red.start(now)
        if last is not None:
            red.pass_in(last, 3)
        if older is not None:
            gat.pass_near(older)
        if last is not None:
            red.pass_in(last, 2)
        if older is not None:
            gat.pass_far(older)
        if last is not None:
            red.pass_out(last)
            red.finish(last)
            norm(last)
            gat.start(last)
    for c in order:
        red.close(c)
        gat.close(c)


def mlp_kernel(
    chunks,
    dps,
    hidden2,
    resid,
    upstream,
    gain,
    gate_weight,
    up_weight,
    down_weight,
    mixed,
    branch,
    grad_resid,
    grad_gain,
    gate_out,
    up_out,
    down_out,
    active,
    grad_gate,
    grad_up,
    gate_taken,
    gate_sums,
    gate_moved,
    up_taken,
    up_sums,
    up_moved,
    down_taken,
    down_sums,
    down_moved,
    wg,
    wu,
    wd,
    hid,
    dy,
    act_c,
    gate_c,
    up_c,
    part_a,
    part_b,
    held,
    gate_stage,
    up_stage,
    down_stage,
    total,
    own_a,
    own_b,
    near,
    w_sem,
    in_sem,
    out_sem,
    near_sem,
    red_send_a,
    red_recv_a,
    red_send_b,
    red_recv_b,
    gat_send_a,
    gat_recv_a,
    gat_stay_a,
    gat_send_b,
    gat_recv_b,
    gat_stay_b,
    turn_sem,
    pair_sem,
    *dp_sems,
):
    length, width = hidden2.shape
    chunk = length // chunks
    piece = chunk // 4
    units = wg.shape[1]
    line = Line(piece)
    red_a = Reduce(line, part_a, held, total, red_send_a, red_recv_a)
    red_b = Reduce(line, part_b, held, total, red_send_b, red_recv_b)
    gat_a = Gather(line, own_a, branch, gat_send_a, gat_recv_a, gat_stay_a)
    gat_b = Gather(line, own_b, mixed, gat_send_b, gat_recv_b, gat_stay_b)
    order = list(reversed(range(chunks)))

    def load(c, slot):
        rows = slice(c * chunk, (c + 1) * chunk)
        return (
            pltpu.make_async_copy(hidden2.at[rows], hid.at[slot], in_sem.at[slot, 0]),
            pltpu.make_async_copy(upstream.at[rows], dy.at[slot], in_sem.at[slot, 1]),
        )

    def near_copy(c):
        return pltpu.make_async_copy(upstream.at[gat_a.mine(c)], near.at[c], near_sem.at[c])

    weights = [
        pltpu.make_async_copy(src, dst, w_sem.at[i])
        for i, (src, dst) in enumerate(((gate_weight, wg), (up_weight, wu), (down_weight, wd)))
    ]
    for copy in load(order[0], 0):
        copy.start()
    for copy in weights:
        copy.start()
    for c in range(chunks):
        near_copy(c).start()
    line.greet(dps)
    grad_gain[...] = jnp.zeros_like(grad_gain)

    def saves(c, slot):
        rows = slice(c * chunk, (c + 1) * chunk)
        return [
            pltpu.make_async_copy(src.at[slot], dst.at[rows], out_sem.at[slot, i])
            for i, (src, dst) in enumerate(((act_c, active), (gate_c, grad_gate), (up_c, grad_up)))
        ]

    def feed(i):
        c, slot = order[i], i % 2
        for copy in load(c, slot):
            copy.wait()
        if i == 0:
            for copy in weights:
                copy.wait()
        if i + 1 < chunks:
            for copy in load(order[i + 1], 1 - slot):
                copy.start()
        if i >= 2:
            for copy in saves(order[i - 2], slot):
                copy.wait()
        step = 512
        for n in range(0, units, step):
            cols = slice(n, min(n + step, units))
            gate = nn(hid[slot], wg[:, cols])
            up = nn(hid[slot], wu[:, cols])
            grad = nt(dy[slot], wd[cols, :])
            sig = 1.0 / (1.0 + jnp.exp(-gate))
            silu = gate * sig
            act_c[slot, :, cols] = (silu * up).astype(BF)
            gate_c[slot, :, cols] = (grad * up * sig * (1.0 + gate * (1.0 - sig))).astype(BF)
            up_c[slot, :, cols] = (grad * silu).astype(BF)
        for copy in saves(c, slot):
            copy.start()
        for n in range(0, width, step):
            cols = slice(n, n + step)
            part_a[c, :, cols] = (
                nt(gate_c[slot], wg[cols, :]) + nt(up_c[slot], wu[cols, :])
            ).astype(BF)
        red_a.start(c)
        for n in range(0, width, step):
            cols = slice(n, n + step)
            part_b[c, :, cols] = nn(act_c[slot], wd[:, cols]).astype(BF)

    spreads = [
        Spread(line, gate_stage, gate_out, gate_taken, gate_sums, gate_moved, dp_sems[:5]),
        Spread(line, up_stage, up_out, up_taken, up_sums, up_moved, dp_sems[5:10]),
        Spread(line, down_stage, down_out, down_taken, down_sums, down_moved, dp_sems[10:]),
    ]
    pair = 2 * width // dps
    groups = dps // 2
    turns = [
        pltpu.make_async_copy(src, dst, turn_sem.at[i])
        for i, (src, dst) in enumerate(
            (
                (grad_gate, wg.at[:length]),
                (grad_up, wg.at[length : 2 * length]),
                (active, wu.at[:length]),
            )
        )
    ]

    def pair_load(j, slot):
        cols = pl.ds(pl.multiple_of(line.group(j) * pair, pair), pair)
        at = 2 * slot * pair
        return (
            pltpu.make_async_copy(
                hidden2.at[:, cols], wd.at[:length, at : at + pair], pair_sem.at[slot, 0]
            ),
            pltpu.make_async_copy(
                upstream.at[:, cols],
                wd.at[:length, at + pair : at + 2 * pair],
                pair_sem.at[slot, 1],
            ),
        )

    units_order = list(range(1, groups)) + [0]

    def turn():
        for i in range(max(0, chunks - 2), chunks):
            for copy in saves(order[i], i % 2):
                copy.wait()
        for copy in turns:
            copy.start()
        for copy in pair_load(units_order[0], 0):
            copy.start()

    def unit(n):
        j, slot = units_order[n], n % 2
        for copy in pair_load(j, slot):
            copy.wait()
        if n == 0:
            for copy in turns:
                copy.wait()
        if n + 1 < groups:
            for copy in pair_load(units_order[n + 1], 1 - slot):
                copy.start()
        at = 2 * slot * pair
        hid_pair = wd[:length, at : at + pair]
        halves(gate_stage, tn(hid_pair, wg[:length, :]), 0)
        spreads[0].give(j).start()
        halves(up_stage, tn(hid_pair, wg[length : 2 * length, :]), 0)
        spreads[1].give(j).start()
        halves(down_stage, tn(wu[:length, :], wd[:length, at + pair : at + 2 * pair]), 1)
        spreads[2].give(j).start()

    work = []
    for n in range(groups):
        work.append(functools.partial(unit, n))
        work.append(functools.partial(merged, spreads, units_order[n]))

    def background(count=1):
        for _ in range(count):
            if work:
                work.pop(0)()

    def done_a(c):
        near_copy(c).wait()
        grad = total[...]
        vector = resid[c]
        scale = lax.rsqrt(jnp.mean(vector * vector, axis=-1, keepdims=True) + EPS)
        scaled = grad * gain[...]
        inner = jnp.mean(scaled * vector, axis=-1, keepdims=True)
        grad_gain[...] += jnp.sum(grad * vector * scale, axis=0, keepdims=True)
        back = near[c].astype(F32) + scale * scaled - vector * (scale * scale * scale) * inner
        grad_resid[c] = back
        own_a[c] = back.astype(BF)

    def done_b(c):
        own_b[c] = (resid[c] + total[...]).astype(BF)

    slots = [(red_a, gat_a, done_a, c) for c in order] + [(red_b, gat_b, done_b, c) for c in order]
    for i in range(len(slots) + 2):
        if i < chunks:
            feed(i)
        elif i < len(slots):
            red_b.start(slots[i][3])
        if i == chunks - 1:
            turn()
        if i >= chunks:
            background()
        last = slots[i - 1] if 0 <= i - 1 < len(slots) else None
        older = slots[i - 2] if i - 2 >= 0 else None
        if last is not None:
            last[0].pass_in(last[3], 3)
        if older is not None:
            older[1].pass_near(older[3])
        if i >= chunks:
            background()
        if last is not None:
            last[0].pass_in(last[3], 2)
        if older is not None:
            older[1].pass_far(older[3])
        if i >= chunks:
            background()
        if last is not None:
            red, gat, done, c = last
            red.pass_out(c)
            red.finish(c)
            done(c)
            gat.start(c)
    background(len(work))
    finished(spreads)
    for red, gat, done, c in slots:
        red.close(c)
        gat.close(c)


def back_kernel(
    chunks,
    dps,
    branch,
    tokens,
    grad_resid,
    gain,
    seg_row,
    seg_key,
    cosine,
    sine,
    query_t,
    query,
    keys,
    keys_t,
    values,
    logs,
    out_weight,
    query_weight,
    kv_weight,
    heads_out,
    hidden1,
    tokens_grad,
    grad_gain,
    out_out,
    qkv_out,
    out_taken,
    out_sums,
    out_moved,
    qkv_taken,
    qkv_sums,
    qkv_moved,
    grad_qkv,
    out_stage,
    qkv_stage,
    pair_out,
    pair_qkv,
    bias,
    dy,
    do_t,
    do_h,
    dq_t,
    dk,
    dv,
    part,
    held,
    total,
    own,
    near,
    in_sem,
    tok_sem,
    red_send,
    red_recv,
    gat_send,
    gat_recv,
    gat_stay,
    pair_sem,
    *dp_sems,
):
    length, width = tokens.shape
    chunk = length // chunks
    piece = chunk // 4
    heads = query.shape[0]
    half = HD // 2
    factor = HD ** (-0.5)
    line = Line(piece)
    red = Reduce(line, part, held, total, red_send, red_recv)
    gat = Gather(line, own, tokens_grad, gat_send, gat_recv, gat_stay)
    order = list(reversed(range(chunks)))

    def load(c, slot):
        return pltpu.make_async_copy(
            branch.at[c * chunk : (c + 1) * chunk], dy.at[slot], in_sem.at[slot]
        )

    def near_copy(c):
        return pltpu.make_async_copy(tokens.at[gat.mine(c)], near.at[c], tok_sem.at[c])

    load(order[0], 0).start()
    for c in range(chunks):
        near_copy(c).start()
    line.greet(dps)
    grad_gain[...] = jnp.zeros_like(grad_gain)
    dk[...] = jnp.zeros_like(dk)
    dv[...] = jnp.zeros_like(dv)

    def unrope(t, cols):
        first, second = t[:half], t[half:]
        cos, sin = cosine[:, cols], sine[:, cols]
        return jnp.concatenate([first * cos + second * sin, second * cos - first * sin], axis=0)

    def attend(i):
        c, slot = order[i], i % 2
        load(c, slot).wait()
        if i + 1 < chunks:
            load(order[i + 1], 1 - slot).start()
        keys_n = (c + 1) * chunk
        cols = slice(c * chunk, keys_n)
        bias[:keys_n, :] = visible_bias(seg_row[...], seg_key[...], c, chunk)
        grad_heads = nt(dy[slot], out_weight[...])
        do_t[...] = grad_heads.T.astype(BF)
        for h in range(heads):
            do_h[h] = grad_heads[:, h * HD : (h + 1) * HD].astype(BF)

        def head(h, carry):
            here = pl.ds(pl.multiple_of(h * HD, HD), HD)
            scores = nn(keys[:keys_n, :], query_t[here, cols]) + bias[:keys_n, :]
            probs = jnp.exp(scores - logs[h, :, cols])
            grad_probs = nn(values[:keys_n, :], do_t[here, :])
            delta = jnp.sum(probs * grad_probs, axis=0, keepdims=True)
            grad_scores = (probs * (grad_probs - delta)).astype(BF)
            dv[:keys_n, :] += nn(probs.astype(BF), do_h[h])
            dk[:keys_n, :] += nn(grad_scores, query[h, cols, :])
            grad = nn(keys_t[:, :keys_n], grad_scores) * factor
            dq_t[here, :] = unrope(grad, cols)
            return carry

        lax.fori_loop(0, heads, head, 0)
        grad_q = dq_t[...].T.astype(BF)
        grad_qkv[cols, : heads * HD] = grad_q
        grad_k = unrope(dk[cols, :].T, cols).T
        both = jnp.concatenate([grad_k, dv[cols, :]], axis=1).astype(BF)
        grad_qkv[cols, heads * HD :] = both
        step = min(512, width)
        for n in range(0, width, step):
            here = slice(n, n + step)
            part[c, :, here] = (
                nt(grad_q, query_weight[here, :]) + nt(both, kv_weight[here, :])
            ).astype(BF)

    spread_out = Spread(line, out_stage, out_out, out_taken, out_sums, out_moved, dp_sems[:5])
    spread_qkv = Spread(line, qkv_stage, qkv_out, qkv_taken, qkv_sums, qkv_moved, dp_sems[5:])
    pair = 2 * width // dps
    groups = dps // 2
    units_order = list(range(1, groups)) + [0]

    def pair_load(j, slot, src, dst, number):
        cols = pl.ds(pl.multiple_of(line.group(j) * pair, pair), pair)
        return pltpu.make_async_copy(src.at[:, cols], dst.at[slot], pair_sem.at[slot, number])

    def unit_out(n):
        j, slot = units_order[n], n % 2
        pair_load(j, slot, branch, pair_out, 0).wait()
        if n + 1 < groups:
            pair_load(units_order[n + 1], 1 - slot, branch, pair_out, 0).start()
        halves(out_stage, tn(heads_out[...], pair_out[slot]), 1)
        spread_out.give(j).start()

    def unit_qkv(n):
        j, slot = units_order[n], n % 2
        pair_load(j, slot, hidden1, pair_qkv, 1).wait()
        if n + 1 < groups:
            pair_load(units_order[n + 1], 1 - slot, hidden1, pair_qkv, 1).start()
        halves(qkv_stage, tn(pair_qkv[slot], grad_qkv[...]), 0)
        spread_qkv.give(j).start()

    pair_load(units_order[0], 0, branch, pair_out, 0).start()
    pair_load(units_order[0], 0, hidden1, pair_qkv, 1).start()
    work_out, work_qkv = [], []
    for n in range(groups):
        work_out.append(functools.partial(unit_out, n))
        work_out.append(functools.partial(merged, [spread_out], units_order[n]))
        work_qkv.append(functools.partial(unit_qkv, n))
        work_qkv.append(functools.partial(merged, [spread_qkv], units_order[n]))

    def background(i, count=1):
        for _ in range(count):
            if work_out:
                work_out.pop(0)()
            elif work_qkv and i >= chunks:
                work_qkv.pop(0)()

    def done(c):
        near_copy(c).wait()
        grad = total[...]
        vector = near[c].astype(F32)
        scale = lax.rsqrt(jnp.mean(vector * vector, axis=-1, keepdims=True) + EPS)
        scaled = grad * gain[...]
        inner = jnp.mean(scaled * vector, axis=-1, keepdims=True)
        grad_gain[...] += jnp.sum(grad * vector * scale, axis=0, keepdims=True)
        back = grad_resid[c] + scale * scaled - vector * (scale * scale * scale) * inner
        own[c] = back.astype(BF)

    for i in range(chunks + 2):
        now = order[i] if i < chunks else None
        last = order[i - 1] if 0 <= i - 1 < chunks else None
        older = order[i - 2] if i - 2 >= 0 else None
        if now is not None:
            attend(i)
            red.start(now)
        if last is not None:
            red.pass_in(last, 3)
        if i > 0:
            background(i)
        if older is not None:
            gat.pass_near(older)
        if last is not None:
            red.pass_in(last, 2)
        if i > 0:
            background(i)
        if older is not None:
            gat.pass_far(older)
        if last is not None:
            red.pass_out(last)
            red.finish(last)
            done(last)
            gat.start(last)
        if i > 0:
            background(i, 2)
    background(chunks, len(work_out) + len(work_qkv))
    finished([spread_out, spread_qkv])
    for c in order:
        red.close(c)
        gat.close(c)


def call(kernel, ins, outs, scratch, number, cost):
    return pl.pallas_call(
        kernel,
        in_specs=[spec for spec, _ in ins],
        out_specs=[spec for spec, _, _ in outs],
        out_shape=[jax.ShapeDtypeStruct(shape, kind) for _, shape, kind in outs],
        scratch_shapes=scratch,
        compiler_params=pltpu.CompilerParams(
            collective_id=number, has_side_effects=True, vmem_limit_bytes=LIMIT
        ),
        cost_estimate=pl.CostEstimate(flops=cost, bytes_accessed=cost // 1000, transcendentals=0),
    )(*[array for _, array in ins])


def line_scratch(chunks, piece, width):
    dma = pltpu.SemaphoreType.DMA
    buffers = [
        pltpu.VMEM((chunks, 4 * piece, width), BF),
        pltpu.VMEM((chunks, 5, piece, width), BF),
        pltpu.VMEM((chunks, piece, width), BF),
    ]
    sems = [dma((chunks, 3)), dma((chunks, 5)), dma((chunks, 5)), dma((chunks, 4)), dma((chunks,))]
    return buffers, sems


def spread_shapes(groups, rows, cols):
    dma = pltpu.SemaphoreType.DMA
    outs = [(VMEM, (rows, cols), F32)]
    boxes = [(ANY, (groups, rows, cols), BF)] * 3
    stage = pltpu.VMEM((2, rows, cols), BF)
    return outs, boxes, stage, [dma((groups,))] * 4 + [dma((2,))]


def tables(seg_row):
    length = seg_row.shape[0]
    start = jnp.sum((seg_row[None, :] < seg_row[:, None]).astype(jnp.int32), axis=1)
    place = (jnp.arange(length, dtype=jnp.int32) - start).astype(F32)
    half = HD // 2
    freq = jnp.power(jnp.float32(THETA), -jnp.arange(half, dtype=F32) / half)
    angle = freq[:, None] * place[None, :]
    return jnp.cos(angle), jnp.sin(angle)


def rope_t(raw, cosine, sine):
    heads = raw.shape[0] // HD
    raw = raw.reshape(heads, HD, -1)
    first, second = raw[:, : HD // 2], raw[:, HD // 2 :]
    return jnp.concatenate(
        [first * cosine - second * sine, second * cosine + first * sine], axis=1
    )


def local(
    dps,
    tokens,
    segments,
    counts,
    cotangent,
    attn_gain,
    mlp_gain,
    query_weight,
    key_weight,
    value_weight,
    out_weight,
    gate_weight,
    up_weight,
    down_weight,
):
    length, width = tokens.shape
    units = gate_weight.shape[1]
    lanes = query_weight.shape[1]
    heads = lanes // HD
    chunks = CHUNKS
    chunk = length // chunks
    piece = chunk // 4
    dma = pltpu.SemaphoreType.DMA
    groups = dps // 2
    block = width // dps

    live = jnp.arange(length, dtype=jnp.int32) < counts[0]
    seg_row = segments.reshape(1, length)
    seg_key = jnp.where(live, segments, -1).reshape(length, 1)
    cosine, sine = tables(segments)
    xfull = tokens.astype(F32)
    scale1 = lax.rsqrt(jnp.mean(xfull * xfull, axis=-1, keepdims=True) + EPS)
    hidden1 = (xfull * scale1 * attn_gain).astype(BF)
    dims = (((0,), (1,)), ((), ()))
    query_raw = lax.dot_general(query_weight, hidden1, dims, preferred_element_type=F32)
    key_raw = lax.dot_general(key_weight, hidden1, dims, preferred_element_type=F32)
    values = jnp.dot(hidden1, value_weight, preferred_element_type=F32).astype(BF)
    query_h = rope_t(query_raw, cosine, sine).astype(BF) * BF(HD ** (-0.5))
    keys_t = rope_t(key_raw, cosine, sine).astype(BF)[0]
    query_t = query_h.reshape(lanes, length)
    query = query_h.transpose(0, 2, 1)
    keys = keys_t.T
    values_t = values.T
    gain1 = attn_gain.reshape(1, width)
    gain2 = mlp_gain.reshape(1, width)
    upstream = jnp.where(live[:, None], cotangent, BF(0))

    buffers, sems = line_scratch(chunks, piece, width)
    total = pltpu.VMEM((piece, width), F32)
    near = pltpu.VMEM((chunks, piece, width), BF)
    hidden2, resid, heads_out, logs = call(
        functools.partial(attn_kernel, chunks),
        [
            (ANY, tokens),
            (VMEM, gain2),
            (VMEM, seg_row),
            (VMEM, seg_key),
            (VMEM, query_t),
            (VMEM, keys),
            (VMEM, values_t),
            (VMEM, out_weight),
        ],
        [
            (ANY, (length, width), BF),
            (VMEM, (chunks, piece, width), F32),
            (VMEM, (length, lanes), BF),
            (VMEM, (heads, 1, length), F32),
        ],
        [
            pltpu.VMEM((length, chunk), F32),
            pltpu.VMEM((lanes, chunk), F32),
            buffers[0],
            buffers[1],
            total,
            buffers[2],
            near,
            dma((chunks,)),
            *sems,
        ],
        0,
        10**10,
    )

    by_rows = spread_shapes(groups, block, units)
    by_cols = spread_shapes(groups, units, block)
    mixed, branch, grad_resid, grad_gain2, gate_grad, up_grad, down_grad, *_ = call(
        functools.partial(mlp_kernel, chunks, dps),
        [
            (ANY, hidden2),
            (VMEM, resid),
            (ANY, upstream),
            (VMEM, gain2),
            (ANY, gate_weight),
            (ANY, up_weight),
            (ANY, down_weight),
        ],
        [
            (ANY, (length, width), BF),
            (ANY, (length, width), BF),
            (VMEM, (chunks, piece, width), F32),
            (VMEM, (1, width), F32),
            *by_rows[0],
            *by_rows[0],
            *by_cols[0],
            *[(ANY, (length, units), BF)] * 3,
            *by_rows[1],
            *by_rows[1],
            *by_cols[1],
        ],
        [
            pltpu.VMEM((width, units), BF),
            pltpu.VMEM((width, units), BF),
            pltpu.VMEM((units, width), BF),
            pltpu.VMEM((2, chunk, width), BF),
            pltpu.VMEM((2, chunk, width), BF),
            pltpu.VMEM((2, chunk, units), BF),
            pltpu.VMEM((2, chunk, units), BF),
            pltpu.VMEM((2, chunk, units), BF),
            buffers[0],
            buffers[0],
            buffers[1],
            by_rows[2],
            by_rows[2],
            by_cols[2],
            total,
            buffers[2],
            buffers[2],
            near,
            dma((3,)),
            dma((2, 2)),
            dma((2, 3)),
            dma((chunks,)),
            sems[0],
            sems[1],
            sems[0],
            sems[1],
            *sems[2:],
            *sems[2:],
            dma((3,)),
            dma((2, 2)),
            *by_rows[3],
            *by_rows[3],
            *by_cols[3],
        ],
        1,
        4 * 10**10,
    )

    by_cols = spread_shapes(groups, lanes, block)
    by_rows = spread_shapes(groups, block, lanes + 2 * HD)
    tokens_grad, grad_gain1, out_grad, qkv_grad, *_ = call(
        functools.partial(back_kernel, chunks, dps),
        [
            (ANY, branch),
            (ANY, tokens),
            (VMEM, grad_resid),
            (VMEM, gain1),
            (VMEM, seg_row),
            (VMEM, seg_key),
            (VMEM, cosine),
            (VMEM, sine),
            (VMEM, query_t),
            (VMEM, query),
            (VMEM, keys),
            (VMEM, keys_t),
            (VMEM, values),
            (VMEM, logs),
            (VMEM, out_weight),
            (VMEM, query_weight),
            (VMEM, jnp.concatenate([key_weight, value_weight], axis=1)),
            (VMEM, heads_out),
            (ANY, hidden1),
        ],
        [
            (ANY, (length, width), BF),
            (VMEM, (1, width), F32),
            *by_cols[0],
            *by_rows[0],
            *by_cols[1],
            *by_rows[1],
        ],
        [
            pltpu.VMEM((length, lanes + 2 * HD), BF),
            by_cols[2],
            by_rows[2],
            pltpu.VMEM((2, length, 2 * block), BF),
            pltpu.VMEM((2, length, 2 * block), BF),
            pltpu.VMEM((length, chunk), F32),
            pltpu.VMEM((2, chunk, width), BF),
            pltpu.VMEM((lanes, chunk), BF),
            pltpu.VMEM((heads, chunk, HD), BF),
            pltpu.VMEM((lanes, chunk), F32),
            pltpu.VMEM((length, HD), F32),
            pltpu.VMEM((length, HD), F32),
            buffers[0],
            buffers[1],
            total,
            buffers[2],
            near,
            dma((2,)),
            dma((chunks,)),
            *sems,
            dma((2, 2)),
            *by_cols[3],
            *by_rows[3],
        ],
        2,
        2 * 10**10,
    )

    gains = lax.psum(jnp.concatenate([grad_gain1, grad_gain2], axis=0), "tensor")
    gains = lax.psum_scatter(gains, "dp", scatter_dimension=1, tiled=True)

    return (
        mixed,
        tokens_grad,
        gains[0],
        gains[1],
        qkv_grad[:, :lanes],
        qkv_grad[:, lanes : lanes + HD],
        qkv_grad[:, lanes + HD :],
        out_grad,
        gate_grad,
        up_grad,
        down_grad,
    )


def solution(mesh):
    placed = (
        P("dp", None),
        P("dp"),
        P("dp"),
        P("dp", None),
        P(),
        P(),
        P(None, "tensor"),
        P(None, "tensor"),
        P(None, "tensor"),
        P("tensor", None),
        P(None, "tensor"),
        P(None, "tensor"),
        P("tensor", None),
    )
    return jax.shard_map(
        functools.partial(local, mesh.shape["dp"]),
        mesh=mesh,
        in_specs=placed,
        out_specs=(
            P("dp", None),
            P("dp", None),
            P("dp"),
            P("dp"),
            P("dp", "tensor"),
            P("dp", "tensor"),
            P("dp", "tensor"),
            P("tensor", "dp"),
            P("dp", "tensor"),
            P("dp", "tensor"),
            P("tensor", "dp"),
        ),
        check_vma=False,
    )
```

```python
import functools

import jax
import jax.numpy as jnp
from jax import lax
from jax.experimental import pallas as pl
from jax.experimental.pallas import tpu as pltpu
from jax.sharding import PartitionSpec as P

HD = 64
EPS = 1e-05
THETA = 10000.0
NEGATIVE = -1e30
CHUNKS = 8
BIG = 4
DEPTH = 4
MESH = pl.DeviceIdType.MESH
BF = jnp.bfloat16
F32 = jnp.float32
ANY = pl.BlockSpec(memory_space=pl.ANY)
VMEM = pl.BlockSpec(memory_space=pltpu.VMEM)
LIMIT = 60 * 1024 * 1024


def nn(a, b):
    return lax.dot_general(a, b, (((1,), (0,)), ((), ())), preferred_element_type=F32)


def nt(a, b):
    return lax.dot_general(a, b, (((1,), (1,)), ((), ())), preferred_element_type=F32)


def tn(a, b):
    return lax.dot_general(a, b, (((0,), (0,)), ((), ())), preferred_element_type=F32)


class Line:
    def __init__(self, piece):
        self.z = lax.axis_index("tensor")
        self.dp = lax.axis_index("dp")
        self.low = self.z < 2
        self.inner = jnp.where(self.low, self.z + 1, self.z - 1)
        self.outer = jnp.where(self.low, self.z - 1, self.z + 1)
        self.end = (self.z == 0) | (self.z == 3)
        self.mid = (self.z == 1) | (self.z == 2)
        self.piece = piece

    def at(self, m):
        place = jnp.where(self.low, m, 3 - m) * self.piece
        return pl.ds(pl.multiple_of(place, self.piece), self.piece)

    def own(self):
        return pl.ds(pl.multiple_of(self.z * self.piece, self.piece), self.piece)

    def copy(self, src, dst, send, recv, target):
        return pltpu.make_async_remote_copy(
            src_ref=src,
            dst_ref=dst,
            send_sem=send,
            recv_sem=recv,
            device_id=(self.dp, target),
            device_id_type=MESH,
        )

    def greet(self, dps, every=False):
        barrier = pltpu.get_barrier_semaphore()
        self.dps = dps
        self.groups = dps // 2
        self.core = lax.rem(self.dp, 2)
        self.partner = self.dp + 1 - 2 * self.core

        def signal(dp, z):
            pl.semaphore_signal(barrier, inc=1, device_id=(dp, z), device_id_type=MESH)

        if every:
            for j in range(1, dps):
                signal(self.dp_peer(j), self.z)
            for j in range(1, 4):
                signal(self.dp, self.z_peer(j))
            pl.semaphore_wait(barrier, dps - 1 + 3)
            return
        others = [] if dps == 2 else [self.partner] + [self.peer(j) for j in range(1, self.groups)]
        for other in others:
            signal(other, self.z)
        signal(self.dp, self.inner)

        @pl.when(self.mid)
        def _():
            signal(self.dp, self.outer)
            pl.semaphore_wait(barrier, 2 + len(others))

        @pl.when(self.end)
        def _():
            pl.semaphore_wait(barrier, 1 + len(others))

    def dp_peer(self, j):
        return lax.rem(self.dp + j, self.dps)

    def z_peer(self, j):
        return lax.rem(self.z + j, 4)

    def group(self, j):
        return lax.rem(self.dp // 2 + j, self.groups)

    def peer(self, j):
        return 2 * self.group(j) + self.core


class Reduce:
    def __init__(self, line, part, held, total, send, recv):
        self.line, self.part, self.held, self.total = line, part, held, total
        self.send, self.recv = send, recv

    def copy(self, c, m, slot, target, number):
        line = self.line
        return line.copy(
            self.part.at[c, line.at(m)],
            self.held.at[c % DEPTH, slot],
            self.send.at[c, number],
            self.recv.at[c, slot],
            target,
        )

    def arrived(self, c, slot):
        self.copy(c, 0, slot, self.line.inner, 0).wait_recv()

    def start(self, c):
        @pl.when(self.line.end)
        def _():
            for m in (3, 2, 1):
                self.copy(c, m, m - 1, self.line.inner, m - 1).start()

    def pass_in(self, c, m):
        line = self.line

        @pl.when(line.mid)
        def _():
            self.arrived(c, m - 1)
            rows = line.at(m)
            self.part[c, rows] = (
                self.part[c, rows].astype(F32) + self.held[c % DEPTH, m - 1].astype(F32)
            ).astype(BF)
            self.copy(c, m, 6 - m, line.inner, 3 - m).start()

    def pass_out(self, c):
        line = self.line

        @pl.when(line.mid)
        def _():
            self.arrived(c, 3)
            rows = line.at(0)
            self.part[c, rows] = (
                self.part[c, rows].astype(F32) + self.held[c % DEPTH, 3].astype(F32)
            ).astype(BF)
            self.copy(c, 0, 3, line.outer, 2).start()

    def finish(self, c):
        line = self.line

        @pl.when(line.end)
        def _():
            self.arrived(c, 3)
            self.total[...] = self.part[c, line.at(0)].astype(F32) + self.held[c % DEPTH, 3].astype(F32)

        @pl.when(line.mid)
        def _():
            self.arrived(c, 0)
            self.arrived(c, 4)
            self.total[...] = (
                self.part[c, line.at(1)].astype(F32)
                + self.held[c % DEPTH, 0].astype(F32)
                + self.held[c % DEPTH, 4].astype(F32)
            )

    def close(self, c):
        for number in range(3):
            self.copy(c, 0, 0, self.line.inner, number).wait_send()


class Spread:
    def __init__(self, line, stage, out, taken, sums, moved, sems):
        self.line, self.stage, self.out = line, stage, out
        self.taken, self.sums, self.moved = taken, sums, moved
        self.send1, self.recv1, self.send2, self.recv2, self.stay = sems

    def give(self, j):
        line = self.line
        return pltpu.make_async_remote_copy(
            src_ref=self.stage.at[1 - line.core],
            dst_ref=self.taken.at[j],
            send_sem=self.send1.at[j],
            recv_sem=self.recv1.at[j],
            device_id=(line.partner, line.z),
            device_id_type=MESH,
        )

    def move(self, j):
        line = self.line
        return pltpu.make_async_remote_copy(
            src_ref=self.sums.at[j],
            dst_ref=self.moved.at[j],
            send_sem=self.send2.at[j],
            recv_sem=self.recv2.at[j],
            device_id=(line.peer(j), line.z),
            device_id_type=MESH,
        )

    def merge_load(self, j):
        self.give(j).wait()
        self.load(self.taken.at[j], 1 - self.line.core).start()

    def load(self, src, slot):
        return pltpu.make_async_copy(src, self.stage.at[slot], self.stay.at[slot])

    def merge_add(self, j):
        core = self.line.core
        self.load(self.taken.at[j], 1 - core).wait()
        self.stage[core] = (
            self.stage[core].astype(F32) + self.stage[1 - core].astype(F32)
        ).astype(BF)
        pltpu.make_async_copy(self.stage.at[core], self.sums.at[j], self.stay.at[core]).start()

    def merge_move(self, j):
        core = self.line.core
        pltpu.make_async_copy(self.stage.at[core], self.sums.at[j], self.stay.at[core]).wait()
        if j:
            self.move(j).start()

    def sources(self):
        return [self.sums.at[0]] + [self.moved.at[j] for j in range(1, self.line.groups)]

    def last_load(self):
        self.load(self.sources()[0], 0).start()

    def last(self):
        sources = self.sources()
        for j, source in enumerate(sources):
            if j + 1 < len(sources):
                self.move(j + 1).wait()
                self.load(sources[j + 1], (j + 1) % 2).start()
            self.load(source, j % 2).wait()
            block = self.stage[j % 2].astype(F32)
            if j:
                self.out[...] += block
            else:
                self.out[...] = block


def merged(spreads, j):
    def run(name):
        for spread in spreads:
            getattr(spread, name)(j)

    return [functools.partial(run, name) for name in ("merge_load", "merge_add", "merge_move")]


def finished(spreads):
    for spread in spreads:
        spread.last_load()
    for spread in spreads:
        spread.last()


def halves(stage, value, dim):
    size = value.shape[dim] // 2
    if dim == 0:
        stage[0] = value[:size].astype(BF)
        stage[1] = value[size:].astype(BF)
    else:
        stage[0] = value[:, :size].astype(BF)
        stage[1] = value[:, size:].astype(BF)


class Gather:
    def __init__(self, line, own, full, send, recv, stay):
        self.line, self.own, self.full = line, own, full
        self.send, self.recv, self.stay = send, recv, stay
        self.chunk = 4 * line.piece

    def rows(self, c, m):
        line = self.line
        place = c * self.chunk + jnp.where(line.low, m, 3 - m) * line.piece
        return pl.ds(pl.multiple_of(place, line.piece), line.piece)

    def mine(self, c):
        line = self.line
        place = c * self.chunk + line.z * line.piece
        return pl.ds(pl.multiple_of(place, line.piece), line.piece)

    def first(self, c, slot, target, number):
        return self.line.copy(
            self.own.at[c],
            self.full.at[self.mine(c)],
            self.send.at[c, number],
            self.recv.at[c, slot],
            target,
        )

    def onward(self, c, m, slot, target, number):
        rows = self.rows(c, m)
        return self.line.copy(
            self.full.at[rows],
            self.full.at[rows],
            self.send.at[c, number],
            self.recv.at[c, slot],
            target,
        )

    def arrived(self, c, m):
        self.onward(c, m, m, self.line.inner, 0).wait_recv()

    def stays(self, c):
        return pltpu.make_async_copy(
            self.own.at[c], self.full.at[self.mine(c)], self.stay.at[c]
        )

    def start(self, c):
        line = self.line
        self.stays(c).start()

        @pl.when(line.end)
        def _():
            self.first(c, 0, line.inner, 0).start()

        @pl.when(line.mid)
        def _():
            self.first(c, 1, line.outer, 0).start()
            self.first(c, 2, line.inner, 1).start()

    def pass_near(self, c):
        line = self.line

        @pl.when(line.end)
        def _():
            self.arrived(c, 1)

        @pl.when(line.mid)
        def _():
            self.arrived(c, 0)
            self.onward(c, 0, 3, line.inner, 2).start()
            self.arrived(c, 2)
            self.onward(c, 2, 2, line.outer, 3).start()

    def pass_far(self, c):
        line = self.line

        @pl.when(line.mid)
        def _():
            self.arrived(c, 3)
            self.onward(c, 3, 3, line.outer, 4).start()

    def complete(self, c):
        self.stays(c).wait()

        @pl.when(self.line.end)
        def _():
            for m in (2, 3):
                self.arrived(c, m)

    def close(self, c):
        line = self.line

        @pl.when(line.end)
        def _():
            self.first(c, 0, line.inner, 0).wait_send()

        @pl.when(line.mid)
        def _():
            for number in range(5):
                self.first(c, 0, line.inner, number).wait_send()


def drive(slots, begin, plan):
    n = len(slots)
    for i in range(n + 4):
        begin(i)
        work = list(plan.get(i, ()))
        count = len(work)
        for point in range(6):
            if point == 0 and 0 <= i - 4 < n:
                _, gat, _, c = slots[i - 4]
                gat.pass_far(c)
            if point == 1 and 0 <= i - 3 < n:
                _, gat, _, c = slots[i - 3]
                gat.pass_near(c)
            if point == 2 and 0 <= i - 2 < n:
                red, gat, done, c = slots[i - 2]
                red.finish(c)
                done(c)
                gat.start(c)
            if point == 3 and 0 <= i - 1 < n:
                red, _, _, c = slots[i - 1]
                red.pass_out(c)
            if point == 4 and i < n:
                red, _, _, c = slots[i]
                red.pass_in(c, 3)
            if point == 5 and i < n:
                red, _, _, c = slots[i]
                red.pass_in(c, 2)
            while work and count - len(work) < (point + 1) * count // 6:
                work.pop(0)()
        for task in work:
            task()


def schedule(plan, tasks, first, per_step):
    for k, task in enumerate(tasks):
        plan.setdefault(first + k // per_step, []).append(task)


def put(part, big, cols, value):
    chunk = part.shape[1]
    sub = value.shape[0] // chunk
    for k in range(sub):
        part[big * sub + k, :, cols] = value[k * chunk : (k + 1) * chunk].astype(BF)


def rope(t, cos, sin):
    half = HD // 2
    first, second = t[:half], t[half:]
    return jnp.concatenate([first * cos - second * sin, second * cos + first * sin], axis=0)


def unrope(t, cos, sin):
    half = HD // 2
    first, second = t[:half], t[half:]
    return jnp.concatenate([first * cos + second * sin, second * cos - first * sin], axis=0)


def normed(vector):
    return lax.rsqrt(jnp.mean(vector * vector, axis=-1, keepdims=True) + EPS)


def visible_bias(seg_row, key_row, c, chunk):
    keys = (c + 1) * chunk
    seg_q = seg_row[:, c * chunk : keys]
    seg_k = key_row[:keys, :]
    shape = (keys, chunk)
    key_at = lax.broadcasted_iota(jnp.int32, shape, 0)
    query_at = lax.broadcasted_iota(jnp.int32, shape, 1) + c * chunk
    seen = ((seg_k == seg_q) & (key_at < query_at)) | (key_at == query_at)
    return jnp.where(seen, 0.0, NEGATIVE)


def front_kernel(
    chunks,
    big,
    dps,
    tokens,
    cotangent,
    live,
    gain1,
    gain2,
    seg_row,
    seg_key,
    cosine,
    sine,
    query_weight,
    kv_weight,
    out_weight,
    gate_weight,
    up_weight,
    down_weight,
    mixed,
    branch,
    hidden1,
    grad_resid,
    grad_gain,
    heads_out,
    logs,
    query_t,
    keys,
    keys_t,
    values,
    gate_out,
    up_out,
    down_out,
    hidden2,
    active,
    grad_gate,
    grad_up,
    gate_taken,
    gate_sums,
    gate_moved,
    up_taken,
    up_sums,
    up_moved,
    down_taken,
    down_sums,
    down_moved,
    wg,
    wu,
    wd,
    hid,
    dy,
    act_c,
    gate_c,
    up_c,
    gate_stage,
    up_stage,
    down_stage,
    values_t,
    bias,
    heads_t,
    resid,
    part_p,
    part_a,
    held,
    own_p,
    own_a,
    near,
    total,
    w_sem,
    in_sem,
    out_sem,
    save_sem,
    near_sem,
    turn_sem,
    pair_sem,
    *sems,
):
    length, width = tokens.shape
    units = wg.shape[1]
    chunk = length // chunks
    wide = length // big
    sub = chunks // big
    piece = chunk // 4
    lanes = query_t.shape[0]
    heads = lanes // HD
    if gate_stage.shape[1] != width // dps:
        gate_stage, up_stage = gate_c, up_c
    line = Line(piece)
    red_p = Reduce(line, part_p, held, total, *sems[0:2])
    gat_p = Gather(line, own_p, hidden2, *sems[2:5])
    red_a = Reduce(line, part_a, held, total, *sems[5:7])
    gat_a = Gather(line, own_a, branch, *sems[7:10])
    red_b = Reduce(line, part_p, held, total, *sems[10:12])
    gat_b = Gather(line, own_p, mixed, *sems[12:15])
    dp_sems = sems[15:]
    upstream = cotangent
    gain = gain2

    def near_copy(c, src=cotangent):
        return pltpu.make_async_copy(src.at[gat_p.mine(c)], near.at[c], near_sem.at[c])

    def token_load(n):
        rows = slice(n * wide, (n + 1) * wide)
        return pltpu.make_async_copy(tokens.at[rows], hid.at[n % 2], in_sem.at[n % 2, 0])

    def hidden_save(n):
        rows = slice(n * wide, (n + 1) * wide)
        return pltpu.make_async_copy(dy.at[n % 2], hidden1.at[rows], save_sem.at[n % 2])

    def load(n):
        slot = n % 2
        rows = slice(n * wide, (n + 1) * wide)
        return (
            pltpu.make_async_copy(hidden2.at[rows], hid.at[slot], in_sem.at[slot, 0]),
            pltpu.make_async_copy(cotangent.at[rows], dy.at[slot], in_sem.at[slot, 1]),
        )

    weights = [
        pltpu.make_async_copy(src, dst, w_sem.at[i])
        for i, (src, dst) in enumerate(
            (
                (query_weight, wu.at[:, :lanes]),
                (kv_weight, wu.at[:, lanes : lanes + 2 * HD]),
                (out_weight, wd.at[:lanes]),
                (gate_weight, wg),
                (up_weight, wu),
                (down_weight, wd),
            )
        )
    ]
    token_load(0).start()
    for copy in weights[:4]:
        copy.start()
    for c in range(chunks):
        near_copy(c, tokens).start()
    line.greet(dps)
    grad_gain[...] = jnp.zeros_like(grad_gain)

    def project(n):
        rows = slice(n * wide, (n + 1) * wide)
        token_load(n).wait()
        if n + 1 < big:
            token_load(n + 1).start()
        if n >= 2:
            hidden_save(n - 2).wait()
        if n == 0:
            weights[0].wait()
            weights[1].wait()
        vector = hid[n % 2].astype(F32)
        hidden = (vector * normed(vector) * gain1[...]).astype(BF)
        dy[n % 2] = hidden
        hidden_save(n).start()
        cos, sin = cosine[:, rows], sine[:, rows]
        raw = nn(hidden, wu[:, :lanes]).T
        for h in range(heads):
            here = slice(h * HD, (h + 1) * HD)
            turned = rope(raw[here], cos, sin) * (HD ** (-0.5))
            query_t[here, rows] = turned.astype(BF)
        raw = nn(hidden, wu[:, lanes : lanes + 2 * HD]).T
        turned = rope(raw[:HD], cos, sin)
        keys_t[:, rows] = turned.astype(BF)
        keys[rows, :] = turned.T.astype(BF)
        values_t[:, rows] = raw[HD:].astype(BF)
        values[rows, :] = raw[HD:].T.astype(BF)

    def attend(n, begin, end):
        keys_n = (n + 1) * wide
        cols = slice(n * wide, keys_n)
        if begin == 0:
            bias[:keys_n, :] = visible_bias(seg_row[...], seg_key[...], n, wide)

        def head(h, carry):
            here = pl.ds(pl.multiple_of(h * HD, HD), HD)
            scores = nn(keys[:keys_n, :], query_t[here, cols]) + bias[:keys_n, :]
            peak = jnp.max(scores, axis=0, keepdims=True)
            weights = jnp.exp(scores - peak)
            sums = jnp.sum(weights, axis=0, keepdims=True)
            probs = (weights * (1.0 / sums)).astype(BF)
            heads_t[here, :] = nn(values_t[:, :keys_n], probs)
            logs[h, :, cols] = peak + jnp.log(sums)
            return carry

        lax.fori_loop(begin, end, head, 0)

    def close_heads(n):
        if n == 0:
            weights[2].wait()
        heads_n = heads_t[...].T.astype(BF)
        heads_out[n * wide : (n + 1) * wide, :] = heads_n
        step = min(512, width)
        for at in range(0, width, step):
            cols = slice(at, at + step)
            put(part_p, n, cols, nn(heads_n, wd[:lanes, cols]))
        if n == big - 1:
            weights[4].start()
            weights[5].start()

    def attn_tasks(n):
        return [
            functools.partial(project, n),
            functools.partial(attend, n, 0, heads // 2),
            functools.partial(attend, n, heads // 2, heads),
            functools.partial(close_heads, n),
        ]

    def norm(c):
        near_copy(c, tokens).wait()
        vector = near[c].astype(F32) + total[...]
        near_copy(c).start()
        resid[c] = vector
        own_p[c] = (vector * normed(vector) * gain2[...]).astype(BF)

    def saves(n):
        slot = n % 2
        rows = slice(n * wide, (n + 1) * wide)
        return [
            pltpu.make_async_copy(src.at[slot], dst.at[rows], out_sem.at[slot, i])
            for i, (src, dst) in enumerate(((act_c, active), (gate_c, grad_gate), (up_c, grad_up)))
        ]

    def enter(n):
        if n == 0:
            for k in range(max(0, big - 2), big):
                hidden_save(k).wait()
        for c in range(n * sub, (n + 1) * sub):
            gat_p.complete(c)
        for copy in load(n):
            copy.start()
        for c in range(n * sub, (n + 1) * sub):
            red_p.close(c)
            gat_p.close(c)
        for copy in load(n):
            copy.wait()
        if n == 0:
            for copy in weights[3:]:
                copy.wait()
        if n >= 2:
            for copy in saves(n - 2):
                copy.wait()
        slot = n % 2
        dy[slot] = jnp.where(live[n * wide : (n + 1) * wide, :] > 0, dy[slot], BF(0))

    def hidden_units(n, cols):
        slot = n % 2
        gate = nn(hid[slot], wg[:, cols])
        up = nn(hid[slot], wu[:, cols])
        grad = nt(dy[slot], wd[cols, :])
        sig = 1.0 / (1.0 + jnp.exp(-gate))
        silu = gate * sig
        act_c[slot, :, cols] = (silu * up).astype(BF)
        gate_c[slot, :, cols] = (grad * up * sig * (1.0 + gate * (1.0 - sig))).astype(BF)
        up_c[slot, :, cols] = (grad * silu).astype(BF)
        if cols.stop == units:
            for copy in saves(n):
                copy.start()

    def back_part(n, cols):
        slot = n % 2
        put(part_a, n, cols, nt(gate_c[slot], wg[cols, :]) + nt(up_c[slot], wu[cols, :]))

    def down_part(n, cols):
        put(part_p, n, cols, nn(act_c[n % 2], wd[:, cols]))

    def feed_tasks(n):
        step = 512
        unit_cols = [slice(at, min(at + step, units)) for at in range(0, units, step)]
        cols = [slice(at, at + step) for at in range(0, width, step)]

        def first():
            enter(n)
            hidden_units(n, unit_cols[0])

        def several(f, group):
            for here in group:
                f(n, here)

        return [
            first,
            *[functools.partial(hidden_units, n, here) for here in unit_cols[1:]],
            functools.partial(several, back_part, cols[:2]),
            functools.partial(several, back_part, cols[2:]),
            functools.partial(several, down_part, cols),
        ]

    spreads = [
        Spread(line, gate_stage, gate_out, gate_taken, gate_sums, gate_moved, dp_sems[:5]),
        Spread(line, up_stage, up_out, up_taken, up_sums, up_moved, dp_sems[5:10]),
        Spread(line, down_stage, down_out, down_taken, down_sums, down_moved, dp_sems[10:]),
    ]
    pair = 2 * width // dps
    groups = dps // 2
    turns = [
        pltpu.make_async_copy(src, dst, turn_sem.at[i])
        for i, (src, dst) in enumerate(
            (
                (grad_gate, wg.at[:length]),
                (grad_up, wg.at[length : 2 * length]),
                (active, wu.at[:length]),
            )
        )
    ]

    def pair_load(j, slot):
        cols = pl.ds(pl.multiple_of(line.group(j) * pair, pair), pair)
        at = 2 * slot * pair
        return (
            pltpu.make_async_copy(
                hidden2.at[:, cols], wd.at[:length, at : at + pair], pair_sem.at[slot, 0]
            ),
            pltpu.make_async_copy(
                upstream.at[:, cols],
                wd.at[:length, at + pair : at + 2 * pair],
                pair_sem.at[slot, 1],
            ),
        )

    units_order = list(range(1, groups)) + [0]

    def turn():
        for n in range(max(0, big - 2), big):
            for copy in saves(n):
                copy.wait()
        for copy in turns:
            copy.start()
        for copy in pair_load(units_order[0], 0):
            copy.start()

    def unit_enter(n):
        slot = n % 2
        for copy in pair_load(units_order[n], slot):
            copy.wait()
        if n == 0:
            for copy in turns:
                copy.wait()
            wu[:length, :] = jnp.where(live[...] > 0, wu[:length, :], BF(0))
        if n + 1 < groups:
            for copy in pair_load(units_order[n + 1], 1 - slot):
                copy.start()

    def unit_gate(n):
        at = 2 * (n % 2) * pair
        unit_enter(n)
        halves(gate_stage, tn(wd[:length, at : at + pair], wg[:length, :]), 0)
        spreads[0].give(units_order[n]).start()

    def unit_up(n):
        at = 2 * (n % 2) * pair
        halves(up_stage, tn(wd[:length, at : at + pair], wg[length : 2 * length, :]), 0)
        spreads[1].give(units_order[n]).start()

    def unit_down(n):
        at = 2 * (n % 2) * pair + pair
        halves(down_stage, tn(wu[:length, :], wd[:length, at : at + pair]), 1)
        spreads[2].give(units_order[n]).start()

    after = []
    for n in range(groups):
        for task in (unit_gate, unit_up, unit_down):
            after.append(functools.partial(task, n))
        after += merged(spreads, units_order[n])

    def done_a(c):
        near_copy(c).wait()
        grad = total[...]
        vector = resid[c]
        scale = normed(vector)
        scaled = grad * gain[...]
        inner = jnp.mean(scaled * vector, axis=-1, keepdims=True)
        grad_gain[...] += jnp.sum(grad * vector * scale, axis=0, keepdims=True)
        seen = live[gat_a.mine(c), :] > 0
        back = jnp.where(seen, near[c].astype(F32), 0.0)
        back = back + scale * scaled - vector * (scale * scale * scale) * inner
        grad_resid[c] = back
        own_a[c] = back.astype(BF)

    def done_b(c):
        own_p[c] = (resid[c] + total[...]).astype(BF)

    slots = [(red_p, gat_p, norm, c) for c in range(chunks)]
    slots += [(red_a, gat_a, done_a, c) for c in range(chunks)]
    slots += [(red_b, gat_b, done_b, c) for c in range(chunks)]
    plan = {}
    for n in range(1, big):
        schedule(plan, attn_tasks(n), sub * (n - 1), 4 // sub)
    for n in range(big):
        schedule(plan, feed_tasks(n), sub * (big - 1 + n), 6 // sub)
    schedule(plan, [turn], sub * (2 * big - 1), 1)
    schedule(plan, after, sub * (2 * big - 1), 4)

    def begin(i):
        if i == 0:
            for task in attn_tasks(0):
                task()
        if i < len(slots):
            red, _, _, c = slots[i]
            red.start(c)

    drive(slots, begin, plan)
    for i in sorted(plan):
        if i >= len(slots) + 4:
            for task in plan[i]:
                task()
    finished(spreads)
    for red, gat, done, c in slots[chunks:]:
        red.close(c)
        gat.complete(c)
        gat.close(c)


def back_kernel(
    chunks,
    big,
    dps,
    branch,
    tokens,
    resid_in,
    gain,
    seg_row,
    seg_key,
    cosine,
    sine,
    query_t,
    keys,
    keys_t,
    values,
    logs,
    out_weight,
    query_in,
    kv_weight,
    other_gain,
    heads_in,
    hidden1,
    tokens_grad,
    gains_out,
    out_out,
    qkv_out,
    out_taken,
    out_sums,
    out_moved,
    qkv_taken,
    qkv_sums,
    qkv_moved,
    grad_resid,
    query_weight,
    heads_out,
    grad_gain,
    gain_parts,
    gain_dp,
    gain_sum,
    gain_z,
    grad_qkv,
    out_stage,
    qkv_stage,
    pair_out,
    pair_qkv,
    bias,
    dy,
    do_t,
    do_h,
    dq_t,
    dk,
    dv,
    part,
    held,
    total,
    own,
    near,
    in_sem,
    tok_sem,
    red_send,
    red_recv,
    gat_send,
    gat_recv,
    gat_stay,
    pair_sem,
    late_sem,
    gain_send,
    gain_recv,
    zsum_send,
    zsum_recv,
    *dp_sems,
):
    length, width = tokens.shape
    chunk = length // chunks
    wide = length // big
    sub = chunks // big
    piece = chunk // 4
    heads = query_t.shape[0] // HD
    factor = HD ** (-0.5)
    line = Line(piece)
    red = Reduce(line, part, held, total, red_send, red_recv)
    gat = Gather(line, own, tokens_grad, gat_send, gat_recv, gat_stay)
    order = list(reversed(range(big)))

    def load(c, slot):
        return pltpu.make_async_copy(
            branch.at[c * wide : (c + 1) * wide], dy.at[slot], in_sem.at[slot]
        )

    def near_copy(c):
        return pltpu.make_async_copy(tokens.at[gat.mine(c)], near.at[c], tok_sem.at[c])

    load(order[0], 0).start()
    for c in range(chunks):
        near_copy(c).start()
    late = [
        pltpu.make_async_copy(src, dst, late_sem.at[i])
        for i, (src, dst) in enumerate(
            ((query_in, query_weight), (resid_in, grad_resid), (heads_in, heads_out))
        )
    ]
    for copy in late:
        copy.start()
    line.greet(dps, every=True)
    grad_gain[...] = jnp.zeros_like(grad_gain)
    dk[...] = jnp.zeros_like(dk)
    dv[...] = jnp.zeros_like(dv)

    def enter(i):
        c, slot = order[i], i % 2
        load(c, slot).wait()
        if i + 1 < big:
            load(order[i + 1], 1 - slot).start()
        keys_n = (c + 1) * wide
        bias[:keys_n, :] = visible_bias(seg_row[...], seg_key[...], c, wide)
        grad_heads = nt(dy[slot], out_weight[...])
        do_t[...] = grad_heads.T.astype(BF)
        for h in range(heads):
            do_h[h] = grad_heads[:, h * HD : (h + 1) * HD].astype(BF)

    def attend(i, begin, end):
        c = order[i]
        keys_n = (c + 1) * wide
        cols = slice(c * wide, keys_n)

        def head(h, carry):
            here = pl.ds(pl.multiple_of(h * HD, HD), HD)
            scores = nn(keys[:keys_n, :], query_t[here, cols]) + bias[:keys_n, :]
            probs = jnp.exp(scores - logs[h, :, cols])
            grad_probs = nn(values[:keys_n, :], do_t[here, :])
            delta = jnp.sum(probs * grad_probs, axis=0, keepdims=True)
            grad_scores = (probs * (grad_probs - delta)).astype(BF)
            dv[:keys_n, :] += nn(probs.astype(BF), do_h[h])
            dk[:keys_n, :] += nn(grad_scores, query_t[here, cols].T)
            grad = nn(keys_t[:, :keys_n], grad_scores) * factor
            dq_t[here, :] = unrope(grad, cosine[:, cols], sine[:, cols])
            return carry

        lax.fori_loop(begin, end, head, 0)

    def leave(i):
        c = order[i]
        cols = slice(c * wide, (c + 1) * wide)
        lanes = heads * HD
        grad_qkv[cols, :lanes] = dq_t[...].T.astype(BF)
        grad_k = unrope(dk[cols, :].T, cosine[:, cols], sine[:, cols]).T
        grad_qkv[cols, lanes:] = jnp.concatenate([grad_k, dv[cols, :]], axis=1).astype(BF)
        if i == 0:
            for copy in late:
                copy.wait()
        step = min(512, width)
        for n in range(0, width, step):
            here = slice(n, n + step)
            value = nt(grad_qkv[cols, :lanes], query_weight[here, :])
            put(part, c, here, value + nt(grad_qkv[cols, lanes:], kv_weight[here, :]))

    def tasks(i):
        half = heads // 2
        return [
            functools.partial(enter, i),
            functools.partial(attend, i, 0, half),
            functools.partial(attend, i, half, heads),
            functools.partial(leave, i),
        ]

    spread_out = Spread(line, out_stage, out_out, out_taken, out_sums, out_moved, dp_sems[:5])
    spread_qkv = Spread(line, qkv_stage, qkv_out, qkv_taken, qkv_sums, qkv_moved, dp_sems[5:])
    pair = 2 * width // dps
    groups = dps // 2
    units_order = list(range(1, groups)) + [0]

    def pair_load(j, slot, src, dst, number):
        cols = pl.ds(pl.multiple_of(line.group(j) * pair, pair), pair)
        return pltpu.make_async_copy(src.at[:, cols], dst.at[slot], pair_sem.at[slot, number])

    def unit_out(n):
        j, slot = units_order[n], n % 2
        pair_load(j, slot, branch, pair_out, 0).wait()
        if n + 1 < groups:
            pair_load(units_order[n + 1], 1 - slot, branch, pair_out, 0).start()
        halves(out_stage, tn(heads_out[...], pair_out[slot]), 1)
        spread_out.give(j).start()

    def unit_qkv(n):
        j, slot = units_order[n], n % 2
        pair_load(j, slot, hidden1, pair_qkv, 1).wait()
        if n + 1 < groups:
            pair_load(units_order[n + 1], 1 - slot, hidden1, pair_qkv, 1).start()
        halves(qkv_stage, tn(pair_qkv[slot], grad_qkv[...]), 0)
        spread_qkv.give(j).start()

    pair_load(units_order[0], 0, branch, pair_out, 0).start()
    pair_load(units_order[0], 0, hidden1, pair_qkv, 1).start()
    work_out, work_qkv = [], []
    for n in range(groups):
        work_out.append(functools.partial(unit_out, n))
        work_out += merged([spread_out], units_order[n])
        work_qkv.append(functools.partial(unit_qkv, n))
        work_qkv += merged([spread_qkv], units_order[n])

    def done(c):
        near_copy(c).wait()
        grad = total[...]
        vector = near[c].astype(F32)
        scale = normed(vector)
        scaled = grad * gain[...]
        inner = jnp.mean(scaled * vector, axis=-1, keepdims=True)
        grad_gain[...] += jnp.sum(grad * vector * scale, axis=0, keepdims=True)
        back = grad_resid[c] + scale * scaled - vector * (scale * scale * scale) * inner
        own[c] = back.astype(BF)

    block = width // dps
    slots = [(red, gat, done, c) for c in reversed(range(chunks))]

    def gain_move(j):
        return pltpu.make_async_remote_copy(
            src_ref=gain_parts.at[line.dp_peer(j)],
            dst_ref=gain_dp.at[j],
            send_sem=gain_send.at[j],
            recv_sem=gain_recv.at[j],
            device_id=(line.dp_peer(j), line.z),
            device_id_type=MESH,
        )

    def gain_share(j):
        return pltpu.make_async_remote_copy(
            src_ref=gain_sum,
            dst_ref=gain_z.at[j],
            send_sem=zsum_send.at[j],
            recv_sem=zsum_recv.at[j],
            device_id=(line.dp, line.z_peer(j)),
            device_id_type=MESH,
        )

    def gains_dp():
        both = jnp.concatenate([grad_gain[...], other_gain[...]], axis=0)
        for d in range(dps):
            gain_parts[d] = both[:, d * block : (d + 1) * block]
        for j in range(1, dps):
            gain_move(j).start()

    def gains_line():
        for j in range(1, dps):
            gain_move(j).wait()
        value = gain_parts[line.dp]
        for j in range(1, dps):
            value = value + gain_dp[j]
        gain_sum[...] = value
        for j in range(1, 4):
            gain_share(j).start()

    def gains_end():
        value = gain_sum[...]
        for j in range(1, 4):
            gain_share(j).wait()
            value = value + gain_z[j]
        gains_out[...] = value

    plan = {}
    for i in range(1, big):
        schedule(plan, tasks(i), sub * (i - 1), 4 // sub)
    schedule(plan, work_out, 1, 3)
    schedule(plan, work_qkv, sub * (big - 1), 4)

    def begin(i):
        if i == 0:
            for task in tasks(0):
                task()
        if i < chunks:
            red.start(slots[i][3])
        if i == chunks + 2:
            gains_dp()
        if i == chunks + 3:
            gains_line()

    drive(slots, begin, plan)
    for i in sorted(plan):
        if i >= chunks + 4:
            for task in plan[i]:
                task()
    gains_end()
    finished([spread_out, spread_qkv])
    for red, gat, done, c in slots:
        red.close(c)
        gat.complete(c)
        gat.close(c)


def call(kernel, ins, outs, scratch, number, cost):
    return pl.pallas_call(
        kernel,
        in_specs=[spec for spec, _ in ins],
        out_specs=[spec for spec, _, _ in outs],
        out_shape=[jax.ShapeDtypeStruct(shape, kind) for _, shape, kind in outs],
        scratch_shapes=scratch,
        compiler_params=pltpu.CompilerParams(
            collective_id=number, has_side_effects=True, vmem_limit_bytes=LIMIT
        ),
        cost_estimate=pl.CostEstimate(flops=cost, bytes_accessed=cost // 1000, transcendentals=0),
    )(*[array for _, array in ins])


def line_scratch(chunks, piece, width):
    dma = pltpu.SemaphoreType.DMA
    buffers = [
        pltpu.VMEM((chunks, 4 * piece, width), BF),
        pltpu.VMEM((DEPTH, 5, piece, width), BF),
        pltpu.VMEM((chunks, piece, width), BF),
    ]
    sems = [dma((chunks, 3)), dma((chunks, 5)), dma((chunks, 5)), dma((chunks, 4)), dma((chunks,))]
    return buffers, sems


def spread_shapes(groups, rows, cols):
    dma = pltpu.SemaphoreType.DMA
    outs = [(VMEM, (rows, cols), F32)]
    boxes = [(ANY, (groups, rows, cols), BF)] * 3
    stage = pltpu.VMEM((2, rows, cols), BF)
    return outs, boxes, stage, [dma((groups,))] * 4 + [dma((2,))]


def tables(seg_row):
    length = seg_row.shape[0]
    start = jnp.sum((seg_row[None, :] < seg_row[:, None]).astype(jnp.int32), axis=1)
    place = (jnp.arange(length, dtype=jnp.int32) - start).astype(F32)
    half = HD // 2
    freq = jnp.power(jnp.float32(THETA), -jnp.arange(half, dtype=F32) / half)
    angle = freq[:, None] * place[None, :]
    return jnp.cos(angle), jnp.sin(angle)


def local(
    dps,
    tokens,
    segments,
    counts,
    cotangent,
    attn_gain,
    mlp_gain,
    query_weight,
    key_weight,
    value_weight,
    out_weight,
    gate_weight,
    up_weight,
    down_weight,
):
    length, width = tokens.shape
    units = gate_weight.shape[1]
    lanes = query_weight.shape[1]
    heads = lanes // HD
    chunks, big = CHUNKS, BIG
    chunk = length // chunks
    wide = length // big
    piece = chunk // 4
    dma = pltpu.SemaphoreType.DMA
    groups = dps // 2
    block = width // dps

    live = jnp.arange(length, dtype=jnp.int32) < counts[0]
    seg_row = segments.reshape(1, length)
    seg_key = jnp.where(live, segments, -1).reshape(length, 1)
    live = live.astype(jnp.int32).reshape(length, 1)
    cosine, sine = tables(segments)
    gain1 = attn_gain.reshape(1, width)
    gain2 = mlp_gain.reshape(1, width)

    buffers, sems = line_scratch(chunks, piece, width)
    total = pltpu.VMEM((piece, width), F32)
    near = pltpu.VMEM((chunks, piece, width), BF)
    by_rows = spread_shapes(groups, block, units)
    by_cols = spread_shapes(groups, units, block)
    kv_weight = jnp.concatenate([key_weight, value_weight], axis=1)
    (
        mixed,
        branch,
        hidden1,
        grad_resid,
        grad_gain2,
        heads_out,
        logs,
        query_t,
        keys,
        keys_t,
        values,
        gate_grad,
        up_grad,
        down_grad,
        *_,
    ) = call(
        functools.partial(front_kernel, chunks, big, dps),
        [
            (ANY, tokens),
            (ANY, cotangent),
            (VMEM, live),
            (VMEM, gain1),
            (VMEM, gain2),
            (VMEM, seg_row),
            (VMEM, seg_key),
            (VMEM, cosine),
            (VMEM, sine),
            (ANY, query_weight),
            (ANY, kv_weight),
            (ANY, out_weight),
            (ANY, gate_weight),
            (ANY, up_weight),
            (ANY, down_weight),
        ],
        [
            (ANY, (length, width), BF),
            (ANY, (length, width), BF),
            (ANY, (length, width), BF),
            (VMEM, (chunks, piece, width), F32),
            (VMEM, (1, width), F32),
            (VMEM, (length, lanes), BF),
            (VMEM, (heads, 1, length), F32),
            (VMEM, (lanes, length), BF),
            (VMEM, (length, HD), BF),
            (VMEM, (HD, length), BF),
            (VMEM, (length, HD), BF),
            *by_rows[0],
            *by_rows[0],
            *by_cols[0],
            (ANY, (length, width), BF),
            *[(ANY, (length, units), BF)] * 3,
            *by_rows[1],
            *by_rows[1],
            *by_cols[1],
        ],
        [
            pltpu.VMEM((width, units), BF),
            pltpu.VMEM((width, units), BF),
            pltpu.VMEM((units, width), BF),
            pltpu.VMEM((2, wide, width), BF),
            pltpu.VMEM((2, wide, width), BF),
            pltpu.VMEM((2, wide, units), BF),
            pltpu.VMEM((2, wide, units), BF),
            pltpu.VMEM((2, wide, units), BF),
            *[pltpu.VMEM((2, 16, units), BF) if block == wide else by_rows[2]] * 2,
            by_cols[2],
            pltpu.VMEM((HD, length), BF),
            pltpu.VMEM((length, wide), F32),
            pltpu.VMEM((lanes, wide), F32),
            pltpu.VMEM((chunks, piece, width), F32),
            buffers[0],
            buffers[0],
            buffers[1],
            buffers[2],
            buffers[2],
            near,
            total,
            dma((6,)),
            dma((2, 2)),
            dma((2, 3)),
            dma((2,)),
            dma((chunks,)),
            dma((3,)),
            dma((2, 2)),
            *sems,
            *sems,
            *sems,
            *by_rows[3],
            *by_rows[3],
            *by_cols[3],
        ],
        0,
        5 * 10**10,
    )

    by_cols = spread_shapes(groups, lanes, block)
    by_rows = spread_shapes(groups, block, lanes + 2 * HD)
    tokens_grad, gains, out_grad, qkv_grad, *_ = call(
        functools.partial(back_kernel, chunks, big, dps),
        [
            (ANY, branch),
            (ANY, tokens),
            (ANY, grad_resid),
            (VMEM, gain1),
            (VMEM, seg_row),
            (VMEM, seg_key),
            (VMEM, cosine),
            (VMEM, sine),
            (VMEM, query_t),
            (VMEM, keys),
            (VMEM, keys_t),
            (VMEM, values),
            (VMEM, logs),
            (VMEM, out_weight),
            (ANY, query_weight),
            (VMEM, kv_weight),
            (VMEM, grad_gain2),
            (ANY, heads_out),
            (ANY, hidden1),
        ],
        [
            (ANY, (length, width), BF),
            (VMEM, (2, block), F32),
            *by_cols[0],
            *by_rows[0],
            *by_cols[1],
            *by_rows[1],
        ],
        [
            pltpu.VMEM((chunks, piece, width), F32),
            pltpu.VMEM((width, lanes), BF),
            pltpu.VMEM((length, lanes), BF),
            pltpu.VMEM((1, width), F32),
            pltpu.VMEM((dps, 2, block), F32),
            pltpu.VMEM((dps, 2, block), F32),
            pltpu.VMEM((2, block), F32),
            pltpu.VMEM((4, 2, block), F32),
            pltpu.VMEM((length, lanes + 2 * HD), BF),
            by_cols[2],
            by_rows[2],
            pltpu.VMEM((2, length, 2 * block), BF),
            pltpu.VMEM((2, length, 2 * block), BF),
            pltpu.VMEM((length, wide), F32),
            pltpu.VMEM((2, wide, width), BF),
            pltpu.VMEM((lanes, wide), BF),
            pltpu.VMEM((heads, wide, HD), BF),
            pltpu.VMEM((lanes, wide), F32),
            pltpu.VMEM((length, HD), F32),
            pltpu.VMEM((length, HD), F32),
            buffers[0],
            buffers[1],
            total,
            buffers[2],
            near,
            dma((2,)),
            dma((chunks,)),
            *sems,
            dma((2, 2)),
            dma((3,)),
            dma((dps,)),
            dma((dps,)),
            dma((4,)),
            dma((4,)),
            *by_cols[3],
            *by_rows[3],
        ],
        1,
        2 * 10**10,
    )

    return (
        mixed,
        tokens_grad,
        gains[0],
        gains[1],
        qkv_grad[:, :lanes],
        qkv_grad[:, lanes : lanes + HD],
        qkv_grad[:, lanes + HD :],
        out_grad,
        gate_grad,
        up_grad,
        down_grad,
    )


def solution(mesh):
    placed = (
        P("dp", None),
        P("dp"),
        P("dp"),
        P("dp", None),
        P(),
        P(),
        P(None, "tensor"),
        P(None, "tensor"),
        P(None, "tensor"),
        P("tensor", None),
        P(None, "tensor"),
        P(None, "tensor"),
        P("tensor", None),
    )
    return jax.shard_map(
        functools.partial(local, mesh.shape["dp"]),
        mesh=mesh,
        in_specs=placed,
        out_specs=(
            P("dp", None),
            P("dp", None),
            P("dp"),
            P("dp"),
            P("dp", "tensor"),
            P("dp", "tensor"),
            P("dp", "tensor"),
            P("tensor", "dp"),
            P("dp", "tensor"),
            P("dp", "tensor"),
            P("tensor", "dp"),
        ),
        check_vma=False,
    )
```

```python
import functools

import jax
import jax.numpy as jnp
from jax import lax
from jax.experimental import pallas as pl
from jax.experimental.pallas import tpu as pltpu
from jax.sharding import PartitionSpec as P

HD = 64
EPS = 1e-05
THETA = 10000.0
NEGATIVE = -1e30
CHUNKS = 8
BIG = 4
DEPTH = 4
MESH = pl.DeviceIdType.MESH
BF = jnp.bfloat16
F32 = jnp.float32
ANY = pl.BlockSpec(memory_space=pl.ANY)
VMEM = pl.BlockSpec(memory_space=pltpu.VMEM)
LIMIT = 62 * 1024 * 1024


def nn(a, b):
    return lax.dot_general(a, b, (((1,), (0,)), ((), ())), preferred_element_type=F32)


def nt(a, b):
    return lax.dot_general(a, b, (((1,), (1,)), ((), ())), preferred_element_type=F32)


def tn(a, b):
    return lax.dot_general(a, b, (((0,), (0,)), ((), ())), preferred_element_type=F32)


class Line:
    def __init__(self, piece):
        self.z = lax.axis_index("tensor")
        self.dp = lax.axis_index("dp")
        self.low = self.z < 2
        self.inner = jnp.where(self.low, self.z + 1, self.z - 1)
        self.outer = jnp.where(self.low, self.z - 1, self.z + 1)
        self.end = (self.z == 0) | (self.z == 3)
        self.mid = (self.z == 1) | (self.z == 2)
        self.piece = piece

    def at(self, m):
        place = jnp.where(self.low, m, 3 - m) * self.piece
        return pl.ds(pl.multiple_of(place, self.piece), self.piece)

    def own(self):
        return pl.ds(pl.multiple_of(self.z * self.piece, self.piece), self.piece)

    def copy(self, src, dst, send, recv, target):
        return pltpu.make_async_remote_copy(
            src_ref=src,
            dst_ref=dst,
            send_sem=send,
            recv_sem=recv,
            device_id=(self.dp, target),
            device_id_type=MESH,
        )

    def greet(self, dps, every=False):
        barrier = pltpu.get_barrier_semaphore()
        self.dps = dps
        self.groups = dps // 2
        self.core = lax.rem(self.dp, 2)
        self.partner = self.dp + 1 - 2 * self.core

        def signal(dp, z):
            pl.semaphore_signal(barrier, inc=1, device_id=(dp, z), device_id_type=MESH)

        if every:
            for j in range(1, dps):
                signal(self.dp_peer(j), self.z)
            for j in range(1, 4):
                signal(self.dp, self.z_peer(j))
            pl.semaphore_wait(barrier, dps - 1 + 3)
            return
        others = [] if dps == 2 else [self.partner] + [self.peer(j) for j in range(1, self.groups)]
        for other in others:
            signal(other, self.z)
        signal(self.dp, self.inner)

        @pl.when(self.mid)
        def _():
            signal(self.dp, self.outer)
            pl.semaphore_wait(barrier, 2 + len(others))

        @pl.when(self.end)
        def _():
            pl.semaphore_wait(barrier, 1 + len(others))

    def dp_peer(self, j):
        return lax.rem(self.dp + j, self.dps)

    def z_peer(self, j):
        return lax.rem(self.z + j, 4)

    def group(self, j):
        return lax.rem(self.dp // 2 + j, self.groups)

    def peer(self, j):
        return 2 * self.group(j) + self.core


class Reduce:
    def __init__(self, line, part, held, total, send, recv, last=None):
        self.last = last
        self.line, self.part, self.held, self.total = line, part, held, total
        self.send, self.recv = send, recv

    def place(self, c):
        return (c if self.last is None else self.last - c) % DEPTH

    def copy(self, c, m, slot, target, number):
        line = self.line
        return line.copy(
            self.part.at[c, line.at(m)],
            self.held.at[self.place(c), slot],
            self.send.at[c, number],
            self.recv.at[c, slot],
            target,
        )

    def arrived(self, c, slot):
        self.copy(c, 0, slot, self.line.inner, 0).wait_recv()

    def start(self, c):
        @pl.when(self.line.end)
        def _():
            for m in (3, 2, 1):
                self.copy(c, m, m - 1, self.line.inner, m - 1).start()

    def pass_in(self, c, m):
        line = self.line

        @pl.when(line.mid)
        def _():
            self.arrived(c, m - 1)
            rows = line.at(m)
            self.part[c, rows] = (
                self.part[c, rows].astype(F32) + self.held[self.place(c), m - 1].astype(F32)
            ).astype(BF)
            self.copy(c, m, 6 - m, line.inner, 3 - m).start()

    def pass_out(self, c):
        line = self.line

        @pl.when(line.mid)
        def _():
            self.arrived(c, 3)
            rows = line.at(0)
            self.part[c, rows] = (
                self.part[c, rows].astype(F32) + self.held[self.place(c), 3].astype(F32)
            ).astype(BF)
            self.copy(c, 0, 3, line.outer, 2).start()

    def finish(self, c):
        line = self.line

        @pl.when(line.end)
        def _():
            self.arrived(c, 3)
            self.total[...] = self.part[c, line.at(0)].astype(F32) + self.held[self.place(c), 3].astype(F32)

        @pl.when(line.mid)
        def _():
            self.arrived(c, 0)
            self.arrived(c, 4)
            self.total[...] = (
                self.part[c, line.at(1)].astype(F32)
                + self.held[self.place(c), 0].astype(F32)
                + self.held[self.place(c), 4].astype(F32)
            )

    def close(self, c):
        for number in range(3):
            self.copy(c, 0, 0, self.line.inner, number).wait_send()


class Spread:
    def __init__(self, line, stage, acc, taken, sums, moved, sems):
        self.line, self.stage, self.acc = line, stage, acc
        self.taken, self.sums, self.moved = taken, sums, moved
        self.send1, self.recv1, self.send2, self.recv2, self.stay = sems

    def give(self, j):
        line = self.line
        return pltpu.make_async_remote_copy(
            src_ref=self.stage.at[1 - line.core],
            dst_ref=self.taken.at[j],
            send_sem=self.send1.at[j],
            recv_sem=self.recv1.at[j],
            device_id=(line.partner, line.z),
            device_id_type=MESH,
        )

    def move(self, j):
        line = self.line
        return pltpu.make_async_remote_copy(
            src_ref=self.sums.at[j],
            dst_ref=self.moved.at[j],
            send_sem=self.send2.at[j],
            recv_sem=self.recv2.at[j],
            device_id=(line.peer(j), line.z),
            device_id_type=MESH,
        )

    def merge_load(self, j):
        self.give(j).wait()
        self.load(self.taken.at[j], 1 - self.line.core).start()

    def load(self, src, slot):
        return pltpu.make_async_copy(src, self.stage.at[slot], self.stay.at[slot])

    def merge_add(self, j):
        core = self.line.core
        self.load(self.taken.at[j], 1 - core).wait()
        self.stage[core] = (
            self.stage[core].astype(F32) + self.stage[1 - core].astype(F32)
        ).astype(BF)
        pltpu.make_async_copy(self.stage.at[core], self.sums.at[j], self.stay.at[core]).start()

    def merge_move(self, j):
        core = self.line.core
        pltpu.make_async_copy(self.stage.at[core], self.sums.at[j], self.stay.at[core]).wait()
        if j:
            self.move(j).start()

    def sources(self):
        return [self.sums.at[0]] + [self.moved.at[j] for j in range(1, self.line.groups)]

    def last_load(self):
        self.load(self.sources()[0], 0).start()

    def last(self):
        sources = self.sources()
        for j, source in enumerate(sources):
            if j + 1 < len(sources):
                self.move(j + 1).wait()
                self.load(sources[j + 1], (j + 1) % 2).start()
            self.load(source, j % 2).wait()
            block = self.stage[j % 2].astype(F32)
            if j:
                self.acc[...] += block
            else:
                self.acc[...] = block


def merged(spreads, j):
    def run(name):
        for spread in spreads:
            getattr(spread, name)(j)

    return [functools.partial(run, name) for name in ("merge_load", "merge_add", "merge_move")]


def finished(spread, copies, before=()):
    def run():
        spread.last_load()
        for copy in before:
            copy.wait()
        spread.last()
        for copy in copies:
            copy.start()

    return run


def halves(stage, value, dim):
    size = value.shape[dim] // 2
    if dim == 0:
        stage[0] = value[:size].astype(BF)
        stage[1] = value[size:].astype(BF)
    else:
        stage[0] = value[:, :size].astype(BF)
        stage[1] = value[:, size:].astype(BF)


class Gather:
    def __init__(self, line, own, full, send, recv, stay):
        self.line, self.own, self.full = line, own, full
        self.send, self.recv, self.stay = send, recv, stay
        self.chunk = 4 * line.piece

    def rows(self, c, m):
        line = self.line
        place = c * self.chunk + jnp.where(line.low, m, 3 - m) * line.piece
        return pl.ds(pl.multiple_of(place, line.piece), line.piece)

    def mine(self, c):
        line = self.line
        place = c * self.chunk + line.z * line.piece
        return pl.ds(pl.multiple_of(place, line.piece), line.piece)

    def first(self, c, slot, target, number):
        return self.line.copy(
            self.own.at[c],
            self.full.at[self.mine(c)],
            self.send.at[c, number],
            self.recv.at[c, slot],
            target,
        )

    def onward(self, c, m, slot, target, number):
        rows = self.rows(c, m)
        return self.line.copy(
            self.full.at[rows],
            self.full.at[rows],
            self.send.at[c, number],
            self.recv.at[c, slot],
            target,
        )

    def arrived(self, c, m):
        self.onward(c, m, m, self.line.inner, 0).wait_recv()

    def stays(self, c):
        return pltpu.make_async_copy(
            self.own.at[c], self.full.at[self.mine(c)], self.stay.at[c]
        )

    def start(self, c):
        line = self.line
        self.stays(c).start()

        @pl.when(line.end)
        def _():
            self.first(c, 0, line.inner, 0).start()

        @pl.when(line.mid)
        def _():
            self.first(c, 1, line.outer, 0).start()
            self.first(c, 2, line.inner, 1).start()

    def pass_near(self, c):
        line = self.line

        @pl.when(line.end)
        def _():
            self.arrived(c, 1)

        @pl.when(line.mid)
        def _():
            self.arrived(c, 0)
            self.onward(c, 0, 3, line.inner, 2).start()
            self.arrived(c, 2)
            self.onward(c, 2, 2, line.outer, 3).start()

    def pass_far(self, c):
        line = self.line

        @pl.when(line.mid)
        def _():
            self.arrived(c, 3)
            self.onward(c, 3, 3, line.outer, 4).start()

    def complete(self, c):
        self.stays(c).wait()

        @pl.when(self.line.end)
        def _():
            for m in (2, 3):
                self.arrived(c, m)

    def close(self, c):
        line = self.line

        @pl.when(line.end)
        def _():
            self.first(c, 0, line.inner, 0).wait_send()

        @pl.when(line.mid)
        def _():
            for number in range(5):
                self.first(c, 0, line.inner, number).wait_send()


def drive(slots, begin, plan):
    n = len(slots)
    for i in range(n + 4):
        begin(i)
        work = list(plan.get(i, ()))
        count = len(work)
        for point in range(6):
            if point == 0 and 0 <= i - 4 < n:
                _, gat, _, c = slots[i - 4]
                gat.pass_far(c)
            if point == 1 and 0 <= i - 3 < n:
                _, gat, _, c = slots[i - 3]
                gat.pass_near(c)
            if point == 2 and 0 <= i - 2 < n:
                red, gat, done, c = slots[i - 2]
                red.finish(c)
                done(c)
                gat.start(c)
            if point == 3 and 0 <= i - 1 < n:
                red, _, _, c = slots[i - 1]
                red.pass_out(c)
            if point == 4 and i < n:
                red, _, _, c = slots[i]
                red.pass_in(c, 3)
            if point == 5 and i < n:
                red, _, _, c = slots[i]
                red.pass_in(c, 2)
            while work and count - len(work) < (point + 1) * count // 6:
                work.pop(0)()
        for task in work:
            task()


def schedule(plan, tasks, first, per_step):
    for k, task in enumerate(tasks):
        plan.setdefault(first + k // per_step, []).append(task)


def put(part, big, cols, value):
    chunk = part.shape[1]
    sub = value.shape[0] // chunk
    for k in range(sub):
        part[big * sub + k, :, cols] = value[k * chunk : (k + 1) * chunk].astype(BF)


def rope(t, cos, sin):
    half = HD // 2
    first, second = t[:half], t[half:]
    return jnp.concatenate([first * cos - second * sin, second * cos + first * sin], axis=0)


def unrope(t, cos, sin):
    half = HD // 2
    first, second = t[:half], t[half:]
    return jnp.concatenate([first * cos + second * sin, second * cos - first * sin], axis=0)


def normed(vector):
    return lax.rsqrt(jnp.mean(vector * vector, axis=-1, keepdims=True) + EPS)


def visible_bias(seg_row, key_row, c, chunk):
    keys = (c + 1) * chunk
    seg_q = seg_row[:, c * chunk : keys]
    seg_k = key_row[:keys, :]
    shape = (keys, chunk)
    key_at = lax.broadcasted_iota(jnp.int32, shape, 0)
    query_at = lax.broadcasted_iota(jnp.int32, shape, 1) + c * chunk
    seen = ((seg_k == seg_q) & (key_at < query_at)) | (key_at == query_at)
    return jnp.where(seen, 0.0, NEGATIVE)


def layer_kernel(
    chunks,
    big,
    dps,
    tokens,
    cotangent,
    live,
    gain1,
    gain2,
    seg_row,
    seg_key,
    cosine,
    sine,
    query_weight,
    kv_weight,
    out_weight,
    gate_weight,
    up_weight,
    down_weight,
    mixed,
    tokens_grad,
    gains_out,
    query_out,
    key_out,
    value_out,
    out_out,
    gate_out,
    up_out,
    down_out,
    branch,
    hidden1,
    hidden2,
    active,
    grad_gate,
    grad_up,
    gate_taken,
    gate_sums,
    gate_moved,
    up_taken,
    up_sums,
    up_moved,
    down_taken,
    down_sums,
    down_moved,
    out_taken,
    out_sums,
    out_moved,
    qkv_taken,
    qkv_sums,
    qkv_moved,
    wg,
    wu,
    wd,
    hid,
    dy,
    act_c,
    gate_c,
    up_c,
    gate_stage,
    up_stage,
    down_stage,
    out_stage,
    qkv_stage,
    rows_acc,
    cols_acc,
    out_acc,
    qkv_acc,
    heads_out,
    logs,
    query_t,
    keys,
    keys_t,
    values,
    do_t,
    dk,
    dv,
    grad_resid,
    grad_gain1,
    grad_gain2,
    gain_parts,
    gain_dp,
    gain_sum,
    gain_z,
    values_t,
    bias,
    heads_t,
    resid,
    part_p,
    part_a,
    held,
    own_p,
    own_a,
    near,
    total,
    w_sem,
    in_sem,
    out_sem,
    save_sem,
    near_sem,
    turn_sem,
    pair_sem,
    late_sem,
    exit_sem,
    gain_send,
    gain_recv,
    zsum_send,
    zsum_recv,
    *sems,
):
    length, width = tokens.shape
    units = wg.shape[1]
    chunk = length // chunks
    wide = length // big
    sub = chunks // big
    piece = chunk // 4
    lanes = query_t.shape[0]
    heads = lanes // HD
    if gate_stage.shape[1] != width // dps:
        gate_stage, up_stage = gate_c, up_c
    line = Line(piece)
    red_p = Reduce(line, part_p, held, total, *sems[0:2])
    gat_p = Gather(line, own_p, hidden2, *sems[2:5])
    red_a = Reduce(line, part_a, held, total, *sems[5:7])
    gat_a = Gather(line, own_a, branch, *sems[7:10])
    red_b = Reduce(line, part_p, held, total, *sems[10:12])
    gat_b = Gather(line, own_p, mixed, *sems[12:15])
    red_q = Reduce(line, part_a, held, total, *sems[15:17], last=chunks - 1)
    gat_q = Gather(line, own_a, tokens_grad, *sems[17:20])
    dp_sems = sems[20:]
    factor = HD ** (-0.5)

    def near_copy(c, src=cotangent):
        return pltpu.make_async_copy(src.at[gat_p.mine(c)], near.at[c], near_sem.at[c])

    def token_load(n):
        rows = slice(n * wide, (n + 1) * wide)
        return pltpu.make_async_copy(tokens.at[rows], hid.at[n % 2], in_sem.at[n % 2, 0])

    def hidden_save(n):
        rows = slice(n * wide, (n + 1) * wide)
        return pltpu.make_async_copy(dy.at[n % 2], hidden1.at[rows], save_sem.at[n % 2])

    def load(n):
        slot = n % 2
        rows = slice(n * wide, (n + 1) * wide)
        return (
            pltpu.make_async_copy(hidden2.at[rows], hid.at[slot], in_sem.at[slot, 0]),
            pltpu.make_async_copy(cotangent.at[rows], dy.at[slot], in_sem.at[slot, 1]),
        )

    weights = [
        pltpu.make_async_copy(src, dst, w_sem.at[i])
        for i, (src, dst) in enumerate(
            (
                (query_weight, wu.at[:, :lanes]),
                (kv_weight, wu.at[:, lanes : lanes + 2 * HD]),
                (out_weight, wd.at[:lanes]),
                (gate_weight, wg),
                (up_weight, wu),
                (down_weight, wd),
            )
        )
    ]
    token_load(0).start()
    for copy in weights[:4]:
        copy.start()
    for c in range(chunks):
        near_copy(c, tokens).start()
    line.greet(dps, every=True)
    for zero in (grad_gain1, grad_gain2, dk, dv):
        zero[...] = jnp.zeros_like(zero)

    def project(n):
        rows = slice(n * wide, (n + 1) * wide)
        token_load(n).wait()
        if n + 1 < big:
            token_load(n + 1).start()
        if n >= 2:
            hidden_save(n - 2).wait()
        if n == 0:
            weights[0].wait()
            weights[1].wait()
        vector = hid[n % 2].astype(F32)
        hidden = (vector * normed(vector) * gain1[...]).astype(BF)
        dy[n % 2] = hidden
        hidden_save(n).start()
        cos, sin = cosine[:, rows], sine[:, rows]
        raw = nn(hidden, wu[:, :lanes]).T
        for h in range(heads):
            here = slice(h * HD, (h + 1) * HD)
            turned = rope(raw[here], cos, sin) * (HD ** (-0.5))
            query_t[here, rows] = turned.astype(BF)
        raw = nn(hidden, wu[:, lanes : lanes + 2 * HD]).T
        turned = rope(raw[:HD], cos, sin)
        keys_t[:, rows] = turned.astype(BF)
        keys[rows, :] = turned.T.astype(BF)
        values_t[:, rows] = raw[HD:].astype(BF)
        values[rows, :] = raw[HD:].T.astype(BF)

    def attend(n, begin, end):
        keys_n = (n + 1) * wide
        cols = slice(n * wide, keys_n)
        if begin == 0:
            bias[:keys_n, :] = visible_bias(seg_row[...], seg_key[...], n, wide)

        def head(h, carry):
            here = pl.ds(pl.multiple_of(h * HD, HD), HD)
            scores = nn(keys[:keys_n, :], query_t[here, cols]) + bias[:keys_n, :]
            peak = jnp.max(scores, axis=0, keepdims=True)
            weights = jnp.exp(scores - peak)
            sums = jnp.sum(weights, axis=0, keepdims=True)
            probs = (weights * (1.0 / sums)).astype(BF)
            heads_t[here, :] = nn(values_t[:, :keys_n], probs)
            logs[h, :, cols] = peak + jnp.log(sums)
            return carry

        lax.fori_loop(begin, end, head, 0)

    def close_heads(n):
        if n == 0:
            weights[2].wait()
        heads_n = heads_t[...].T.astype(BF)
        heads_out[n * wide : (n + 1) * wide, :] = heads_n
        step = min(512, width)
        for at in range(0, width, step):
            cols = slice(at, at + step)
            put(part_p, n, cols, nn(heads_n, wd[:lanes, cols]))
        if n == big - 1:
            weights[4].start()
            weights[5].start()

    def attn_tasks(n):
        return [
            functools.partial(project, n),
            functools.partial(attend, n, 0, heads // 2),
            functools.partial(attend, n, heads // 2, heads),
            functools.partial(close_heads, n),
        ]

    def norm(c):
        near_copy(c, tokens).wait()
        vector = near[c].astype(F32) + total[...]
        near_copy(c).start()
        resid[c] = vector
        own_p[c] = (vector * normed(vector) * gain2[...]).astype(BF)

    def saves(n):
        slot = n % 2
        rows = slice(n * wide, (n + 1) * wide)
        return [
            pltpu.make_async_copy(src.at[slot], dst.at[rows], out_sem.at[slot, i])
            for i, (src, dst) in enumerate(((act_c, active), (gate_c, grad_gate), (up_c, grad_up)))
        ]

    def enter(n):
        if n == 0:
            for k in range(max(0, big - 2), big):
                hidden_save(k).wait()
        for c in range(n * sub, (n + 1) * sub):
            gat_p.complete(c)
        for copy in load(n):
            copy.start()
        for c in range(n * sub, (n + 1) * sub):
            red_p.close(c)
            gat_p.close(c)
        for copy in load(n):
            copy.wait()
        if n == 0:
            for copy in weights[3:]:
                copy.wait()
        if n >= 2:
            for copy in saves(n - 2):
                copy.wait()
        slot = n % 2
        dy[slot] = jnp.where(live[n * wide : (n + 1) * wide, :] > 0, dy[slot], BF(0))

    def hidden_units(n, cols):
        slot = n % 2
        gate = nn(hid[slot], wg[:, cols])
        up = nn(hid[slot], wu[:, cols])
        grad = nt(dy[slot], wd[cols, :])
        sig = 1.0 / (1.0 + jnp.exp(-gate))
        silu = gate * sig
        act_c[slot, :, cols] = (silu * up).astype(BF)
        gate_c[slot, :, cols] = (grad * up * sig * (1.0 + gate * (1.0 - sig))).astype(BF)
        up_c[slot, :, cols] = (grad * silu).astype(BF)
        if cols.stop == units:
            for copy in saves(n):
                copy.start()

    def back_part(n, cols):
        slot = n % 2
        put(part_a, n, cols, nt(gate_c[slot], wg[cols, :]) + nt(up_c[slot], wu[cols, :]))

    def down_part(n, cols):
        put(part_p, n, cols, nn(act_c[n % 2], wd[:, cols]))

    def feed_tasks(n):
        step = 512
        unit_cols = [slice(at, min(at + step, units)) for at in range(0, units, step)]
        cols = [slice(at, at + step) for at in range(0, width, step)]

        def first():
            enter(n)
            hidden_units(n, unit_cols[0])

        def several(f, group):
            for here in group:
                f(n, here)

        return [
            first,
            *[functools.partial(hidden_units, n, here) for here in unit_cols[1:]],
            functools.partial(several, back_part, cols[:2]),
            functools.partial(several, back_part, cols[2:]),
            functools.partial(several, down_part, cols),
        ]

    spreads = [
        Spread(line, gate_stage, rows_acc, gate_taken, gate_sums, gate_moved, dp_sems[:5]),
        Spread(line, up_stage, rows_acc, up_taken, up_sums, up_moved, dp_sems[5:10]),
        Spread(line, down_stage, cols_acc, down_taken, down_sums, down_moved, dp_sems[10:15]),
    ]
    spread_out = Spread(line, out_stage, out_acc, out_taken, out_sums, out_moved, dp_sems[15:20])
    spread_qkv = Spread(line, qkv_stage, qkv_acc, qkv_taken, qkv_sums, qkv_moved, dp_sems[20:])
    pair = 2 * width // dps
    groups = dps // 2
    turns = [
        pltpu.make_async_copy(src, dst, turn_sem.at[i])
        for i, (src, dst) in enumerate(
            (
                (grad_gate, wg.at[:length]),
                (grad_up, wg.at[length : 2 * length]),
                (active, wu.at[:length]),
            )
        )
    ]

    half_lanes = lanes // 2
    kv = 2 * HD
    late = [
        pltpu.make_async_copy(src, dst, late_sem.at[i])
        for i, (src, dst) in enumerate(
            [(out_weight.at[k * wide : (k + 1) * wide], dy.at[k]) for k in range(2)]
            + [
                (
                    query_weight.at[k * length : (k + 1) * length],
                    wu.at[length : 2 * length, k * lanes : (k + 1) * lanes],
                )
                for k in range(2)
            ]
            + [
                (
                    kv_weight.at[k * length : (k + 1) * length],
                    wu.at[length : 2 * length, 2 * lanes + k * kv : 2 * lanes + (k + 1) * kv],
                )
                for k in range(2)
            ]
        )
    ]

    def pair_load(j, slot):
        cols = pl.ds(pl.multiple_of(line.group(j) * pair, pair), pair)
        at = 2 * slot * pair
        return (
            pltpu.make_async_copy(
                hidden2.at[:, cols], wd.at[:length, at : at + pair], pair_sem.at[slot, 0]
            ),
            pltpu.make_async_copy(
                cotangent.at[:, cols],
                wd.at[:length, at + pair : at + 2 * pair],
                pair_sem.at[slot, 1],
            ),
        )

    units_order = list(range(1, groups)) + [0]

    def turn():
        for n in range(max(0, big - 2), big):
            for copy in saves(n):
                copy.wait()
        for copy in turns + late:
            copy.start()
        for copy in pair_load(units_order[0], 0):
            copy.start()

    def unit_enter(n):
        slot = n % 2
        for copy in pair_load(units_order[n], slot):
            copy.wait()
        if n == 0:
            for copy in turns:
                copy.wait()
            wu[:length, :] = jnp.where(live[...] > 0, wu[:length, :], BF(0))
        if n + 1 < groups:
            for copy in pair_load(units_order[n + 1], 1 - slot):
                copy.start()

    def unit_gate(n):
        at = 2 * (n % 2) * pair
        unit_enter(n)
        halves(gate_stage, tn(wd[:length, at : at + pair], wg[:length, :]), 0)
        spreads[0].give(units_order[n]).start()

    def unit_up(n):
        at = 2 * (n % 2) * pair
        halves(up_stage, tn(wd[:length, at : at + pair], wg[length : 2 * length, :]), 0)
        spreads[1].give(units_order[n]).start()

    def unit_down(n):
        at = 2 * (n % 2) * pair + pair
        halves(down_stage, tn(wu[:length, :], wd[:length, at : at + pair]), 1)
        spreads[2].give(units_order[n]).start()

    after = []
    for n in range(groups):
        for task in (unit_gate, unit_up, unit_down):
            after.append(functools.partial(task, n))
        after += merged(spreads, units_order[n])

    def done_a(c):
        near_copy(c).wait()
        grad = total[...]
        vector = resid[c]
        scale = normed(vector)
        scaled = grad * gain2[...]
        inner = jnp.mean(scaled * vector, axis=-1, keepdims=True)
        grad_gain2[...] += jnp.sum(grad * vector * scale, axis=0, keepdims=True)
        seen = live[gat_a.mine(c), :] > 0
        back = jnp.where(seen, near[c].astype(F32), 0.0)
        back = back + scale * scaled - vector * (scale * scale * scale) * inner
        grad_resid[c] = back
        own_a[c] = back.astype(BF)
        near_copy(c, tokens).start()

    def done_b(c):
        own_p[c] = (resid[c] + total[...]).astype(BF)

    order = list(reversed(range(big)))

    def branch_load(c, slot):
        return pltpu.make_async_copy(
            branch.at[c * wide : (c + 1) * wide], hid.at[slot], in_sem.at[slot, 0]
        )

    def back_enter(i):
        c, slot = order[i], i % 2
        if i == 0:
            for k in range(chunks):
                gat_a.complete(k)
        branch_load(c, slot).start()
        for k in range(c * sub, (c + 1) * sub):
            red_a.close(k)
            gat_a.close(k)
        if i == 0:
            for copy in late:
                copy.wait()
        branch_load(c, slot).wait()
        keys_n = (c + 1) * wide
        bias[:keys_n, :] = visible_bias(seg_row[...], seg_key[...], c, wide)
        for k in range(2):
            grad_heads = nt(hid[slot], dy[k])
            do_t[k * half_lanes : (k + 1) * half_lanes, :] = grad_heads.T.astype(BF)

    def back_attend(i, begin, end):
        c = order[i]
        keys_n = (c + 1) * wide
        cols = slice(c * wide, keys_n)

        def head(h, carry):
            here = pl.ds(pl.multiple_of(h * HD, HD), HD)
            scores = nn(keys[:keys_n, :], query_t[here, cols]) + bias[:keys_n, :]
            probs = jnp.exp(scores - logs[h, :, cols])
            grad_probs = nn(values[:keys_n, :], do_t[here, :])
            delta = jnp.sum(probs * grad_probs, axis=0, keepdims=True)
            grad_scores = (probs * (grad_probs - delta)).astype(BF)
            dv[:keys_n, :] += nn(probs.astype(BF), do_t[here, :].T)
            dk[:keys_n, :] += nn(grad_scores, query_t[here, cols].T)
            grad = nn(keys_t[:, :keys_n], grad_scores) * factor
            heads_t[here, :] = unrope(grad, cosine[:, cols], sine[:, cols])
            return carry

        lax.fori_loop(begin, end, head, 0)

    def back_leave(i):
        c = order[i]
        cols = slice(c * wide, (c + 1) * wide)
        wg[cols, :lanes] = heads_t[...].T.astype(BF)
        grad_k = unrope(dk[cols, :].T, cosine[:, cols], sine[:, cols]).T
        wg[cols, lanes : lanes + kv] = jnp.concatenate([grad_k, dv[cols, :]], axis=1).astype(BF)
        step = 512
        for n in range(0, width, step):
            here = slice(n, n + step)
            k, row = n // length, length + n % length
            rows = slice(row, row + step)
            value = nt(wg[cols, :lanes], wu[rows, k * lanes : (k + 1) * lanes])
            at = 2 * lanes + k * kv
            value = value + nt(wg[cols, lanes : lanes + kv], wu[rows, at : at + kv])
            put(part_a, c, here, value)

    def back_tasks(i):
        quarter = heads // 4
        return [
            functools.partial(back_enter, i),
            *[functools.partial(back_attend, i, k * quarter, (k + 1) * quarter) for k in range(4)],
            functools.partial(back_leave, i),
        ]

    def one_load(n, src, at):
        slot = n % 2
        cols = pl.ds(pl.multiple_of(line.group(units_order[n]) * pair, pair), pair)
        at = 2 * slot * pair + at * pair
        return pltpu.make_async_copy(
            src.at[:, cols], wd.at[:length, at : at + pair], pair_sem.at[slot, 0]
        )

    def unit_out(n):
        at = 2 * (n % 2) * pair + pair
        if n == 0:
            one_load(n, branch, 1).start()
        one_load(n, branch, 1).wait()
        if n + 1 < groups:
            one_load(n + 1, branch, 1).start()
        halves(out_stage, tn(heads_out[...], wd[:length, at : at + pair]), 1)
        spread_out.give(units_order[n]).start()

    def unit_qkv(n):
        at = 2 * (n % 2) * pair
        if n == 0:
            one_load(n, hidden1, 0).start()
        one_load(n, hidden1, 0).wait()
        if n + 1 < groups:
            one_load(n + 1, hidden1, 0).start()
        halves(qkv_stage, tn(wd[:length, at : at + pair], wg[:length, : lanes + kv]), 0)
        spread_qkv.give(units_order[n]).start()

    work_out, work_qkv = [], []
    for n in range(groups):
        work_out.append(functools.partial(unit_out, n))
        work_out += merged([spread_out], units_order[n])
        work_qkv.append(functools.partial(unit_qkv, n))
        work_qkv += merged([spread_qkv], units_order[n])

    exits = [
        pltpu.make_async_copy(src, dst, exit_sem.at[i])
        for i, (src, dst) in enumerate(
            (
                (rows_acc, gate_out),
                (rows_acc, up_out),
                (cols_acc, down_out),
                (out_acc, out_out),
                (qkv_acc.at[:, :lanes], query_out),
            )
        )
    ]

    def done_q(c):
        near_copy(c, tokens).wait()
        grad = total[...]
        vector = near[c].astype(F32)
        scale = normed(vector)
        scaled = grad * gain1[...]
        inner = jnp.mean(scaled * vector, axis=-1, keepdims=True)
        grad_gain1[...] += jnp.sum(grad * vector * scale, axis=0, keepdims=True)
        back = grad_resid[c] + scale * scaled - vector * (scale * scale * scale) * inner
        own_a[c] = back.astype(BF)

    block = width // dps
    def gain_move(j):
        return pltpu.make_async_remote_copy(
            src_ref=gain_parts.at[line.dp_peer(j)],
            dst_ref=gain_dp.at[j],
            send_sem=gain_send.at[j],
            recv_sem=gain_recv.at[j],
            device_id=(line.dp_peer(j), line.z),
            device_id_type=MESH,
        )

    def gain_share(j):
        return pltpu.make_async_remote_copy(
            src_ref=gain_sum,
            dst_ref=gain_z.at[j],
            send_sem=zsum_send.at[j],
            recv_sem=zsum_recv.at[j],
            device_id=(line.dp, line.z_peer(j)),
            device_id_type=MESH,
        )

    def gains_dp():
        both = jnp.concatenate([grad_gain1[...], grad_gain2[...]], axis=0)
        for d in range(dps):
            gain_parts[d] = both[:, d * block : (d + 1) * block]
        for j in range(1, dps):
            gain_move(j).start()

    def gains_line():
        for j in range(1, dps):
            gain_move(j).wait()
        value = gain_parts[line.dp]
        for j in range(1, dps):
            value = value + gain_dp[j]
        gain_sum[...] = value
        for j in range(1, 4):
            gain_share(j).start()

    def gains_end():
        value = gain_sum[...]
        for j in range(1, 4):
            gain_share(j).wait()
            value = value + gain_z[j]
        gains_out[...] = value

    slots = [(red_p, gat_p, norm, c) for c in range(chunks)]
    slots += [(red_a, gat_a, done_a, c) for c in range(chunks)]
    slots += [(red_b, gat_b, done_b, c) for c in range(chunks)]
    slots += [(red_q, gat_q, done_q, c) for c in reversed(range(chunks))]
    count = len(slots)
    plan = {}
    for n in range(1, big):
        schedule(plan, attn_tasks(n), sub * (n - 1), 4 // sub)
    for n in range(big):
        schedule(plan, feed_tasks(n), sub * (big - 1 + n), 6 // sub)
    first = sub * (2 * big - 1)
    schedule(plan, [turn], first, 1)
    schedule(plan, after, first + 1, -(-len(after) // 5))
    first = 2 * chunks + 3
    for i in range(big):
        schedule(plan, back_tasks(i), first + sub * i, 6 // sub)
    schedule(plan, work_out, first + 2, -(-len(work_out) // 8))
    ends = [
        finished(spreads[0], exits[:1]),
        finished(spreads[2], exits[2:3]),
        finished(spreads[1], exits[1:2], exits[:1]),
    ]
    schedule(plan, ends, 3 * chunks + 3, 1)
    first += sub * big
    schedule(plan, work_qkv, first, -(-len(work_qkv) // 4))
    schedule(plan, [finished(spread_out, exits[3:4])], count + 1, 1)

    def begin(i):
        if i == 0:
            for task in attn_tasks(0):
                task()
        if i < count:
            red, _, _, c = slots[i]
            red.start(c)
        if i == count + 2:
            gains_dp()
        if i == count + 3:
            gains_line()

    drive(slots, begin, plan)
    finished(spread_qkv, exits[4:])()
    key_out[...] = qkv_acc[:, lanes : lanes + HD]
    value_out[...] = qkv_acc[:, lanes + HD :]
    gains_end()
    for copy in exits[1:]:
        copy.wait()
    for red, gat, done, c in slots[2 * chunks :]:
        red.close(c)
        gat.complete(c)
        gat.close(c)


def call(kernel, ins, outs, scratch, number, cost):
    return pl.pallas_call(
        kernel,
        in_specs=[spec for spec, _ in ins],
        out_specs=[spec for spec, _, _ in outs],
        out_shape=[jax.ShapeDtypeStruct(shape, kind) for _, shape, kind in outs],
        scratch_shapes=scratch,
        compiler_params=pltpu.CompilerParams(
            collective_id=number, has_side_effects=True, vmem_limit_bytes=LIMIT
        ),
        cost_estimate=pl.CostEstimate(flops=cost, bytes_accessed=cost // 1000, transcendentals=0),
    )(*[array for _, array in ins])


def line_scratch(chunks, piece, width):
    dma = pltpu.SemaphoreType.DMA
    buffers = [
        pltpu.VMEM((chunks, 4 * piece, width), BF),
        pltpu.VMEM((DEPTH, 5, piece, width), BF),
        pltpu.VMEM((chunks, piece, width), BF),
    ]
    sems = [dma((chunks, 3)), dma((chunks, 5)), dma((chunks, 5)), dma((chunks, 4)), dma((chunks,))]
    return buffers, sems


def spread_shapes(groups, rows, cols):
    dma = pltpu.SemaphoreType.DMA
    outs = [(ANY, (rows, cols), F32)]
    boxes = [(ANY, (groups, rows, cols), BF)] * 3
    stage = pltpu.VMEM((2, rows, cols), BF)
    return outs, boxes, stage, [dma((groups,))] * 4 + [dma((2,))]


def tables(seg_row):
    length = seg_row.shape[0]
    start = jnp.sum((seg_row[None, :] < seg_row[:, None]).astype(jnp.int32), axis=1)
    place = (jnp.arange(length, dtype=jnp.int32) - start).astype(F32)
    half = HD // 2
    freq = jnp.power(jnp.float32(THETA), -jnp.arange(half, dtype=F32) / half)
    angle = freq[:, None] * place[None, :]
    return jnp.cos(angle), jnp.sin(angle)


def local(
    dps,
    tokens,
    segments,
    counts,
    cotangent,
    attn_gain,
    mlp_gain,
    query_weight,
    key_weight,
    value_weight,
    out_weight,
    gate_weight,
    up_weight,
    down_weight,
):
    length, width = tokens.shape
    units = gate_weight.shape[1]
    lanes = query_weight.shape[1]
    heads = lanes // HD
    chunks, big = CHUNKS, BIG
    chunk = length // chunks
    wide = length // big
    piece = chunk // 4
    dma = pltpu.SemaphoreType.DMA
    groups = dps // 2
    block = width // dps

    live = jnp.arange(length, dtype=jnp.int32) < counts[0]
    seg_row = segments.reshape(1, length)
    seg_key = jnp.where(live, segments, -1).reshape(length, 1)
    live = live.astype(jnp.int32).reshape(length, 1)
    cosine, sine = tables(segments)
    gain1 = attn_gain.reshape(1, width)
    gain2 = mlp_gain.reshape(1, width)

    buffers, sems = line_scratch(chunks, piece, width)
    total = pltpu.VMEM((piece, width), F32)
    near = pltpu.VMEM((chunks, piece, width), BF)
    by_rows = spread_shapes(groups, block, units)
    by_cols = spread_shapes(groups, units, block)
    for_out = spread_shapes(groups, lanes, block)
    for_qkv = spread_shapes(groups, block, lanes + 2 * HD)
    kv_weight = jnp.concatenate([key_weight, value_weight], axis=1)
    outs = call(
        functools.partial(layer_kernel, chunks, big, dps),
        [
            (ANY, tokens),
            (ANY, cotangent),
            (VMEM, live),
            (VMEM, gain1),
            (VMEM, gain2),
            (VMEM, seg_row),
            (VMEM, seg_key),
            (VMEM, cosine),
            (VMEM, sine),
            (ANY, query_weight),
            (ANY, kv_weight),
            (ANY, out_weight),
            (ANY, gate_weight),
            (ANY, up_weight),
            (ANY, down_weight),
        ],
        [
            (ANY, (length, width), BF),
            (ANY, (length, width), BF),
            (VMEM, (2, block), F32),
            (ANY, (block, lanes), F32),
            (VMEM, (block, HD), F32),
            (VMEM, (block, HD), F32),
            *for_out[0],
            *by_rows[0],
            *by_rows[0],
            *by_cols[0],
            *[(ANY, (length, width), BF)] * 3,
            *[(ANY, (length, units), BF)] * 3,
            *by_rows[1],
            *by_rows[1],
            *by_cols[1],
            *for_out[1],
            *for_qkv[1],
        ],
        [
            pltpu.VMEM((width, units), BF),
            pltpu.VMEM((width, units), BF),
            pltpu.VMEM((units, width), BF),
            pltpu.VMEM((2, wide, width), BF),
            pltpu.VMEM((2, wide, width), BF),
            pltpu.VMEM((2, wide, units), BF),
            pltpu.VMEM((2, wide, units), BF),
            pltpu.VMEM((2, wide, units), BF),
            *[pltpu.VMEM((2, 16, units), BF) if block == wide else by_rows[2]] * 2,
            by_cols[2],
            for_out[2],
            for_qkv[2],
            pltpu.VMEM((block, units), F32),
            pltpu.VMEM((units, block), F32),
            pltpu.VMEM((lanes, block), F32),
            pltpu.VMEM((block, lanes + 2 * HD), F32),
            pltpu.VMEM((length, lanes), BF),
            pltpu.VMEM((heads, 1, length), F32),
            pltpu.VMEM((lanes, length), BF),
            pltpu.VMEM((length, HD), BF),
            pltpu.VMEM((HD, length), BF),
            pltpu.VMEM((length, HD), BF),
            pltpu.VMEM((lanes, wide), BF),
            pltpu.VMEM((length, HD), F32),
            pltpu.VMEM((length, HD), F32),
            pltpu.VMEM((chunks, piece, width), F32),
            pltpu.VMEM((1, width), F32),
            pltpu.VMEM((1, width), F32),
            pltpu.VMEM((dps, 2, block), F32),
            pltpu.VMEM((dps, 2, block), F32),
            pltpu.VMEM((2, block), F32),
            pltpu.VMEM((4, 2, block), F32),
            pltpu.VMEM((HD, length), BF),
            pltpu.VMEM((length, wide), F32),
            pltpu.VMEM((lanes, wide), F32),
            pltpu.VMEM((chunks, piece, width), F32),
            buffers[0],
            buffers[0],
            buffers[1],
            buffers[2],
            buffers[2],
            near,
            total,
            dma((6,)),
            dma((2, 2)),
            dma((2, 3)),
            dma((2,)),
            dma((chunks,)),
            dma((3,)),
            dma((2, 2)),
            dma((6,)),
            dma((5,)),
            dma((dps,)),
            dma((dps,)),
            dma((4,)),
            dma((4,)),
            *sems,
            *sems,
            *sems,
            *sems,
            *by_rows[3],
            *by_rows[3],
            *by_cols[3],
            *for_out[3],
            *for_qkv[3],
        ],
        0,
        8 * 10**10,
    )
    mixed, tokens_grad, gains = outs[:3]
    return (mixed, tokens_grad, gains[0], gains[1], *outs[3:10])


def solution(mesh):
    placed = (
        P("dp", None),
        P("dp"),
        P("dp"),
        P("dp", None),
        P(),
        P(),
        P(None, "tensor"),
        P(None, "tensor"),
        P(None, "tensor"),
        P("tensor", None),
        P(None, "tensor"),
        P(None, "tensor"),
        P("tensor", None),
    )
    return jax.shard_map(
        functools.partial(local, mesh.shape["dp"]),
        mesh=mesh,
        in_specs=placed,
        out_specs=(
            P("dp", None),
            P("dp", None),
            P("dp"),
            P("dp"),
            P("dp", "tensor"),
            P("dp", "tensor"),
            P("dp", "tensor"),
            P("tensor", "dp"),
            P("dp", "tensor"),
            P("dp", "tensor"),
            P("tensor", "dp"),
        ),
        check_vma=False,
    )
```

```python
import functools

import jax
import jax.numpy as jnp
from jax import lax
from jax.experimental import pallas as pl
from jax.experimental.pallas import tpu as pltpu
from jax.sharding import PartitionSpec as P

HD = 64
EPS = 1e-05
THETA = 10000.0
NEGATIVE = -1e30
CHUNKS = 8
BIG = 4
DEPTH = 4
MESH = pl.DeviceIdType.MESH
BF = jnp.bfloat16
F32 = jnp.float32
ANY = pl.BlockSpec(memory_space=pl.ANY)
VMEM = pl.BlockSpec(memory_space=pltpu.VMEM)
LIMIT = 62 * 1024 * 1024


def nn(a, b):
    return lax.dot_general(a, b, (((1,), (0,)), ((), ())), preferred_element_type=F32)


def nt(a, b):
    return lax.dot_general(a, b, (((1,), (1,)), ((), ())), preferred_element_type=F32)


def tn(a, b):
    return lax.dot_general(a, b, (((0,), (0,)), ((), ())), preferred_element_type=F32)


class Part:
    def __init__(self, number, row, size, chunk):
        self.id, self.row, self.size = number, row, size
        self.slot, self.low, self.piece = row // chunk, row % chunk, size // 4
        self.span = slice(self.low // 4, self.low // 4 + self.piece)


def parts_of(length, chunks):
    chunk = length // chunks
    sizes = [chunk] * chunks
    return [Part(n, sum(sizes[:n]), size, chunk) for n, size in enumerate(sizes)]


class Line:
    def __init__(self):
        self.z = lax.axis_index("tensor")
        self.dp = lax.axis_index("dp")
        self.low = self.z < 2
        self.inner = jnp.where(self.low, self.z + 1, self.z - 1)
        self.outer = jnp.where(self.low, self.z - 1, self.z + 1)
        self.end = (self.z == 0) | (self.z == 3)
        self.mid = (self.z == 1) | (self.z == 2)

    def quarter(self, c, m, start):
        place = start + jnp.where(self.low, m, 3 - m) * c.piece
        return pl.ds(pl.multiple_of(place, c.piece), c.piece)

    def mine(self, c):
        return pl.ds(pl.multiple_of(c.row + self.z * c.piece, c.piece), c.piece)

    def copy(self, src, dst, send, recv, target):
        return pltpu.make_async_remote_copy(
            src_ref=src,
            dst_ref=dst,
            send_sem=send,
            recv_sem=recv,
            device_id=(self.dp, target),
            device_id_type=MESH,
        )

    def greet(self, dps, every=False):
        barrier = pltpu.get_barrier_semaphore()
        self.dps = dps
        self.groups = dps // 2
        self.core = lax.rem(self.dp, 2)
        self.partner = self.dp + 1 - 2 * self.core

        def signal(dp, z):
            pl.semaphore_signal(barrier, inc=1, device_id=(dp, z), device_id_type=MESH)

        if every:
            for j in range(1, dps):
                signal(self.dp_peer(j), self.z)
            for j in range(1, 4):
                signal(self.dp, self.z_peer(j))
            pl.semaphore_wait(barrier, dps - 1 + 3)
            return
        others = [] if dps == 2 else [self.partner] + [self.peer(j) for j in range(1, self.groups)]
        for other in others:
            signal(other, self.z)
        signal(self.dp, self.inner)

        @pl.when(self.mid)
        def _():
            signal(self.dp, self.outer)
            pl.semaphore_wait(barrier, 2 + len(others))

        @pl.when(self.end)
        def _():
            pl.semaphore_wait(barrier, 1 + len(others))

    def dp_peer(self, j):
        return lax.rem(self.dp + j, self.dps)

    def z_peer(self, j):
        return lax.rem(self.z + j, 4)

    def group(self, j):
        return lax.rem(self.dp // 2 + j, self.groups)

    def peer(self, j):
        return 2 * self.group(j) + self.core


class Reduce:
    def __init__(self, line, part, held, total, send, recv, turn):
        self.turn = turn
        self.line, self.part, self.held, self.total = line, part, held, total
        self.send, self.recv = send, recv

    def place(self, c):
        return self.turn[c.id] % DEPTH

    def rows(self, c, m):
        return self.line.quarter(c, m, c.low)

    def copy(self, c, m, slot, target, number):
        line = self.line
        return line.copy(
            self.part.at[c.slot, self.rows(c, m)],
            self.held.at[self.place(c), slot, : c.piece],
            self.send.at[c.id, number],
            self.recv.at[c.id, slot],
            target,
        )

    def arrived(self, c, slot):
        self.copy(c, 0, slot, self.line.inner, 0).wait_recv()

    def start(self, c):
        @pl.when(self.line.end)
        def _():
            for m in (3, 2, 1):
                self.copy(c, m, m - 1, self.line.inner, m - 1).start()

    def pass_in(self, c, m):
        line = self.line

        @pl.when(line.mid)
        def _():
            self.arrived(c, m - 1)
            rows = self.rows(c, m)
            self.part[c.slot, rows] = (
                self.part[c.slot, rows].astype(F32) + self.held[self.place(c), m - 1, : c.piece].astype(F32)
            ).astype(BF)
            self.copy(c, m, 6 - m, line.inner, 3 - m).start()

    def pass_out(self, c):
        line = self.line

        @pl.when(line.mid)
        def _():
            self.arrived(c, 3)
            rows = self.rows(c, 0)
            self.part[c.slot, rows] = (
                self.part[c.slot, rows].astype(F32) + self.held[self.place(c), 3, : c.piece].astype(F32)
            ).astype(BF)
            self.copy(c, 0, 3, line.outer, 2).start()

    def finish(self, c):
        line = self.line

        @pl.when(line.end)
        def _():
            self.arrived(c, 3)
            self.total[: c.piece] = self.part[c.slot, self.rows(c, 0)].astype(F32) + self.held[self.place(c), 3, : c.piece].astype(F32)

        @pl.when(line.mid)
        def _():
            self.arrived(c, 0)
            self.arrived(c, 4)
            self.total[: c.piece] = (
                self.part[c.slot, self.rows(c, 1)].astype(F32)
                + self.held[self.place(c), 0, : c.piece].astype(F32)
                + self.held[self.place(c), 4, : c.piece].astype(F32)
            )

    def close(self, c):
        for number in range(3):
            self.copy(c, 0, 0, self.line.inner, number).wait_send()


class Spread:
    def __init__(self, line, stage, acc, taken, sums, moved, sems):
        self.line, self.stage, self.acc = line, stage, acc
        self.taken, self.sums, self.moved = taken, sums, moved
        self.send1, self.recv1, self.send2, self.recv2, self.stay = sems

    def give(self, j):
        line = self.line
        return pltpu.make_async_remote_copy(
            src_ref=self.stage.at[1 - line.core],
            dst_ref=self.taken.at[j],
            send_sem=self.send1.at[j],
            recv_sem=self.recv1.at[j],
            device_id=(line.partner, line.z),
            device_id_type=MESH,
        )

    def move(self, j):
        line = self.line
        return pltpu.make_async_remote_copy(
            src_ref=self.sums.at[j],
            dst_ref=self.moved.at[j],
            send_sem=self.send2.at[j],
            recv_sem=self.recv2.at[j],
            device_id=(line.peer(j), line.z),
            device_id_type=MESH,
        )

    def merge_load(self, j):
        self.give(j).wait()
        self.load(self.taken.at[j], 1 - self.line.core).start()

    def load(self, src, slot):
        return pltpu.make_async_copy(src, self.stage.at[slot], self.stay.at[slot])

    def merge_add(self, j):
        core = self.line.core
        self.load(self.taken.at[j], 1 - core).wait()
        self.stage[core] = (
            self.stage[core].astype(F32) + self.stage[1 - core].astype(F32)
        ).astype(BF)
        pltpu.make_async_copy(self.stage.at[core], self.sums.at[j], self.stay.at[core]).start()

    def merge_move(self, j):
        core = self.line.core
        pltpu.make_async_copy(self.stage.at[core], self.sums.at[j], self.stay.at[core]).wait()
        if j:
            self.move(j).start()

    def sources(self):
        return [self.sums.at[0]] + [self.moved.at[j] for j in range(1, self.line.groups)]

    def last_load(self):
        self.load(self.sources()[0], 0).start()

    def last(self):
        sources = self.sources()
        for j, source in enumerate(sources):
            if j + 1 < len(sources):
                self.move(j + 1).wait()
                self.load(sources[j + 1], (j + 1) % 2).start()
            self.load(source, j % 2).wait()
            block = self.stage[j % 2].astype(F32)
            if j:
                self.acc[...] += block
            else:
                self.acc[...] = block


def merged(spreads, j):
    def run(name):
        for spread in spreads:
            getattr(spread, name)(j)

    return [functools.partial(run, name) for name in ("merge_load", "merge_add", "merge_move")]


def finished(spread, copies, before=()):
    def run():
        spread.last_load()
        for copy in before:
            copy.wait()
        spread.last()
        for copy in copies:
            copy.start()

    return run


def halves(stage, value, dim):
    size = value.shape[dim] // 2
    if dim == 0:
        stage[0] = value[:size].astype(BF)
        stage[1] = value[size:].astype(BF)
    else:
        stage[0] = value[:, :size].astype(BF)
        stage[1] = value[:, size:].astype(BF)


class Gather:
    def __init__(self, line, own, full, send, recv, stay):
        self.line, self.own, self.full = line, own, full
        self.send, self.recv, self.stay = send, recv, stay

    def rows(self, c, m):
        return self.line.quarter(c, m, c.row)

    def first(self, c, slot, target, number):
        return self.line.copy(
            self.own.at[c.slot, c.span],
            self.full.at[self.line.mine(c)],
            self.send.at[c.id, number],
            self.recv.at[c.id, slot],
            target,
        )

    def onward(self, c, m, slot, target, number):
        rows = self.rows(c, m)
        return self.line.copy(
            self.full.at[rows],
            self.full.at[rows],
            self.send.at[c.id, number],
            self.recv.at[c.id, slot],
            target,
        )

    def arrived(self, c, m):
        self.onward(c, m, m, self.line.inner, 0).wait_recv()

    def stays(self, c):
        return pltpu.make_async_copy(
            self.own.at[c.slot, c.span], self.full.at[self.line.mine(c)], self.stay.at[c.id]
        )

    def start(self, c):
        line = self.line
        self.stays(c).start()

        @pl.when(line.end)
        def _():
            self.first(c, 0, line.inner, 0).start()

        @pl.when(line.mid)
        def _():
            self.first(c, 1, line.outer, 0).start()
            self.first(c, 2, line.inner, 1).start()

    def pass_near(self, c):
        line = self.line

        @pl.when(line.end)
        def _():
            self.arrived(c, 1)

        @pl.when(line.mid)
        def _():
            self.arrived(c, 0)
            self.onward(c, 0, 3, line.inner, 2).start()
            self.arrived(c, 2)
            self.onward(c, 2, 2, line.outer, 3).start()

    def pass_far(self, c):
        line = self.line

        @pl.when(line.mid)
        def _():
            self.arrived(c, 3)
            self.onward(c, 3, 3, line.outer, 4).start()

    def complete(self, c):
        self.stays(c).wait()

        @pl.when(self.line.end)
        def _():
            for m in (2, 3):
                self.arrived(c, m)

    def close(self, c):
        line = self.line

        @pl.when(line.end)
        def _():
            self.first(c, 0, line.inner, 0).wait_send()

        @pl.when(line.mid)
        def _():
            for number in range(5):
                self.first(c, 0, line.inner, number).wait_send()


def drive(slots, begin, plan):
    n = len(slots)
    for i in range(n + 4):
        begin(i)
        work = list(plan.get(i, ()))
        count = len(work)
        for point in range(6):
            if point == 0 and 0 <= i - 4 < n:
                _, gat, _, c = slots[i - 4]
                gat.pass_far(c)
            if point == 1 and 0 <= i - 3 < n:
                _, gat, _, c = slots[i - 3]
                gat.pass_near(c)
            if point == 2 and 0 <= i - 2 < n:
                red, gat, done, c = slots[i - 2]
                red.finish(c)
                done(c)
                gat.start(c)
            if point == 3 and 0 <= i - 1 < n:
                red, _, _, c = slots[i - 1]
                red.pass_out(c)
            if point == 4 and i < n:
                red, _, _, c = slots[i]
                red.pass_in(c, 3)
            if point == 5 and i < n:
                red, _, _, c = slots[i]
                red.pass_in(c, 2)
            while work and count - len(work) < (point + 1) * count // 6:
                work.pop(0)()
        for task in work:
            task()


def schedule(plan, tasks, first, per_step):
    for k, task in enumerate(tasks):
        plan.setdefault(first + k // per_step, []).append(task)


def put(part, row, cols, value):
    chunk, rows = part.shape[1], value.shape[0]
    done = 0
    while done < rows:
        slot, low = (row + done) // chunk, (row + done) % chunk
        size = min(chunk - low, rows - done)
        part[slot, low : low + size, cols] = value[done : done + size].astype(BF)
        done += size


def rope(t, cos, sin):
    half = HD // 2
    first, second = t[:half], t[half:]
    return jnp.concatenate([first * cos - second * sin, second * cos + first * sin], axis=0)


def unrope(t, cos, sin):
    half = HD // 2
    first, second = t[:half], t[half:]
    return jnp.concatenate([first * cos + second * sin, second * cos - first * sin], axis=0)


def normed(vector):
    return lax.rsqrt(jnp.mean(vector * vector, axis=-1, keepdims=True) + EPS)


def visible_bias(seg_row, key_row, row, rows):
    keys = row + rows
    seg_q = seg_row[:, row:keys]
    seg_k = key_row[:keys, :]
    shape = (keys, rows)
    key_at = lax.broadcasted_iota(jnp.int32, shape, 0)
    query_at = lax.broadcasted_iota(jnp.int32, shape, 1) + row
    seen = ((seg_k == seg_q) & (key_at < query_at)) | (key_at == query_at)
    return jnp.where(seen, 0.0, NEGATIVE)


def layer_kernel(
    chunks,
    big,
    dps,
    tokens,
    cotangent,
    gain1,
    gain2,
    seg_row,
    key_row,
    cosine,
    sine,
    query_weight,
    kv_weight,
    out_weight,
    gate_weight,
    up_weight,
    down_weight,
    mixed,
    tokens_grad,
    gains_out,
    query_out,
    key_out,
    value_out,
    out_out,
    gate_out,
    up_out,
    down_out,
    branch,
    hidden1,
    hidden2,
    active,
    grad_gate,
    grad_up,
    gate_taken,
    gate_sums,
    gate_moved,
    up_taken,
    up_sums,
    up_moved,
    down_taken,
    down_sums,
    down_moved,
    out_taken,
    out_sums,
    out_moved,
    qkv_taken,
    qkv_sums,
    qkv_moved,
    wg,
    wu,
    wd,
    hid,
    dy,
    act_c,
    gate_c,
    up_c,
    gate_stage,
    up_stage,
    down_stage,
    out_stage,
    qkv_stage,
    rows_acc,
    cols_acc,
    out_acc,
    qkv_acc,
    heads_out,
    logs,
    query_t,
    keys,
    keys_t,
    values,
    do_t,
    dk,
    dv,
    grad_resid,
    grad_gain1,
    grad_gain2,
    gain_parts,
    gain_dp,
    gain_sum,
    gain_z,
    values_t,
    seg_key,
    bias,
    heads_t,
    resid,
    part_p,
    part_a,
    held,
    own_p,
    own_a,
    near,
    total,
    w_sem,
    in_sem,
    out_sem,
    save_sem,
    near_sem,
    turn_sem,
    pair_sem,
    late_sem,
    exit_sem,
    gain_send,
    gain_recv,
    zsum_send,
    zsum_recv,
    *sems,
):
    length, width = tokens.shape
    units = wg.shape[1]
    chunk = length // chunks
    wide = length // big
    sub = chunks // big
    parts = parts_of(length, chunks)
    count = len(parts)
    lanes = query_t.shape[0]
    heads = lanes // HD
    if gate_stage.shape[1] != width // dps:
        gate_stage, up_stage = gate_c, up_c
    line = Line()
    turns_of = [{c.id: k * count + c.id for c in parts} for k in range(3)]
    turns_of.append({c.id: 4 * count - 1 - c.id for c in parts})
    red_p = Reduce(line, part_p, held, total, *sems[0:2], turns_of[0])
    gat_p = Gather(line, own_p, hidden2, *sems[2:5])
    red_a = Reduce(line, part_a, held, total, *sems[5:7], turns_of[1])
    gat_a = Gather(line, own_a, branch, *sems[7:10])
    red_b = Reduce(line, part_p, held, total, *sems[10:12], turns_of[2])
    gat_b = Gather(line, own_p, mixed, *sems[12:15])
    red_q = Reduce(line, part_a, held, total, *sems[15:17], turns_of[3])
    gat_q = Gather(line, own_a, tokens_grad, *sems[17:20])
    dp_sems = sems[20:]
    factor = HD ** (-0.5)

    def near_copy(c, src=cotangent):
        return pltpu.make_async_copy(
            src.at[line.mine(c)], near.at[c.slot, c.span], near_sem.at[c.id]
        )

    def token_load(n):
        rows = slice(n * wide, (n + 1) * wide)
        return pltpu.make_async_copy(tokens.at[rows], hid.at[n % 2], in_sem.at[n % 2, 0])

    def hidden_save(n):
        rows = slice(n * wide, (n + 1) * wide)
        return pltpu.make_async_copy(dy.at[n % 2], hidden1.at[rows], save_sem.at[n % 2])

    def load(n):
        slot = n % 2
        rows = slice(n * wide, (n + 1) * wide)
        return (
            pltpu.make_async_copy(hidden2.at[rows], hid.at[slot], in_sem.at[slot, 0]),
            pltpu.make_async_copy(cotangent.at[rows], dy.at[slot], in_sem.at[slot, 1]),
        )

    weights = [
        pltpu.make_async_copy(src, dst, w_sem.at[i])
        for i, (src, dst) in enumerate(
            (
                (query_weight, wu.at[:, :lanes]),
                (kv_weight, wd.at[lanes : lanes + 2 * HD]),
                (out_weight, wd.at[:lanes]),
                (gate_weight, wg),
                (up_weight, wu),
                (down_weight, wd),
            )
        )
    ]
    token_load(0).start()
    for copy in weights[:4]:
        copy.start()
    for c in parts:
        near_copy(c, tokens).start()
    line.greet(dps, every=True)
    seg_key[...] = jnp.broadcast_to(key_row[...], (128, length)).T[:, :1]
    for zero in (grad_gain1, grad_gain2, dk, dv):
        zero[...] = jnp.zeros_like(zero)

    def project(row, size):
        n, low = row // wide, row % wide
        rows = slice(row, row + size)
        here = slice(low, low + size)
        if low == 0:
            token_load(n).wait()
            if n + 1 < big:
                token_load(n + 1).start()
            if n >= 2:
                hidden_save(n - 2).wait()
        if row == 0:
            weights[0].wait()
            weights[1].wait()
        vector = hid[n % 2, here].astype(F32)
        hidden = (vector * normed(vector) * gain1[...]).astype(BF)
        dy[n % 2, here] = hidden
        if low + size == wide:
            hidden_save(n).start()
        cos, sin = cosine[:, rows], sine[:, rows]
        raw = nn(hidden, wu[:, :lanes]).T
        for h in range(heads):
            here = slice(h * HD, (h + 1) * HD)
            turned = rope(raw[here], cos, sin) * (HD ** (-0.5))
            query_t[here, rows] = turned.astype(BF)
        raw = nt(wd[lanes : lanes + 2 * HD, :], hidden)
        turned = rope(raw[:HD], cos, sin)
        keys_t[:, rows] = turned.astype(BF)
        keys[rows, :] = turned.T.astype(BF)
        values_t[:, rows] = raw[HD:].astype(BF)
        values[rows, :] = raw[HD:].T.astype(BF)

    def attend(row, size, begin, end):
        keys_n = row + size
        cols = slice(row, keys_n)
        if begin == 0:
            bias[:keys_n, :size] = visible_bias(seg_row[...], seg_key[...], row, size)

        def head(h, carry):
            here = pl.ds(pl.multiple_of(h * HD, HD), HD)
            scores = nn(keys[:keys_n, :], query_t[here, cols]) + bias[:keys_n, :size]
            peak = jnp.max(scores, axis=0, keepdims=True)
            weights = jnp.exp(scores - peak)
            sums = jnp.sum(weights, axis=0, keepdims=True)
            probs = (weights * (1.0 / sums)).astype(BF)
            heads_t[here, :size] = nn(values_t[:, :keys_n], probs)
            logs[h, :, cols] = peak + jnp.log(sums)
            return carry

        lax.fori_loop(begin, end, head, 0)

    def close_heads(row, size):
        if row == 0:
            weights[2].wait()
        heads_n = heads_t[:, :size].T.astype(BF)
        heads_out[row : row + size, :] = heads_n
        step = min(512, width)
        for at in range(0, width, step):
            cols = slice(at, at + step)
            put(part_p, row, cols, nn(heads_n, wd[:lanes, cols]))
        if row + size == length:
            weights[4].start()
            weights[5].start()

    def attn_tasks(row, size):
        return [
            functools.partial(project, row, size),
            functools.partial(attend, row, size, 0, heads // 2),
            functools.partial(attend, row, size, heads // 2, heads),
            functools.partial(close_heads, row, size),
        ]

    def norm(c):
        near_copy(c, tokens).wait()
        vector = near[c.slot, c.span].astype(F32) + total[: c.piece]
        near_copy(c).start()
        resid[c.slot, c.span] = vector
        own_p[c.slot, c.span] = (vector * normed(vector) * gain2[...]).astype(BF)

    def saves(n):
        slot = n % 2
        rows = slice(n * wide, (n + 1) * wide)
        return [
            pltpu.make_async_copy(src.at[slot], dst.at[rows], out_sem.at[slot, i])
            for i, (src, dst) in enumerate(((act_c, active), (gate_c, grad_gate), (up_c, grad_up)))
        ]

    def inside(n):
        return [c for c in parts if c.row // wide == n]

    def enter(n):
        if n == 0:
            for k in range(max(0, big - 2), big):
                hidden_save(k).wait()
        for c in inside(n):
            gat_p.complete(c)
        for copy in load(n):
            copy.start()
        for c in inside(n):
            red_p.close(c)
            gat_p.close(c)
        for copy in load(n):
            copy.wait()
        if n == 0:
            for copy in weights[3:]:
                copy.wait()
        if n >= 2:
            for copy in saves(n - 2):
                copy.wait()
        slot = n % 2
        dy[slot] = jnp.where(seg_key[n * wide : (n + 1) * wide, :] >= 0.0, dy[slot], BF(0))

    def hidden_units(n, cols):
        slot = n % 2
        gate = nn(hid[slot], wg[:, cols])
        up = nn(hid[slot], wu[:, cols])
        grad = nt(dy[slot], wd[cols, :])
        sig = 1.0 / (1.0 + jnp.exp(-gate))
        silu = gate * sig
        act_c[slot, :, cols] = (silu * up).astype(BF)
        gate_c[slot, :, cols] = (grad * up * sig * (1.0 + gate * (1.0 - sig))).astype(BF)
        up_c[slot, :, cols] = (grad * silu).astype(BF)
        if cols.stop == units:
            for copy in saves(n):
                copy.start()

    def back_part(n, cols):
        slot = n % 2
        put(part_a, n * wide, cols, nt(gate_c[slot], wg[cols, :]) + nt(up_c[slot], wu[cols, :]))

    def down_part(n, cols):
        put(part_p, n * wide, cols, nn(act_c[n % 2], wd[:, cols]))

    def feed_tasks(n):
        step = 512
        unit_cols = [slice(at, min(at + step, units)) for at in range(0, units, step)]
        cols = [slice(at, at + step) for at in range(0, width, step)]

        def first():
            enter(n)
            hidden_units(n, unit_cols[0])

        def several(f, group):
            for here in group:
                f(n, here)

        return [
            first,
            *[functools.partial(hidden_units, n, here) for here in unit_cols[1:]],
            functools.partial(several, back_part, cols[:2]),
            functools.partial(several, back_part, cols[2:]),
            functools.partial(several, down_part, cols),
        ]

    spreads = [
        Spread(line, gate_stage, rows_acc, gate_taken, gate_sums, gate_moved, dp_sems[:5]),
        Spread(line, up_stage, rows_acc, up_taken, up_sums, up_moved, dp_sems[5:10]),
        Spread(line, down_stage, cols_acc, down_taken, down_sums, down_moved, dp_sems[10:15]),
    ]
    spread_out = Spread(line, out_stage, out_acc, out_taken, out_sums, out_moved, dp_sems[15:20])
    spread_qkv = Spread(line, qkv_stage, qkv_acc, qkv_taken, qkv_sums, qkv_moved, dp_sems[20:])
    pair = 2 * width // dps
    groups = dps // 2
    turns = [
        pltpu.make_async_copy(src, dst, turn_sem.at[i])
        for i, (src, dst) in enumerate(
            (
                (grad_gate, wg.at[:length]),
                (grad_up, wg.at[length : 2 * length]),
                (active, wu.at[:length]),
            )
        )
    ]

    half_lanes = lanes // 2
    kv = 2 * HD
    late = [
        pltpu.make_async_copy(src, dst, late_sem.at[i])
        for i, (src, dst) in enumerate(
            [(out_weight.at[k * wide : (k + 1) * wide], dy.at[k]) for k in range(2)]
            + [
                (
                    query_weight.at[k * length : (k + 1) * length],
                    wu.at[length : 2 * length, k * lanes : (k + 1) * lanes],
                )
                for k in range(2)
            ]
            + [(kv_weight, wd.at[length : length + kv])]
        )
    ]

    def pair_load(j, slot):
        cols = pl.ds(pl.multiple_of(line.group(j) * pair, pair), pair)
        at = 2 * slot * pair
        return (
            pltpu.make_async_copy(
                hidden2.at[:, cols], wd.at[:length, at : at + pair], pair_sem.at[slot, 0]
            ),
            pltpu.make_async_copy(
                cotangent.at[:, cols],
                wd.at[:length, at + pair : at + 2 * pair],
                pair_sem.at[slot, 1],
            ),
        )

    units_order = list(range(1, groups)) + [0]

    def turn():
        for n in range(max(0, big - 2), big):
            for copy in saves(n):
                copy.wait()
        for copy in turns + late:
            copy.start()
        for copy in pair_load(units_order[0], 0):
            copy.start()

    def unit_enter(n):
        slot = n % 2
        for copy in pair_load(units_order[n], slot):
            copy.wait()
        if n == 0:
            for copy in turns:
                copy.wait()
            wu[:length, :] = jnp.where(seg_key[...] >= 0.0, wu[:length, :], BF(0))
        if n + 1 < groups:
            for copy in pair_load(units_order[n + 1], 1 - slot):
                copy.start()

    def unit_gate(n):
        at = 2 * (n % 2) * pair
        unit_enter(n)
        halves(gate_stage, tn(wd[:length, at : at + pair], wg[:length, :]), 0)
        spreads[0].give(units_order[n]).start()

    def unit_up(n):
        at = 2 * (n % 2) * pair
        halves(up_stage, tn(wd[:length, at : at + pair], wg[length : 2 * length, :]), 0)
        spreads[1].give(units_order[n]).start()

    def unit_down(n):
        at = 2 * (n % 2) * pair + pair
        halves(down_stage, tn(wu[:length, :], wd[:length, at : at + pair]), 1)
        spreads[2].give(units_order[n]).start()

    after = []
    for n in range(groups):
        for task in (unit_gate, unit_up, unit_down):
            after.append(functools.partial(task, n))
        after += merged(spreads, units_order[n])

    def done_a(c):
        near_copy(c).wait()
        grad = total[: c.piece]
        vector = resid[c.slot, c.span]
        scale = normed(vector)
        scaled = grad * gain2[...]
        inner = jnp.mean(scaled * vector, axis=-1, keepdims=True)
        grad_gain2[...] += jnp.sum(grad * vector * scale, axis=0, keepdims=True)
        seen = seg_key[line.mine(c), :] >= 0.0
        back = jnp.where(seen, near[c.slot, c.span].astype(F32), 0.0)
        back = back + scale * scaled - vector * (scale * scale * scale) * inner
        grad_resid[c.slot, c.span] = back
        own_a[c.slot, c.span] = back.astype(BF)
        near_copy(c, tokens).start()

    def done_b(c):
        own_p[c.slot, c.span] = (resid[c.slot, c.span] + total[: c.piece]).astype(BF)

    order = list(reversed(range(big)))

    def branch_load(c, slot):
        return pltpu.make_async_copy(
            branch.at[c * wide : (c + 1) * wide], hid.at[slot], in_sem.at[slot, 0]
        )

    def back_enter(i):
        c, slot = order[i], i % 2
        if i == 0:
            for k in parts:
                gat_a.complete(k)
        branch_load(c, slot).start()
        for k in inside(c):
            red_a.close(k)
            gat_a.close(k)
        if i == 0:
            for copy in late:
                copy.wait()
        branch_load(c, slot).wait()
        keys_n = (c + 1) * wide
        bias[:keys_n, :] = visible_bias(seg_row[...], seg_key[...], c * wide, wide)
        for k in range(2):
            grad_heads = nt(hid[slot], dy[k])
            do_t[k * half_lanes : (k + 1) * half_lanes, :] = grad_heads.T.astype(BF)

    def back_attend(i, begin, end):
        c = order[i]
        keys_n = (c + 1) * wide
        cols = slice(c * wide, keys_n)

        def head(h, carry):
            here = pl.ds(pl.multiple_of(h * HD, HD), HD)
            scores = nn(keys[:keys_n, :], query_t[here, cols]) + bias[:keys_n, :]
            probs = jnp.exp(scores - logs[h, :, cols])
            grad_probs = nn(values[:keys_n, :], do_t[here, :])
            delta = jnp.sum(probs * grad_probs, axis=0, keepdims=True)
            grad_scores = (probs * (grad_probs - delta)).astype(BF)
            dv[:keys_n, :] += nn(probs.astype(BF), do_t[here, :].T)
            dk[:keys_n, :] += nn(grad_scores, query_t[here, cols].T)
            grad = nn(keys_t[:, :keys_n], grad_scores) * factor
            heads_t[here, :] = unrope(grad, cosine[:, cols], sine[:, cols])
            return carry

        lax.fori_loop(begin, end, head, 0)

    def back_leave(i):
        c = order[i]
        cols = slice(c * wide, (c + 1) * wide)
        wg[cols, :lanes] = heads_t[...].T.astype(BF)
        grad_k = unrope(dk[cols, :].T, cosine[:, cols], sine[:, cols]).T
        wg[cols, lanes : lanes + kv] = jnp.concatenate([grad_k, dv[cols, :]], axis=1).astype(BF)
        step = 512
        for n in range(0, width, step):
            here = slice(n, n + step)
            k, row = n // length, length + n % length
            rows = slice(row, row + step)
            value = nt(wg[cols, :lanes], wu[rows, k * lanes : (k + 1) * lanes])
            value = value + nn(wg[cols, lanes : lanes + kv], wd[length : length + kv, here])
            put(part_a, c * wide, here, value)

    def back_tasks(i):
        quarter = heads // 4
        return [
            functools.partial(back_enter, i),
            *[functools.partial(back_attend, i, k * quarter, (k + 1) * quarter) for k in range(4)],
            functools.partial(back_leave, i),
        ]

    def one_load(n, src, at):
        slot = n % 2
        cols = pl.ds(pl.multiple_of(line.group(units_order[n]) * pair, pair), pair)
        at = 2 * slot * pair + at * pair
        return pltpu.make_async_copy(
            src.at[:, cols], wd.at[:length, at : at + pair], pair_sem.at[slot, 0]
        )

    def unit_out(n):
        at = 2 * (n % 2) * pair + pair
        if n == 0:
            one_load(n, branch, 1).start()
        one_load(n, branch, 1).wait()
        if n + 1 < groups:
            one_load(n + 1, branch, 1).start()
        halves(out_stage, tn(heads_out[...], wd[:length, at : at + pair]), 1)
        spread_out.give(units_order[n]).start()

    def unit_qkv(n):
        at = 2 * (n % 2) * pair
        if n == 0:
            one_load(n, hidden1, 0).start()
        one_load(n, hidden1, 0).wait()
        if n + 1 < groups:
            one_load(n + 1, hidden1, 0).start()
        halves(qkv_stage, tn(wd[:length, at : at + pair], wg[:length, : lanes + kv]), 0)
        spread_qkv.give(units_order[n]).start()

    work_out, work_qkv = [], []
    for n in range(groups):
        work_out.append(functools.partial(unit_out, n))
        work_out += merged([spread_out], units_order[n])
        work_qkv.append(functools.partial(unit_qkv, n))
        work_qkv += merged([spread_qkv], units_order[n])

    exits = [
        pltpu.make_async_copy(src, dst, exit_sem.at[i])
        for i, (src, dst) in enumerate(
            (
                (rows_acc, gate_out),
                (rows_acc, up_out),
                (cols_acc, down_out),
                (out_acc, out_out),
                (qkv_acc.at[:, :lanes], query_out),
            )
        )
    ]

    def done_q(c):
        near_copy(c, tokens).wait()
        grad = total[: c.piece]
        vector = near[c.slot, c.span].astype(F32)
        scale = normed(vector)
        scaled = grad * gain1[...]
        inner = jnp.mean(scaled * vector, axis=-1, keepdims=True)
        grad_gain1[...] += jnp.sum(grad * vector * scale, axis=0, keepdims=True)
        back = grad_resid[c.slot, c.span] + scale * scaled - vector * (scale * scale * scale) * inner
        own_a[c.slot, c.span] = back.astype(BF)

    block = width // dps
    def gain_move(j):
        return pltpu.make_async_remote_copy(
            src_ref=gain_parts.at[line.dp_peer(j)],
            dst_ref=gain_dp.at[j],
            send_sem=gain_send.at[j],
            recv_sem=gain_recv.at[j],
            device_id=(line.dp_peer(j), line.z),
            device_id_type=MESH,
        )

    def gain_share(j):
        return pltpu.make_async_remote_copy(
            src_ref=gain_sum,
            dst_ref=gain_z.at[j],
            send_sem=zsum_send.at[j],
            recv_sem=zsum_recv.at[j],
            device_id=(line.dp, line.z_peer(j)),
            device_id_type=MESH,
        )

    def gains_dp():
        both = jnp.concatenate([grad_gain1[...], grad_gain2[...]], axis=0)
        for d in range(dps):
            gain_parts[d] = both[:, d * block : (d + 1) * block]
        for j in range(1, dps):
            gain_move(j).start()

    def gains_line():
        for j in range(1, dps):
            gain_move(j).wait()
        value = gain_parts[line.dp]
        for j in range(1, dps):
            value = value + gain_dp[j]
        gain_sum[...] = value
        for j in range(1, 4):
            gain_share(j).start()

    def gains_end():
        value = gain_sum[...]
        for j in range(1, 4):
            gain_share(j).wait()
            value = value + gain_z[j]
        gains_out[...] = value

    slots = [(red_p, gat_p, norm, c) for c in parts]
    slots += [(red_a, gat_a, done_a, c) for c in parts]
    slots += [(red_b, gat_b, done_b, c) for c in parts]
    slots += [(red_q, gat_q, done_q, c) for c in reversed(parts)]
    plan = {}
    half = wide // 2
    first_rows = attn_tasks(0, half)
    schedule(plan, attn_tasks(half, half), 0, 4)
    for n in range(1, big):
        schedule(plan, attn_tasks(n * wide, wide), sub * (n - 1), 4 // sub)
    for n in range(big):
        schedule(plan, feed_tasks(n), sub * (big + n - 1), 6 // sub)
    first = sub * (2 * big) - 1
    schedule(plan, [turn], first, 1)
    schedule(plan, after, first + 1, -(-len(after) // 5))
    first = 2 * count + 3
    for i in range(big):
        per_step = 2 if i < 2 else 3
        schedule(plan, back_tasks(i), first, per_step)
        first += 6 // per_step
    schedule(plan, work_out, 2 * count + 6, -(-len(work_out) // 8))
    ends = [
        finished(spreads[0], exits[:1]),
        finished(spreads[2], exits[2:3]),
        finished(spreads[1], exits[1:2], exits[:1]),
    ]
    schedule(plan, ends, 3 * count + 3, 1)
    schedule(plan, work_qkv, first, -(-len(work_qkv) // 4))
    schedule(plan, [finished(spread_out, exits[3:4])], len(slots) + 1, 1)

    def begin(i):
        if i == 0:
            for task in first_rows:
                task()
        if i < len(slots):
            red, _, _, c = slots[i]
            red.start(c)
        if i == len(slots) + 2:
            gains_dp()
        if i == len(slots) + 3:
            gains_line()

    drive(slots, begin, plan)
    finished(spread_qkv, exits[4:])()
    both = qkv_acc[:, lanes:].T
    key_out[...] = both[:HD]
    value_out[...] = both[HD:]
    gains_end()
    for copy in exits[1:]:
        copy.wait()
    for red, gat, done, c in slots[2 * count :]:
        red.close(c)
        gat.complete(c)
        gat.close(c)


def call(kernel, ins, outs, scratch, number, cost):
    return pl.pallas_call(
        kernel,
        in_specs=[spec for spec, _ in ins],
        out_specs=[spec for spec, _, _ in outs],
        out_shape=[jax.ShapeDtypeStruct(shape, kind) for _, shape, kind in outs],
        scratch_shapes=scratch,
        compiler_params=pltpu.CompilerParams(
            collective_id=number, has_side_effects=True, vmem_limit_bytes=LIMIT
        ),
        cost_estimate=pl.CostEstimate(flops=cost, bytes_accessed=cost // 1000, transcendentals=0),
    )(*[array for _, array in ins])


def line_scratch(chunks, piece, width):
    dma = pltpu.SemaphoreType.DMA
    buffers = [
        pltpu.VMEM((chunks, 4 * piece, width), BF),
        pltpu.VMEM((DEPTH, 5, piece, width), BF),
        pltpu.VMEM((chunks, piece, width), BF),
    ]
    n = chunks + 1
    sems = [dma((n, 3)), dma((n, 5)), dma((n, 5)), dma((n, 4)), dma((n,))]
    return buffers, sems


def spread_shapes(groups, rows, cols):
    dma = pltpu.SemaphoreType.DMA
    outs = [(ANY, (rows, cols), F32)]
    boxes = [(ANY, (groups, rows, cols), BF)] * 3
    stage = pltpu.VMEM((2, rows, cols), BF)
    return outs, boxes, stage, [dma((groups,))] * 4 + [dma((2,))]


def tables(seg_row):
    length = seg_row.shape[0]
    start = jnp.sum((seg_row[None, :] < seg_row[:, None]).astype(jnp.int32), axis=1)
    place = (jnp.arange(length, dtype=jnp.int32) - start).astype(F32)
    half = HD // 2
    freq = jnp.power(jnp.float32(THETA), -jnp.arange(half, dtype=F32) / half)
    angle = freq[:, None] * place[None, :]
    return jnp.cos(angle), jnp.sin(angle)


def local(
    dps,
    tokens,
    segments,
    counts,
    cotangent,
    attn_gain,
    mlp_gain,
    query_weight,
    key_weight,
    value_weight,
    out_weight,
    gate_weight,
    up_weight,
    down_weight,
):
    length, width = tokens.shape
    units = gate_weight.shape[1]
    lanes = query_weight.shape[1]
    heads = lanes // HD
    chunks, big = CHUNKS, BIG
    chunk = length // chunks
    wide = length // big
    piece = chunk // 4
    dma = pltpu.SemaphoreType.DMA
    groups = dps // 2
    block = width // dps

    live = jnp.arange(length, dtype=jnp.int32) < counts[0]
    seg_row = segments.astype(F32).reshape(1, length)
    key_row = jnp.where(live, segments, -1).astype(F32).reshape(1, length)
    cosine, sine = tables(segments)
    gain1 = attn_gain.reshape(1, width)
    gain2 = mlp_gain.reshape(1, width)

    buffers, sems = line_scratch(chunks, piece, width)
    total = pltpu.VMEM((piece, width), F32)
    near = pltpu.VMEM((chunks, piece, width), BF)
    by_rows = spread_shapes(groups, block, units)
    by_cols = spread_shapes(groups, units, block)
    for_out = spread_shapes(groups, lanes, block)
    for_qkv = spread_shapes(groups, block, lanes + 2 * HD)
    kv_weight = jnp.concatenate([key_weight.T, value_weight.T], axis=0)
    outs = call(
        functools.partial(layer_kernel, chunks, big, dps),
        [
            (ANY, tokens),
            (ANY, cotangent),
            (VMEM, gain1),
            (VMEM, gain2),
            (VMEM, seg_row),
            (VMEM, key_row),
            (VMEM, cosine),
            (VMEM, sine),
            (ANY, query_weight),
            (ANY, kv_weight),
            (ANY, out_weight),
            (ANY, gate_weight),
            (ANY, up_weight),
            (ANY, down_weight),
        ],
        [
            (ANY, (length, width), BF),
            (ANY, (length, width), BF),
            (VMEM, (2, block), F32),
            (ANY, (block, lanes), F32),
            (VMEM, (HD, block), F32),
            (VMEM, (HD, block), F32),
            *for_out[0],
            *by_rows[0],
            *by_rows[0],
            *by_cols[0],
            *[(ANY, (length, width), BF)] * 3,
            *[(ANY, (length, units), BF)] * 3,
            *by_rows[1],
            *by_rows[1],
            *by_cols[1],
            *for_out[1],
            *for_qkv[1],
        ],
        [
            pltpu.VMEM((width, units), BF),
            pltpu.VMEM((width, units), BF),
            pltpu.VMEM((units, width), BF),
            pltpu.VMEM((2, wide, width), BF),
            pltpu.VMEM((2, wide, width), BF),
            pltpu.VMEM((2, wide, units), BF),
            pltpu.VMEM((2, wide, units), BF),
            pltpu.VMEM((2, wide, units), BF),
            *[pltpu.VMEM((2, 16, units), BF) if block == wide else by_rows[2]] * 2,
            by_cols[2],
            for_out[2],
            for_qkv[2],
            pltpu.VMEM((block, units), F32),
            pltpu.VMEM((units, block), F32),
            pltpu.VMEM((lanes, block), F32),
            pltpu.VMEM((block, lanes + 2 * HD), F32),
            pltpu.VMEM((length, lanes), BF),
            pltpu.VMEM((heads, 1, length), F32),
            pltpu.VMEM((lanes, length), BF),
            pltpu.VMEM((length, HD), BF),
            pltpu.VMEM((HD, length), BF),
            pltpu.VMEM((length, HD), BF),
            pltpu.VMEM((lanes, wide), BF),
            pltpu.VMEM((length, HD), F32),
            pltpu.VMEM((length, HD), F32),
            pltpu.VMEM((chunks, piece, width), F32),
            pltpu.VMEM((1, width), F32),
            pltpu.VMEM((1, width), F32),
            pltpu.VMEM((dps, 2, block), F32),
            pltpu.VMEM((dps, 2, block), F32),
            pltpu.VMEM((2, block), F32),
            pltpu.VMEM((4, 2, block), F32),
            pltpu.VMEM((HD, length), BF),
            pltpu.VMEM((length, 1), F32),
            pltpu.VMEM((length, wide), F32),
            pltpu.VMEM((lanes, wide), F32),
            pltpu.VMEM((chunks, piece, width), F32),
            buffers[0],
            buffers[0],
            buffers[1],
            buffers[2],
            buffers[2],
            near,
            total,
            dma((6,)),
            dma((2, 2)),
            dma((2, 3)),
            dma((2,)),
            dma((chunks + 1,)),
            dma((3,)),
            dma((2, 2)),
            dma((5,)),
            dma((5,)),
            dma((dps,)),
            dma((dps,)),
            dma((4,)),
            dma((4,)),
            *sems,
            *sems,
            *sems,
            *sems,
            *by_rows[3],
            *by_rows[3],
            *by_cols[3],
            *for_out[3],
            *for_qkv[3],
        ],
        0,
        8 * 10**10,
    )
    mixed, tokens_grad, gains = outs[:3]
    return (mixed, tokens_grad, gains[0], gains[1], outs[3], outs[4].T, outs[5].T, *outs[6:10])


def solution(mesh):
    placed = (
        P("dp", None),
        P("dp"),
        P("dp"),
        P("dp", None),
        P(),
        P(),
        P(None, "tensor"),
        P(None, "tensor"),
        P(None, "tensor"),
        P("tensor", None),
        P(None, "tensor"),
        P(None, "tensor"),
        P("tensor", None),
    )
    return jax.shard_map(
        functools.partial(local, mesh.shape["dp"]),
        mesh=mesh,
        in_specs=placed,
        out_specs=(
            P("dp", None),
            P("dp", None),
            P("dp"),
            P("dp"),
            P("dp", "tensor"),
            P("dp", "tensor"),
            P("dp", "tensor"),
            P("tensor", "dp"),
            P("dp", "tensor"),
            P("dp", "tensor"),
            P("tensor", "dp"),
        ),
        check_vma=False,
    )
```

```python
import functools

import jax
import jax.numpy as jnp
from jax import lax
from jax.experimental import pallas as pl
from jax.experimental.pallas import tpu as pltpu
from jax.sharding import PartitionSpec as P

HD = 64
EPS = 1e-05
THETA = 10000.0
NEGATIVE = -1e30
CHUNKS = 8
BIG = 4
DEPTH = 4
MESH = pl.DeviceIdType.MESH
BF = jnp.bfloat16
F32 = jnp.float32
ANY = pl.BlockSpec(memory_space=pl.ANY)
VMEM = pl.BlockSpec(memory_space=pltpu.VMEM)
LIMIT = 62 * 1024 * 1024


def nn(a, b):
    return lax.dot_general(a, b, (((1,), (0,)), ((), ())), preferred_element_type=F32)


def nt(a, b):
    return lax.dot_general(a, b, (((1,), (1,)), ((), ())), preferred_element_type=F32)


def tn(a, b):
    return lax.dot_general(a, b, (((0,), (0,)), ((), ())), preferred_element_type=F32)


class Part:
    def __init__(self, number, row, size, chunk):
        self.id, self.row, self.size = number, row, size
        self.slot, self.low, self.piece = row // chunk, row % chunk, size // 4
        self.span = slice(self.low // 4, self.low // 4 + self.piece)


def parts_of(length, chunks):
    chunk = length // chunks
    sizes = [chunk] * chunks
    return [Part(n, sum(sizes[:n]), size, chunk) for n, size in enumerate(sizes)]


class Line:
    def __init__(self):
        self.z = lax.axis_index("tensor")
        self.dp = lax.axis_index("dp")
        self.low = self.z < 2
        self.inner = jnp.where(self.low, self.z + 1, self.z - 1)
        self.outer = jnp.where(self.low, self.z - 1, self.z + 1)
        self.end = (self.z == 0) | (self.z == 3)
        self.mid = (self.z == 1) | (self.z == 2)

    def quarter(self, c, m, start):
        place = start + jnp.where(self.low, m, 3 - m) * c.piece
        return pl.ds(pl.multiple_of(place, c.piece), c.piece)

    def mine(self, c):
        return pl.ds(pl.multiple_of(c.row + self.z * c.piece, c.piece), c.piece)

    def copy(self, src, dst, send, recv, target):
        return pltpu.make_async_remote_copy(
            src_ref=src,
            dst_ref=dst,
            send_sem=send,
            recv_sem=recv,
            device_id=(self.dp, target),
            device_id_type=MESH,
        )

    def greet(self, dps, every=False):
        barrier = pltpu.get_barrier_semaphore()
        self.dps = dps
        self.groups = dps // 2
        self.core = lax.rem(self.dp, 2)
        self.partner = self.dp + 1 - 2 * self.core

        def signal(dp, z):
            pl.semaphore_signal(barrier, inc=1, device_id=(dp, z), device_id_type=MESH)

        if every:
            for j in range(1, dps):
                signal(self.dp_peer(j), self.z)
            for j in range(1, 4):
                signal(self.dp, self.z_peer(j))
            pl.semaphore_wait(barrier, dps - 1 + 3)
            return
        others = [] if dps == 2 else [self.partner] + [self.peer(j) for j in range(1, self.groups)]
        for other in others:
            signal(other, self.z)
        signal(self.dp, self.inner)

        @pl.when(self.mid)
        def _():
            signal(self.dp, self.outer)
            pl.semaphore_wait(barrier, 2 + len(others))

        @pl.when(self.end)
        def _():
            pl.semaphore_wait(barrier, 1 + len(others))

    def dp_peer(self, j):
        return lax.rem(self.dp + j, self.dps)

    def z_peer(self, j):
        return lax.rem(self.z + j, 4)

    def group(self, j):
        return lax.rem(self.dp // 2 + j, self.groups)

    def peer(self, j):
        return 2 * self.group(j) + self.core


class Reduce:
    def __init__(self, line, part, held, total, send, recv, turn):
        self.turn = turn
        self.line, self.part, self.held, self.total = line, part, held, total
        self.send, self.recv = send, recv

    def place(self, c):
        return self.turn[c.id] % DEPTH

    def rows(self, c, m):
        return self.line.quarter(c, m, c.low)

    def copy(self, c, m, slot, target, number):
        line = self.line
        return line.copy(
            self.part.at[c.slot, self.rows(c, m)],
            self.held.at[self.place(c), slot, : c.piece],
            self.send.at[c.id, number],
            self.recv.at[c.id, slot],
            target,
        )

    def arrived(self, c, slot):
        self.copy(c, 0, slot, self.line.inner, 0).wait_recv()

    def start(self, c):
        @pl.when(self.line.end)
        def _():
            for m in (3, 2, 1):
                self.copy(c, m, m - 1, self.line.inner, m - 1).start()

    def pass_in(self, c, m):
        line = self.line

        @pl.when(line.mid)
        def _():
            self.arrived(c, m - 1)
            rows = self.rows(c, m)
            self.part[c.slot, rows] = (
                self.part[c.slot, rows].astype(F32) + self.held[self.place(c), m - 1, : c.piece].astype(F32)
            ).astype(BF)
            self.copy(c, m, 6 - m, line.inner, 3 - m).start()

    def pass_out(self, c):
        line = self.line

        @pl.when(line.mid)
        def _():
            self.arrived(c, 3)
            rows = self.rows(c, 0)
            self.part[c.slot, rows] = (
                self.part[c.slot, rows].astype(F32) + self.held[self.place(c), 3, : c.piece].astype(F32)
            ).astype(BF)
            self.copy(c, 0, 3, line.outer, 2).start()

    def finish(self, c):
        line = self.line

        @pl.when(line.end)
        def _():
            self.arrived(c, 3)
            self.total[: c.piece] = self.part[c.slot, self.rows(c, 0)].astype(F32) + self.held[self.place(c), 3, : c.piece].astype(F32)

        @pl.when(line.mid)
        def _():
            self.arrived(c, 0)
            self.arrived(c, 4)
            self.total[: c.piece] = (
                self.part[c.slot, self.rows(c, 1)].astype(F32)
                + self.held[self.place(c), 0, : c.piece].astype(F32)
                + self.held[self.place(c), 4, : c.piece].astype(F32)
            )

    def close(self, c):
        for number in range(3):
            self.copy(c, 0, 0, self.line.inner, number).wait_send()


class Spread:
    def __init__(self, line, stage, acc, taken, sums, moved, sems):
        self.line, self.stage, self.acc = line, stage, acc
        self.taken, self.sums, self.moved = taken, sums, moved
        self.send1, self.recv1, self.send2, self.recv2, self.stay = sems

    def give(self, j):
        line = self.line
        return pltpu.make_async_remote_copy(
            src_ref=self.stage.at[1 - line.core],
            dst_ref=self.taken.at[j],
            send_sem=self.send1.at[j],
            recv_sem=self.recv1.at[j],
            device_id=(line.partner, line.z),
            device_id_type=MESH,
        )

    def move(self, j):
        line = self.line
        return pltpu.make_async_remote_copy(
            src_ref=self.sums.at[j],
            dst_ref=self.moved.at[j],
            send_sem=self.send2.at[j],
            recv_sem=self.recv2.at[j],
            device_id=(line.peer(j), line.z),
            device_id_type=MESH,
        )

    def merge_load(self, j):
        self.give(j).wait()
        self.load(self.taken.at[j], 1 - self.line.core).start()

    def load(self, src, slot):
        return pltpu.make_async_copy(src, self.stage.at[slot], self.stay.at[slot])

    def merge_add(self, j):
        core = self.line.core
        self.load(self.taken.at[j], 1 - core).wait()
        self.stage[core] = (
            self.stage[core].astype(F32) + self.stage[1 - core].astype(F32)
        ).astype(BF)
        pltpu.make_async_copy(self.stage.at[core], self.sums.at[j], self.stay.at[core]).start()

    def merge_move(self, j):
        core = self.line.core
        pltpu.make_async_copy(self.stage.at[core], self.sums.at[j], self.stay.at[core]).wait()
        if j:
            self.move(j).start()

    def sources(self):
        return [self.sums.at[0]] + [self.moved.at[j] for j in range(1, self.line.groups)]

    def last_load(self):
        self.load(self.sources()[0], 0).start()

    def last(self):
        sources = self.sources()
        for j, source in enumerate(sources):
            if j + 1 < len(sources):
                self.move(j + 1).wait()
                self.load(sources[j + 1], (j + 1) % 2).start()
            self.load(source, j % 2).wait()
            block = self.stage[j % 2].astype(F32)
            if j:
                self.acc[...] += block
            else:
                self.acc[...] = block


def merged(spreads, j):
    def run(name):
        for spread in spreads:
            getattr(spread, name)(j)

    return [functools.partial(run, name) for name in ("merge_load", "merge_add", "merge_move")]


def finished(spread, copies, before=()):
    def run():
        spread.last_load()
        for copy in before:
            copy.wait()
        spread.last()
        for copy in copies:
            copy.start()

    return run


def halves(stage, value, dim):
    size = value.shape[dim] // 2
    if dim == 0:
        stage[0] = value[:size].astype(BF)
        stage[1] = value[size:].astype(BF)
    else:
        stage[0] = value[:, :size].astype(BF)
        stage[1] = value[:, size:].astype(BF)


class Gather:
    def __init__(self, line, own, full, send, recv, stay):
        self.line, self.own, self.full = line, own, full
        self.send, self.recv, self.stay = send, recv, stay

    def rows(self, c, m):
        return self.line.quarter(c, m, c.row)

    def first(self, c, slot, target, number):
        return self.line.copy(
            self.own.at[c.slot, c.span],
            self.full.at[self.line.mine(c)],
            self.send.at[c.id, number],
            self.recv.at[c.id, slot],
            target,
        )

    def onward(self, c, m, slot, target, number):
        rows = self.rows(c, m)
        return self.line.copy(
            self.full.at[rows],
            self.full.at[rows],
            self.send.at[c.id, number],
            self.recv.at[c.id, slot],
            target,
        )

    def arrived(self, c, m):
        self.onward(c, m, m, self.line.inner, 0).wait_recv()

    def stays(self, c):
        return pltpu.make_async_copy(
            self.own.at[c.slot, c.span], self.full.at[self.line.mine(c)], self.stay.at[c.id]
        )

    def start(self, c):
        line = self.line
        self.stays(c).start()

        @pl.when(line.end)
        def _():
            self.first(c, 0, line.inner, 0).start()

        @pl.when(line.mid)
        def _():
            self.first(c, 1, line.outer, 0).start()
            self.first(c, 2, line.inner, 1).start()

    def pass_near(self, c):
        line = self.line

        @pl.when(line.end)
        def _():
            self.arrived(c, 1)

        @pl.when(line.mid)
        def _():
            self.arrived(c, 0)
            self.onward(c, 0, 3, line.inner, 2).start()
            self.arrived(c, 2)
            self.onward(c, 2, 2, line.outer, 3).start()

    def pass_far(self, c):
        line = self.line

        @pl.when(line.mid)
        def _():
            self.arrived(c, 3)
            self.onward(c, 3, 3, line.outer, 4).start()

    def complete(self, c):
        self.stays(c).wait()

        @pl.when(self.line.end)
        def _():
            for m in (2, 3):
                self.arrived(c, m)

    def close(self, c):
        line = self.line

        @pl.when(line.end)
        def _():
            self.first(c, 0, line.inner, 0).wait_send()

        @pl.when(line.mid)
        def _():
            for number in range(5):
                self.first(c, 0, line.inner, number).wait_send()


def drive(slots, begin, plan):
    n = len(slots)
    for i in range(n + 4):
        begin(i)
        work = list(plan.get(i, ()))
        count = len(work)
        for point in range(6):
            if point == 0 and 0 <= i - 4 < n:
                _, gat, _, c = slots[i - 4]
                gat.pass_far(c)
            if point == 1 and 0 <= i - 3 < n:
                _, gat, _, c = slots[i - 3]
                gat.pass_near(c)
            if point == 2 and 0 <= i - 2 < n:
                red, gat, done, c = slots[i - 2]
                red.finish(c)
                done(c)
                gat.start(c)
            if point == 3 and 0 <= i - 1 < n:
                red, _, _, c = slots[i - 1]
                red.pass_out(c)
            if point == 4 and i < n:
                red, _, _, c = slots[i]
                red.pass_in(c, 3)
            if point == 5 and i < n:
                red, _, _, c = slots[i]
                red.pass_in(c, 2)
            while work and count - len(work) < (point + 1) * count // 6:
                work.pop(0)()
        for task in work:
            task()


def schedule(plan, tasks, first, per_step):
    for k, task in enumerate(tasks):
        plan.setdefault(first + k // per_step, []).append(task)


def put(part, row, cols, value):
    chunk, rows = part.shape[1], value.shape[0]
    done = 0
    while done < rows:
        slot, low = (row + done) // chunk, (row + done) % chunk
        size = min(chunk - low, rows - done)
        part[slot, low : low + size, cols] = value[done : done + size].astype(BF)
        done += size


def rope(t, cos, sin):
    half = HD // 2
    first, second = t[:half], t[half:]
    return jnp.concatenate([first * cos - second * sin, second * cos + first * sin], axis=0)


def unrope(t, cos, sin):
    half = HD // 2
    first, second = t[:half], t[half:]
    return jnp.concatenate([first * cos + second * sin, second * cos - first * sin], axis=0)


def normed(vector):
    return lax.rsqrt(jnp.mean(vector * vector, axis=-1, keepdims=True) + EPS)


def visible_bias(seg_row, key_row, row, rows):
    keys = row + rows
    seg_q = seg_row[:, row:keys]
    seg_k = key_row[:keys, :]
    shape = (keys, rows)
    key_at = lax.broadcasted_iota(jnp.int32, shape, 0)
    query_at = lax.broadcasted_iota(jnp.int32, shape, 1) + row
    seen = ((seg_k == seg_q) & (key_at < query_at)) | (key_at == query_at)
    return jnp.where(seen, 0.0, NEGATIVE)


def layer_kernel(
    chunks,
    big,
    dps,
    tokens,
    cotangent,
    gain1,
    gain2,
    seg_row,
    key_row,
    cosine,
    sine,
    query_weight,
    key_weight,
    value_weight,
    out_weight,
    gate_weight,
    up_weight,
    down_weight,
    mixed,
    tokens_grad,
    gains_out,
    query_out,
    key_out,
    value_out,
    out_out,
    gate_out,
    up_out,
    down_out,
    branch,
    hidden1,
    hidden2,
    active,
    grad_gate,
    grad_up,
    gate_taken,
    gate_sums,
    gate_moved,
    up_taken,
    up_sums,
    up_moved,
    down_taken,
    down_sums,
    down_moved,
    out_taken,
    out_sums,
    out_moved,
    qkv_taken,
    qkv_sums,
    qkv_moved,
    wg,
    wu,
    wd,
    hid,
    dy,
    act_c,
    gate_c,
    up_c,
    gate_stage,
    up_stage,
    down_stage,
    out_stage,
    qkv_stage,
    rows_acc,
    cols_acc,
    out_acc,
    qkv_acc,
    heads_out,
    logs,
    query_t,
    keys,
    keys_t,
    values,
    do_t,
    dk,
    dv,
    grad_resid,
    grad_gain1,
    grad_gain2,
    gain_parts,
    gain_dp,
    gain_sum,
    gain_z,
    values_t,
    seg_key,
    bias,
    heads_t,
    resid,
    part_p,
    part_a,
    held,
    own_p,
    own_a,
    near,
    total,
    w_sem,
    in_sem,
    out_sem,
    save_sem,
    near_sem,
    turn_sem,
    pair_sem,
    late_sem,
    exit_sem,
    gain_send,
    gain_recv,
    zsum_send,
    zsum_recv,
    *sems,
):
    length, width = tokens.shape
    units = wg.shape[1]
    chunk = length // chunks
    wide = length // big
    sub = chunks // big
    parts = parts_of(length, chunks)
    count = len(parts)
    lanes = query_t.shape[0]
    heads = lanes // HD
    if gate_stage.shape[1] != width // dps:
        gate_stage, up_stage = gate_c, up_c
    line = Line()
    turns_of = [{c.id: k * count + c.id for c in parts} for k in range(3)]
    turns_of.append({c.id: 4 * count - 1 - c.id for c in parts})
    red_p = Reduce(line, part_p, held, total, *sems[0:2], turns_of[0])
    gat_p = Gather(line, own_p, hidden2, *sems[2:5])
    red_a = Reduce(line, part_a, held, total, *sems[5:7], turns_of[1])
    gat_a = Gather(line, own_a, branch, *sems[7:10])
    red_b = Reduce(line, part_p, held, total, *sems[10:12], turns_of[2])
    gat_b = Gather(line, own_p, mixed, *sems[12:15])
    red_q = Reduce(line, part_a, held, total, *sems[15:17], turns_of[3])
    gat_q = Gather(line, own_a, tokens_grad, *sems[17:20])
    dp_sems = sems[20:]
    factor = HD ** (-0.5)

    def near_copy(c, src=cotangent):
        return pltpu.make_async_copy(
            src.at[line.mine(c)], near.at[c.slot, c.span], near_sem.at[c.id]
        )

    def token_load(n):
        rows = slice(n * wide, (n + 1) * wide)
        return pltpu.make_async_copy(tokens.at[rows], hid.at[n % 2], in_sem.at[n % 2, 0])

    def hidden_save(n):
        rows = slice(n * wide, (n + 1) * wide)
        return pltpu.make_async_copy(dy.at[n % 2], hidden1.at[rows], save_sem.at[n % 2])

    def load(n):
        slot = n % 2
        rows = slice(n * wide, (n + 1) * wide)
        return (
            pltpu.make_async_copy(hidden2.at[rows], hid.at[slot], in_sem.at[slot, 0]),
            pltpu.make_async_copy(cotangent.at[rows], dy.at[slot], in_sem.at[slot, 1]),
        )

    weights = [
        pltpu.make_async_copy(src, dst, w_sem.at[i])
        for i, (src, dst) in enumerate(
            (
                (query_weight, wu.at[:, :lanes]),
                (key_weight, wd.at[lanes : lanes + HD]),
                (out_weight, wd.at[:lanes]),
                (gate_weight, wg),
                (up_weight, wu),
                (down_weight, wd),
            )
        )
    ]
    value_load = pltpu.make_async_copy(
        value_weight, wd.at[lanes + HD : lanes + 2 * HD], w_sem.at[6]
    )
    token_load(0).start()
    value_load.start()
    for copy in weights[:4]:
        copy.start()
    for c in parts:
        near_copy(c, tokens).start()
    line.greet(dps, every=True)
    seg_key[...] = jnp.broadcast_to(key_row[...], (128, length)).T[:, :1]
    for zero in (grad_gain1, grad_gain2, dk, dv):
        zero[...] = jnp.zeros_like(zero)

    def project(row, size):
        n, low = row // wide, row % wide
        rows = slice(row, row + size)
        here = slice(low, low + size)
        if low == 0:
            token_load(n).wait()
            if n + 1 < big:
                token_load(n + 1).start()
            if n >= 2:
                hidden_save(n - 2).wait()
        if row == 0:
            weights[0].wait()
            weights[1].wait()
            value_load.wait()
        vector = hid[n % 2, here].astype(F32)
        hidden = (vector * normed(vector) * gain1[...]).astype(BF)
        dy[n % 2, here] = hidden
        if low + size == wide:
            hidden_save(n).start()
        cos, sin = cosine[:, rows], sine[:, rows]
        raw = nn(hidden, wu[:, :lanes]).T
        for h in range(heads):
            here = slice(h * HD, (h + 1) * HD)
            turned = rope(raw[here], cos, sin) * (HD ** (-0.5))
            query_t[here, rows] = turned.astype(BF)
        raw = nt(wd[lanes : lanes + 2 * HD, :], hidden)
        turned = rope(raw[:HD], cos, sin)
        keys_t[:, rows] = turned.astype(BF)
        keys[rows, :] = turned.T.astype(BF)
        values_t[:, rows] = raw[HD:].astype(BF)
        values[rows, :] = raw[HD:].T.astype(BF)

    def attend(row, size, begin, end):
        keys_n = row + size
        cols = slice(row, keys_n)
        if begin == 0:
            bias[:keys_n, :size] = visible_bias(seg_row[...], seg_key[...], row, size)

        def head(h, carry):
            here = pl.ds(pl.multiple_of(h * HD, HD), HD)
            scores = nn(keys[:keys_n, :], query_t[here, cols]) + bias[:keys_n, :size]
            peak = jnp.max(scores, axis=0, keepdims=True)
            weights = jnp.exp(scores - peak)
            sums = jnp.sum(weights, axis=0, keepdims=True)
            probs = (weights * (1.0 / sums)).astype(BF)
            heads_t[here, :size] = nn(values_t[:, :keys_n], probs)
            logs[h, :, cols] = peak + jnp.log(sums)
            return carry

        lax.fori_loop(begin, end, head, 0)

    def close_heads(row, size):
        if row == 0:
            weights[2].wait()
        heads_n = heads_t[:, :size].T.astype(BF)
        heads_out[row : row + size, :] = heads_n
        step = min(512, width)
        for at in range(0, width, step):
            cols = slice(at, at + step)
            put(part_p, row, cols, nn(heads_n, wd[:lanes, cols]))
        if row + size == length:
            weights[4].start()
            weights[5].start()

    def attn_tasks(row, size):
        return [
            functools.partial(project, row, size),
            functools.partial(attend, row, size, 0, heads // 2),
            functools.partial(attend, row, size, heads // 2, heads),
            functools.partial(close_heads, row, size),
        ]

    def norm(c):
        near_copy(c, tokens).wait()
        vector = near[c.slot, c.span].astype(F32) + total[: c.piece]
        near_copy(c).start()
        resid[c.slot, c.span] = vector
        own_p[c.slot, c.span] = (vector * normed(vector) * gain2[...]).astype(BF)

    def saves(n):
        slot = n % 2
        rows = slice(n * wide, (n + 1) * wide)
        return [
            pltpu.make_async_copy(src.at[slot], dst.at[rows], out_sem.at[slot, i])
            for i, (src, dst) in enumerate(((act_c, active), (gate_c, grad_gate), (up_c, grad_up)))
        ]

    def inside(n):
        return [c for c in parts if c.row // wide == n]

    def enter(n):
        if n == 0:
            for k in range(max(0, big - 2), big):
                hidden_save(k).wait()
        for c in inside(n):
            gat_p.complete(c)
        for copy in load(n):
            copy.start()
        for c in inside(n):
            red_p.close(c)
            gat_p.close(c)
        for copy in load(n):
            copy.wait()
        if n == 0:
            for copy in weights[3:]:
                copy.wait()
        if n >= 2:
            for copy in saves(n - 2):
                copy.wait()
        slot = n % 2
        dy[slot] = jnp.where(seg_key[n * wide : (n + 1) * wide, :] >= 0.0, dy[slot], BF(0))

    def hidden_units(n, cols):
        slot = n % 2
        gate = nn(hid[slot], wg[:, cols])
        up = nn(hid[slot], wu[:, cols])
        grad = nt(dy[slot], wd[cols, :])
        sig = 1.0 / (1.0 + jnp.exp(-gate))
        silu = gate * sig
        act_c[slot, :, cols] = (silu * up).astype(BF)
        gate_c[slot, :, cols] = (grad * up * sig * (1.0 + gate * (1.0 - sig))).astype(BF)
        up_c[slot, :, cols] = (grad * silu).astype(BF)
        if cols.stop == units:
            for copy in saves(n):
                copy.start()

    def back_part(n, cols):
        slot = n % 2
        put(part_a, n * wide, cols, nt(gate_c[slot], wg[cols, :]) + nt(up_c[slot], wu[cols, :]))

    def down_part(n, cols):
        put(part_p, n * wide, cols, nn(act_c[n % 2], wd[:, cols]))

    def feed_tasks(n):
        step = 512
        unit_cols = [slice(at, min(at + step, units)) for at in range(0, units, step)]
        cols = [slice(at, at + step) for at in range(0, width, step)]

        def first():
            enter(n)
            hidden_units(n, unit_cols[0])

        def several(f, group):
            for here in group:
                f(n, here)

        return [
            first,
            *[functools.partial(hidden_units, n, here) for here in unit_cols[1:]],
            functools.partial(several, back_part, cols[:2]),
            functools.partial(several, back_part, cols[2:]),
            functools.partial(several, down_part, cols),
        ]

    spreads = [
        Spread(line, gate_stage, rows_acc, gate_taken, gate_sums, gate_moved, dp_sems[:5]),
        Spread(line, up_stage, rows_acc, up_taken, up_sums, up_moved, dp_sems[5:10]),
        Spread(line, down_stage, cols_acc, down_taken, down_sums, down_moved, dp_sems[10:15]),
    ]
    spread_out = Spread(line, out_stage, out_acc, out_taken, out_sums, out_moved, dp_sems[15:20])
    spread_qkv = Spread(line, qkv_stage, qkv_acc, qkv_taken, qkv_sums, qkv_moved, dp_sems[20:])
    pair = 2 * width // dps
    groups = dps // 2
    turns = [
        pltpu.make_async_copy(src, dst, turn_sem.at[i])
        for i, (src, dst) in enumerate(
            (
                (grad_gate, wg.at[:length]),
                (grad_up, wg.at[length : 2 * length]),
                (active, wu.at[:length]),
            )
        )
    ]

    half_lanes = lanes // 2
    kv = 2 * HD
    late = [
        pltpu.make_async_copy(src, dst, late_sem.at[i])
        for i, (src, dst) in enumerate(
            [(out_weight.at[k * wide : (k + 1) * wide], dy.at[k]) for k in range(2)]
            + [
                (
                    query_weight.at[k * length : (k + 1) * length],
                    wu.at[length : 2 * length, k * lanes : (k + 1) * lanes],
                )
                for k in range(2)
            ]
            + [
                (key_weight, wd.at[length : length + HD]),
                (value_weight, wd.at[length + HD : length + kv]),
            ]
        )
    ]

    def pair_load(j, slot):
        cols = pl.ds(pl.multiple_of(line.group(j) * pair, pair), pair)
        at = 2 * slot * pair
        return (
            pltpu.make_async_copy(
                hidden2.at[:, cols], wd.at[:length, at : at + pair], pair_sem.at[slot, 0]
            ),
            pltpu.make_async_copy(
                cotangent.at[:, cols],
                wd.at[:length, at + pair : at + 2 * pair],
                pair_sem.at[slot, 1],
            ),
        )

    units_order = list(range(1, groups)) + [0]

    def turn():
        for n in range(max(0, big - 2), big):
            for copy in saves(n):
                copy.wait()
        for copy in turns + late:
            copy.start()
        for copy in pair_load(units_order[0], 0):
            copy.start()

    def unit_enter(n):
        slot = n % 2
        for copy in pair_load(units_order[n], slot):
            copy.wait()
        if n == 0:
            for copy in turns:
                copy.wait()
            wu[:length, :] = jnp.where(seg_key[...] >= 0.0, wu[:length, :], BF(0))
        if n + 1 < groups:
            for copy in pair_load(units_order[n + 1], 1 - slot):
                copy.start()

    def unit_gate(n):
        at = 2 * (n % 2) * pair
        unit_enter(n)
        halves(gate_stage, tn(wd[:length, at : at + pair], wg[:length, :]), 0)
        spreads[0].give(units_order[n]).start()

    def unit_up(n):
        at = 2 * (n % 2) * pair
        halves(up_stage, tn(wd[:length, at : at + pair], wg[length : 2 * length, :]), 0)
        spreads[1].give(units_order[n]).start()

    def unit_down(n):
        at = 2 * (n % 2) * pair + pair
        halves(down_stage, tn(wu[:length, :], wd[:length, at : at + pair]), 1)
        spreads[2].give(units_order[n]).start()

    after = []
    for n in range(groups):
        for task in (unit_gate, unit_up, unit_down):
            after.append(functools.partial(task, n))
        after += merged(spreads, units_order[n])

    def done_a(c):
        near_copy(c).wait()
        grad = total[: c.piece]
        vector = resid[c.slot, c.span]
        scale = normed(vector)
        scaled = grad * gain2[...]
        inner = jnp.mean(scaled * vector, axis=-1, keepdims=True)
        grad_gain2[...] += jnp.sum(grad * vector * scale, axis=0, keepdims=True)
        seen = seg_key[line.mine(c), :] >= 0.0
        back = jnp.where(seen, near[c.slot, c.span].astype(F32), 0.0)
        back = back + scale * scaled - vector * (scale * scale * scale) * inner
        grad_resid[c.slot, c.span] = back
        own_a[c.slot, c.span] = back.astype(BF)
        near_copy(c, tokens).start()

    def done_b(c):
        own_p[c.slot, c.span] = (resid[c.slot, c.span] + total[: c.piece]).astype(BF)

    order = list(reversed(range(big)))

    def branch_load(c, slot):
        return pltpu.make_async_copy(
            branch.at[c * wide : (c + 1) * wide], hid.at[slot], in_sem.at[slot, 0]
        )

    def back_enter(i):
        c, slot = order[i], i % 2
        if i == 0:
            for k in parts:
                gat_a.complete(k)
        branch_load(c, slot).start()
        for k in inside(c):
            red_a.close(k)
            gat_a.close(k)
        if i == 0:
            for copy in late:
                copy.wait()
        branch_load(c, slot).wait()
        keys_n = (c + 1) * wide
        bias[:keys_n, :] = visible_bias(seg_row[...], seg_key[...], c * wide, wide)
        for k in range(2):
            grad_heads = nt(hid[slot], dy[k])
            do_t[k * half_lanes : (k + 1) * half_lanes, :] = grad_heads.T.astype(BF)

    def back_attend(i, begin, end):
        c = order[i]
        keys_n = (c + 1) * wide
        cols = slice(c * wide, keys_n)

        def head(h, carry):
            here = pl.ds(pl.multiple_of(h * HD, HD), HD)
            scores = nn(keys[:keys_n, :], query_t[here, cols]) + bias[:keys_n, :]
            probs = jnp.exp(scores - logs[h, :, cols])
            grad_probs = nn(values[:keys_n, :], do_t[here, :])
            delta = jnp.sum(probs * grad_probs, axis=0, keepdims=True)
            grad_scores = (probs * (grad_probs - delta)).astype(BF)
            dv[:keys_n, :] += nn(probs.astype(BF), do_t[here, :].T)
            dk[:keys_n, :] += nn(grad_scores, query_t[here, cols].T)
            grad = nn(keys_t[:, :keys_n], grad_scores) * factor
            heads_t[here, :] = unrope(grad, cosine[:, cols], sine[:, cols])
            return carry

        lax.fori_loop(begin, end, head, 0)

    def back_leave(i):
        c = order[i]
        cols = slice(c * wide, (c + 1) * wide)
        wg[cols, :lanes] = heads_t[...].T.astype(BF)
        grad_k = unrope(dk[cols, :].T, cosine[:, cols], sine[:, cols]).T
        wg[cols, lanes : lanes + kv] = jnp.concatenate([grad_k, dv[cols, :]], axis=1).astype(BF)
        step = 512
        for n in range(0, width, step):
            here = slice(n, n + step)
            k, row = n // length, length + n % length
            rows = slice(row, row + step)
            value = nt(wg[cols, :lanes], wu[rows, k * lanes : (k + 1) * lanes])
            value = value + nn(wg[cols, lanes : lanes + kv], wd[length : length + kv, here])
            put(part_a, c * wide, here, value)

    def back_tasks(i):
        quarter = heads // 4
        return [
            functools.partial(back_enter, i),
            *[functools.partial(back_attend, i, k * quarter, (k + 1) * quarter) for k in range(4)],
            functools.partial(back_leave, i),
        ]

    def one_load(n, src, at):
        slot = n % 2
        cols = pl.ds(pl.multiple_of(line.group(units_order[n]) * pair, pair), pair)
        at = 2 * slot * pair + at * pair
        return pltpu.make_async_copy(
            src.at[:, cols], wd.at[:length, at : at + pair], pair_sem.at[slot, 0]
        )

    def unit_out(n):
        at = 2 * (n % 2) * pair + pair
        if n == 0:
            one_load(n, branch, 1).start()
        one_load(n, branch, 1).wait()
        if n + 1 < groups:
            one_load(n + 1, branch, 1).start()
        halves(out_stage, tn(heads_out[...], wd[:length, at : at + pair]), 1)
        spread_out.give(units_order[n]).start()

    def unit_qkv(n):
        at = 2 * (n % 2) * pair
        if n == 0:
            one_load(n, hidden1, 0).start()
        one_load(n, hidden1, 0).wait()
        if n + 1 < groups:
            one_load(n + 1, hidden1, 0).start()
        halves(qkv_stage, tn(wd[:length, at : at + pair], wg[:length, : lanes + kv]), 0)
        spread_qkv.give(units_order[n]).start()

    work_out, work_qkv = [], []
    for n in range(groups):
        work_out.append(functools.partial(unit_out, n))
        work_out += merged([spread_out], units_order[n])
        work_qkv.append(functools.partial(unit_qkv, n))
        work_qkv += merged([spread_qkv], units_order[n])

    exits = [
        pltpu.make_async_copy(src, dst, exit_sem.at[i])
        for i, (src, dst) in enumerate(
            (
                (rows_acc, gate_out),
                (rows_acc, up_out),
                (cols_acc, down_out),
                (out_acc, out_out),
                (qkv_acc.at[:, :lanes], query_out),
            )
        )
    ]

    def done_q(c):
        near_copy(c, tokens).wait()
        grad = total[: c.piece]
        vector = near[c.slot, c.span].astype(F32)
        scale = normed(vector)
        scaled = grad * gain1[...]
        inner = jnp.mean(scaled * vector, axis=-1, keepdims=True)
        grad_gain1[...] += jnp.sum(grad * vector * scale, axis=0, keepdims=True)
        back = grad_resid[c.slot, c.span] + scale * scaled - vector * (scale * scale * scale) * inner
        own_a[c.slot, c.span] = back.astype(BF)

    block = width // dps
    def gain_move(j):
        return pltpu.make_async_remote_copy(
            src_ref=gain_parts.at[line.dp_peer(j)],
            dst_ref=gain_dp.at[j],
            send_sem=gain_send.at[j],
            recv_sem=gain_recv.at[j],
            device_id=(line.dp_peer(j), line.z),
            device_id_type=MESH,
        )

    def gain_share(j):
        return pltpu.make_async_remote_copy(
            src_ref=gain_sum,
            dst_ref=gain_z.at[j],
            send_sem=zsum_send.at[j],
            recv_sem=zsum_recv.at[j],
            device_id=(line.dp, line.z_peer(j)),
            device_id_type=MESH,
        )

    def gains_dp():
        both = jnp.concatenate([grad_gain1[...], grad_gain2[...]], axis=0)
        for d in range(dps):
            gain_parts[d] = both[:, d * block : (d + 1) * block]
        for j in range(1, dps):
            gain_move(j).start()

    def gains_line():
        for j in range(1, dps):
            gain_move(j).wait()
        value = gain_parts[line.dp]
        for j in range(1, dps):
            value = value + gain_dp[j]
        gain_sum[...] = value
        for j in range(1, 4):
            gain_share(j).start()

    def gains_end():
        value = gain_sum[...]
        for j in range(1, 4):
            gain_share(j).wait()
            value = value + gain_z[j]
        gains_out[...] = value

    slots = [(red_p, gat_p, norm, c) for c in parts]
    slots += [(red_a, gat_a, done_a, c) for c in parts]
    slots += [(red_b, gat_b, done_b, c) for c in parts]
    slots += [(red_q, gat_q, done_q, c) for c in reversed(parts)]
    plan = {}
    half = wide // 2
    first_rows = attn_tasks(0, half)
    schedule(plan, attn_tasks(half, half), 0, 4)
    for n in range(1, big):
        schedule(plan, attn_tasks(n * wide, wide), sub * (n - 1), 4 // sub)
    for n in range(big):
        schedule(plan, feed_tasks(n), sub * (big + n - 1), 6 // sub)
    first = sub * (2 * big) - 1
    schedule(plan, [turn], first, 1)
    schedule(plan, after, first + 1, -(-len(after) // 5))
    first = 2 * count + 3
    for i in range(big):
        per_step = 2 if i < 2 else 3
        schedule(plan, back_tasks(i), first, per_step)
        first += 6 // per_step
    schedule(plan, work_out, 2 * count + 6, -(-len(work_out) // 8))
    ends = [
        finished(spreads[0], exits[:1]),
        finished(spreads[2], exits[2:3]),
        finished(spreads[1], exits[1:2], exits[:1]),
    ]
    schedule(plan, ends, 3 * count + 3, 1)
    schedule(plan, work_qkv, first, -(-len(work_qkv) // 4))
    schedule(plan, [finished(spread_out, exits[3:4])], len(slots) + 1, 1)

    def begin(i):
        if i == 0:
            for task in first_rows:
                task()
        if i < len(slots):
            red, _, _, c = slots[i]
            red.start(c)
        if i == len(slots) + 2:
            gains_dp()
        if i == len(slots) + 3:
            gains_line()

    drive(slots, begin, plan)
    finished(spread_qkv, exits[4:])()
    both = qkv_acc[:, lanes:].T
    key_out[...] = both[:HD]
    value_out[...] = both[HD:]
    gains_end()
    for copy in exits[1:]:
        copy.wait()
    for red, gat, done, c in slots[2 * count :]:
        red.close(c)
        gat.complete(c)
        gat.close(c)


def call(kernel, ins, outs, scratch, number, cost):
    return pl.pallas_call(
        kernel,
        in_specs=[spec for spec, _ in ins],
        out_specs=[spec for spec, _, _ in outs],
        out_shape=[jax.ShapeDtypeStruct(shape, kind) for _, shape, kind in outs],
        scratch_shapes=scratch,
        compiler_params=pltpu.CompilerParams(
            collective_id=number, has_side_effects=True, vmem_limit_bytes=LIMIT
        ),
        cost_estimate=pl.CostEstimate(flops=cost, bytes_accessed=cost // 1000, transcendentals=0),
    )(*[array for _, array in ins])


def line_scratch(chunks, piece, width):
    dma = pltpu.SemaphoreType.DMA
    buffers = [
        pltpu.VMEM((chunks, 4 * piece, width), BF),
        pltpu.VMEM((DEPTH, 5, piece, width), BF),
        pltpu.VMEM((chunks, piece, width), BF),
    ]
    n = chunks + 1
    sems = [dma((n, 3)), dma((n, 5)), dma((n, 5)), dma((n, 4)), dma((n,))]
    return buffers, sems


def spread_shapes(groups, rows, cols):
    dma = pltpu.SemaphoreType.DMA
    outs = [(ANY, (rows, cols), F32)]
    boxes = [(ANY, (groups, rows, cols), BF)] * 3
    stage = pltpu.VMEM((2, rows, cols), BF)
    return outs, boxes, stage, [dma((groups,))] * 4 + [dma((2,))]


def tables(seg_row):
    length = seg_row.shape[0]
    start = jnp.sum((seg_row[None, :] < seg_row[:, None]).astype(jnp.int32), axis=1)
    place = (jnp.arange(length, dtype=jnp.int32) - start).astype(F32)
    half = HD // 2
    freq = jnp.power(jnp.float32(THETA), -jnp.arange(half, dtype=F32) / half)
    angle = freq[:, None] * place[None, :]
    return jnp.cos(angle), jnp.sin(angle)


def local(
    dps,
    tokens,
    segments,
    counts,
    cotangent,
    attn_gain,
    mlp_gain,
    query_weight,
    key_weight,
    value_weight,
    out_weight,
    gate_weight,
    up_weight,
    down_weight,
):
    length, width = tokens.shape
    units = gate_weight.shape[1]
    lanes = query_weight.shape[1]
    heads = lanes // HD
    chunks, big = CHUNKS, BIG
    chunk = length // chunks
    wide = length // big
    piece = chunk // 4
    dma = pltpu.SemaphoreType.DMA
    groups = dps // 2
    block = width // dps

    live = jnp.arange(length, dtype=jnp.int32) < counts[0]
    seg_row = segments.astype(F32).reshape(1, length)
    key_row = jnp.where(live, segments, -1).astype(F32).reshape(1, length)
    cosine, sine = tables(segments)
    gain1 = attn_gain.reshape(1, width)
    gain2 = mlp_gain.reshape(1, width)

    buffers, sems = line_scratch(chunks, piece, width)
    total = pltpu.VMEM((piece, width), F32)
    near = pltpu.VMEM((chunks, piece, width), BF)
    by_rows = spread_shapes(groups, block, units)
    by_cols = spread_shapes(groups, units, block)
    for_out = spread_shapes(groups, lanes, block)
    for_qkv = spread_shapes(groups, block, lanes + 2 * HD)
    outs = call(
        functools.partial(layer_kernel, chunks, big, dps),
        [
            (ANY, tokens),
            (ANY, cotangent),
            (VMEM, gain1),
            (VMEM, gain2),
            (VMEM, seg_row),
            (VMEM, key_row),
            (VMEM, cosine),
            (VMEM, sine),
            (ANY, query_weight),
            (ANY, key_weight.T),
            (ANY, value_weight.T),
            (ANY, out_weight),
            (ANY, gate_weight),
            (ANY, up_weight),
            (ANY, down_weight),
        ],
        [
            (ANY, (length, width), BF),
            (ANY, (length, width), BF),
            (VMEM, (2, block), F32),
            (ANY, (block, lanes), F32),
            (VMEM, (HD, block), F32),
            (VMEM, (HD, block), F32),
            *for_out[0],
            *by_rows[0],
            *by_rows[0],
            *by_cols[0],
            *[(ANY, (length, width), BF)] * 3,
            *[(ANY, (length, units), BF)] * 3,
            *by_rows[1],
            *by_rows[1],
            *by_cols[1],
            *for_out[1],
            *for_qkv[1],
        ],
        [
            pltpu.VMEM((width, units), BF),
            pltpu.VMEM((width, units), BF),
            pltpu.VMEM((units, width), BF),
            pltpu.VMEM((2, wide, width), BF),
            pltpu.VMEM((2, wide, width), BF),
            pltpu.VMEM((2, wide, units), BF),
            pltpu.VMEM((2, wide, units), BF),
            pltpu.VMEM((2, wide, units), BF),
            *[pltpu.VMEM((2, 16, units), BF) if block == wide else by_rows[2]] * 2,
            by_cols[2],
            for_out[2],
            for_qkv[2],
            pltpu.VMEM((block, units), F32),
            pltpu.VMEM((units, block), F32),
            pltpu.VMEM((lanes, block), F32),
            pltpu.VMEM((block, lanes + 2 * HD), F32),
            pltpu.VMEM((length, lanes), BF),
            pltpu.VMEM((heads, 1, length), F32),
            pltpu.VMEM((lanes, length), BF),
            pltpu.VMEM((length, HD), BF),
            pltpu.VMEM((HD, length), BF),
            pltpu.VMEM((length, HD), BF),
            pltpu.VMEM((lanes, wide), BF),
            pltpu.VMEM((length, HD), F32),
            pltpu.VMEM((length, HD), F32),
            pltpu.VMEM((chunks, piece, width), F32),
            pltpu.VMEM((1, width), F32),
            pltpu.VMEM((1, width), F32),
            pltpu.VMEM((dps, 2, block), F32),
            pltpu.VMEM((dps, 2, block), F32),
            pltpu.VMEM((2, block), F32),
            pltpu.VMEM((4, 2, block), F32),
            pltpu.VMEM((HD, length), BF),
            pltpu.VMEM((length, 1), F32),
            pltpu.VMEM((length, wide), F32),
            pltpu.VMEM((lanes, wide), F32),
            pltpu.VMEM((chunks, piece, width), F32),
            buffers[0],
            buffers[0],
            buffers[1],
            buffers[2],
            buffers[2],
            near,
            total,
            dma((7,)),
            dma((2, 2)),
            dma((2, 3)),
            dma((2,)),
            dma((chunks + 1,)),
            dma((3,)),
            dma((2, 2)),
            dma((6,)),
            dma((5,)),
            dma((dps,)),
            dma((dps,)),
            dma((4,)),
            dma((4,)),
            *sems,
            *sems,
            *sems,
            *sems,
            *by_rows[3],
            *by_rows[3],
            *by_cols[3],
            *for_out[3],
            *for_qkv[3],
        ],
        0,
        8 * 10**10,
    )
    mixed, tokens_grad, gains = outs[:3]
    return (mixed, tokens_grad, gains[0], gains[1], outs[3], outs[4].T, outs[5].T, *outs[6:10])


def solution(mesh):
    placed = (
        P("dp", None),
        P("dp"),
        P("dp"),
        P("dp", None),
        P(),
        P(),
        P(None, "tensor"),
        P(None, "tensor"),
        P(None, "tensor"),
        P("tensor", None),
        P(None, "tensor"),
        P(None, "tensor"),
        P("tensor", None),
    )
    return jax.shard_map(
        functools.partial(local, mesh.shape["dp"]),
        mesh=mesh,
        in_specs=placed,
        out_specs=(
            P("dp", None),
            P("dp", None),
            P("dp"),
            P("dp"),
            P("dp", "tensor"),
            P("dp", "tensor"),
            P("dp", "tensor"),
            P("tensor", "dp"),
            P("dp", "tensor"),
            P("dp", "tensor"),
            P("tensor", "dp"),
        ),
        check_vma=False,
    )
```
